32 devices in a mesh: view: 8 (over z, core), blk: 4 (over y, x).
Axes of the slice: x: 2, y: 2, z: 4, core: 2. Of those that a mesh axis runs over, the one named last changes fastest.
Arguments:
- estimate: float32 [64, 128, 128], P('blk'), may hold values from 0.5 to 2
- images: bfloat16 [8, 64, 128, 128], P('view', 'blk'), may hold values from 0.5 to 2
- point_spread: float32 [8, 9, 7, 25], replicated, may hold values from 0.01 to 1
- covered: int32 [8, 4, 4], P(None, 'blk'), may hold values from 0 to 1, as said below
Outputs:
- estimate_next: float32 [64, 128, 128], P('blk')
The draws below stay inside these ranges and needn't reach their ends.
Inputs may be any that keep to these rules, and one draw needn't show every extreme that they name: For each view and each block layer along the first dimension, the covered blocks are consecutive along the second dimension and at most 3; for every view some block layer has exactly 3.
All inputs are finite; a program needn't handle non-finite values.
Results may differ from the reference program's by a relative error of at most 0.0003.
Values may be sent and summed in bfloat16 or wider, within the bound.
No kernel may reach another device: no remote copies, remote signals or barrier semaphores. Data moves between devices by JAX's collectives and lax.ppermute only.
A program may use at most 128 MiB of HBM per device.

```python
import math
import jax
import jax.numpy as jnp
from jax import lax

VIEWS = 8
KX = 9
KY = 7
KZ = 25
SX = 16
BY = 32
NBY = 4
SHARES = 1
CAP = 3
NBX = 4
NX = 64
NY = 128
NZ = 128
N_VIEW = 8


def draw_covered(key, part):
    key_count = jax.random.fold_in(key, 11)
    key_pick = jax.random.fold_in(key, 12)
    key_start = jax.random.fold_in(key, 13)
    counts = jax.random.randint(key_count, (VIEWS, NBX), 0, CAP + 1)
    chosen = jax.random.randint(key_pick, (VIEWS,), 0, NBX)
    layer_index = jnp.arange(NBX, dtype=jnp.int32)
    counts = jnp.where(layer_index[None, :] == chosen[:, None], CAP, counts)
    starts = jax.random.randint(key_start, (VIEWS, NBX), 0, NBY - counts + 1)
    position = jnp.arange(NBY, dtype=jnp.int32)[None, None, :]
    inside = (position >= starts[:, :, None]) & (position < starts[:, :, None] + counts[:, :, None])
    return inside.astype(jnp.int32)


def block_levels(stream_key, dims, shards, low, high):
    level = 1.0
    for axis_at, blocks in shards:
        heights = jax.random.uniform(jax.random.fold_in(jax.random.fold_in(stream_key, 6), axis_at), (blocks,), jnp.float32, low / len(shards), high / len(shards))
        level = level * jnp.repeat(jnp.exp(heights), dims[axis_at] // blocks).reshape((-1,) + (1,) * (len(dims) - 1 - axis_at))
    return level


def setup_inputs(seed: int = 0) -> dict:
    streams_of = jax.random.split(jax.random.key(seed), 5)
    return {
        "estimate": jnp.clip(0.5 + 1.5 * jax.random.uniform(streams_of[0], (NX, NY, NZ), jnp.float32) ** block_levels(streams_of[0], (NX, NY, NZ), ((0, 4),), -0.2, 0.2), 0.5, 2.0),
        "images": jnp.clip(jnp.exp(math.log(2.0) - 1.3862944 * jax.random.uniform(streams_of[1], (N_VIEW, NX, NY // SHARES, NZ), jnp.float32) ** block_levels(streams_of[1], (N_VIEW, NX, NY // SHARES, NZ), ((0, 8), (1, 4)), -0.2, 0.2)), 0.5, 2.0).astype(jnp.bfloat16),
        "point_spread": jnp.clip(jnp.exp(jax.random.uniform(streams_of[2], (VIEWS, KX, KY, KZ), jnp.float32, math.log(0.01), math.log(1.0))), 0.01, 1.0),
        "covered": draw_covered(jax.random.fold_in(streams_of[4], 71), 0),
    }


def correlate(volume, kernel):
    rims = [((KX - 1) // 2, (KX - 1) // 2), ((KY - 1) // 2, (KY - 1) // 2), ((KZ - 1) // 2, (KZ - 1) // 2)]
    output = lax.conv_general_dilated(volume[None, None].astype(jnp.float32), kernel[None, None].astype(jnp.float32), (1, 1, 1), rims, dimension_numbers=("NCDHW", "OIDHW", "NCDHW"), precision=lax.Precision.HIGHEST)
    return output[0, 0]


def reference(estimate, images, point_spread, covered):
    source = estimate.astype(jnp.bfloat16)
    product_all = jnp.ones(estimate.shape, jnp.float32)
    for view_id in range(VIEWS):
        kernel = (point_spread[view_id] / jnp.sum(point_spread[view_id])).astype(jnp.bfloat16)
        image = jnp.concatenate([images[view_id * SHARES + share] for share in range(SHARES)], axis=1)
        coverage = jnp.repeat(jnp.repeat(covered[view_id], SX, axis=0), BY, axis=1)[:, :, None] > 0
        blurred = correlate(source, kernel)
        quotient = jnp.where(coverage, image.astype(jnp.float32) / blurred, 0.0).astype(jnp.bfloat16)
        correction = correlate(quotient, kernel[::-1, ::-1, ::-1])
        product_all = product_all * jnp.where(coverage, correction, 1.0)
    return estimate * product_all
```

```python
import functools

import jax
import jax.numpy as jnp
from jax import lax
from jax.experimental import pallas as pl
from jax.experimental.pallas import tpu as pltpu
from jax.sharding import PartitionSpec as P

CAP = 3
LANES = 128
PAD = 8
VMEM_LIMIT = 24 * 1024 * 1024


def swap_cores(cells):
    count = lax.axis_size("view")
    return lax.ppermute(cells, "view", [(i, i ^ 1) for i in range(count)])


def swap_chips(cells, step):
    count = lax.axis_size("view")
    return lax.ppermute(cells, "view", [(i, i ^ (2 * step)) for i in range(count)])


def swap_layers(cells):
    views, layers = lax.axis_size("view"), lax.axis_size("blk")
    route = []
    for chip in range(views // 2):
        for layer in range(layers - 1):
            low = (2 * chip + 1) * layers + layer
            high = 2 * chip * layers + layer + 1
            route += [(low, high), (high, low)]
    return lax.ppermute(cells, ("view", "blk"), route)


def window_of(cov, view, blocks, window):
    first = jnp.int32(blocks - window)
    for block in range(blocks - window - 1, -1, -1):
        first = jnp.where(cov[view, 0, block] > 0, jnp.int32(block), first)
    return first


def window_mask(cov, view, first, window, block_width):
    row = lax.broadcasted_iota(jnp.int32, (window * block_width, LANES), 0)
    mask = jnp.zeros(row.shape, jnp.int32)
    for block in range(window):
        inside = (row >= block * block_width) & (row < (block + 1) * block_width)
        mask = jnp.where(inside, cov[view, 0, first + block], mask)
    return mask > 0


def tables_kernel(ids, spread, fwd, bwd, rows_f, rows_b, *, taps):
    taps_x, taps_y, taps_z = taps
    rim_z = (taps_z - 1) // 2
    depth = LANES
    row = lax.broadcasted_iota(jnp.int32, (depth, depth), 0)
    col = lax.broadcasted_iota(jnp.int32, (depth, depth), 1)
    band = jnp.abs(row - col) <= rim_z
    real = row < taps_z
    at_f = rim_z - row
    at_b = row - rim_z
    place_f = ((col == at_f) | (col == at_f + depth)) & real
    place_b = ((col == at_b) | (col == at_b + depth)) & real
    place_f = jnp.where(place_f, 1.0, 0.0).astype(jnp.bfloat16)
    place_b = jnp.where(place_b, 1.0, 0.0).astype(jnp.bfloat16)
    for j in range(fwd.shape[0]):
        taps_all = spread[ids[1] * fwd.shape[0] + j]
        kernel = (taps_all / jnp.sum(taps_all)).astype(jnp.bfloat16)
        kernel = kernel.reshape(-1, LANES)
        rows_f[...] = jnp.dot(kernel, place_f, preferred_element_type=jnp.float32)
        rows_b[...] = jnp.dot(kernel, place_b, preferred_element_type=jnp.float32)
        zero = jnp.zeros((taps_y * depth, depth), jnp.bfloat16)
        for table in (fwd, bwd):
            table[j, 0] = zero
            table[j, taps_x + 1] = zero

        def fill(a, carry):
            for b in range(taps_y):
                for table, source, at in (
                    (fwd, rows_f, a * 8 + b),
                    (bwd, rows_b, (taps_x - 1 - a) * 8 + (taps_y - 1 - b)),
                ):
                    line = jnp.broadcast_to(source[pl.ds(at, 1), :], (depth, depth))
                    line = pltpu.roll(line, 0, 1, stride=1, stride_axis=0)
                    line = jnp.where(band, line, 0.0).astype(jnp.bfloat16)
                    table[j, a + 1, b * depth : (b + 1) * depth, :] = line
            return carry

        lax.fori_loop(0, taps_x, fill, 0)


def fill_columns(pad, cols, taps_y, rows_y):
    rim_y = (taps_y - 1) // 2

    def fill(x, carry):
        for b in range(taps_y):
            low = PAD - rim_y + b
            cols[x, :, b * LANES : (b + 1) * LANES] = pad[x, low : low + rows_y, :].astype(
                jnp.bfloat16
            )
        return carry

    lax.fori_loop(0, pad.shape[0], fill, 0)


def band_dots(cols, y_start, rows_y, table, j, pairs):
    steps = (table.shape[1] - 1) // 2
    total = None
    for s in range(steps):
        left = jnp.concatenate(
            [
                jnp.concatenate(
                    [cols[2 * (i + s) + u, pl.ds(y_start, rows_y), :] for u in range(2)], axis=1
                )
                for i in pairs
            ],
            axis=0,
        )
        right = jnp.concatenate(
            [
                jnp.concatenate([table[j, 2 * s + u + 1], table[j, 2 * s + u]], axis=1)
                for u in range(2)
            ],
            axis=0,
        )
        part = jnp.dot(left, right, preferred_element_type=jnp.float32)
        total = part if total is None else total + part
    return total


def blur_kernel(
    ids, cov, est, halo, img_own, img_other, fwd, quot, remote, near, pad, cols, image, *, taps
):
    core = ids[0]
    views, half, rows_y, depth = quot.shape
    rim = halo.shape[0]
    width = est.shape[1]
    blocks = cov.shape[2]
    block_width = width // blocks
    window = rows_y // block_width
    share_w = img_own.shape[2]
    margin = jnp.zeros((pad.shape[0], PAD, depth), jnp.float32)
    pad[:, :PAD, :] = margin
    pad[:, PAD + width :, :] = margin
    for r in range(half + rim):
        pad[rim * (1 - core) + r, PAD : PAD + width, :] = est[rim * core + r]
    for r in range(rim):
        pad[(half + rim) * core + r, PAD : PAD + width, :] = halo[r].astype(jnp.float32)
    fill_columns(pad, cols, taps[1], width)
    for r in range(half):
        if views == 1:
            own_at = pl.multiple_of(core * share_w, share_w)
            other_at = pl.multiple_of((1 - core) * share_w, share_w)
            image[0, r, pl.ds(own_at, share_w), :] = img_own[0, half * core + r]
            image[0, r, pl.ds(other_at, share_w), :] = img_other[r]
        else:
            image[core, r] = img_own[0, half * core + r]
            image[1 - core, r] = img_other[r]
    for j in range(views):
        view = ids[1] * views + j
        first = window_of(cov, view, blocks, window)
        mask = window_mask(cov, view, first, window, block_width)
        y_start = pl.multiple_of(first * block_width, block_width)
        blurred = band_dots(cols, y_start, rows_y, fwd, j, range(half // 2))
        remote[j] = jnp.zeros(remote.shape[1:], remote.dtype)
        for r in range(half):
            cells = image[j, r, pl.ds(y_start, rows_y), :]
            i, w = r // 2, r % 2
            below = blurred[i * rows_y : (i + 1) * rows_y, w * depth : (w + 1) * depth]
            ratio = jnp.where(mask, cells.astype(jnp.float32) / below, 0.0)
            quot[j, r] = ratio.astype(jnp.bfloat16)
        for r in range(rim):
            remote[j, r, pl.ds(y_start, rows_y), :] = quot[j, rim * core + r]
            near[j, r] = quot[j, rim * (1 - core) + r]


def correct_kernel(ids, cov, quot, near, remote, bwd, *rest, taps):
    *pieces, pad, cols, far, product = rest
    core, chip = ids[0], ids[1]
    views, half, rows_y, depth = quot.shape
    rim = near.shape[1]
    width = remote.shape[2]
    blocks = cov.shape[2]
    block_width = width // blocks
    window = rows_y // block_width
    product[...] = jnp.ones(product.shape, jnp.float32)
    far[...] = jnp.zeros(far.shape, jnp.float32)
    pad[...] = jnp.zeros(pad.shape, jnp.float32)
    for j in range(views):
        view = ids[1] * views + j
        first = window_of(cov, view, blocks, window)
        mask = window_mask(cov, view, first, window, block_width)
        y_start = pl.multiple_of(first * block_width, block_width)
        for r in range(half):
            pad[rim + r, PAD : PAD + rows_y, :] = quot[j, r].astype(jnp.float32)
        for r in range(rim):
            pad[(half + rim) * (1 - core) + r, PAD : PAD + rows_y, :] = near[j, r].astype(
                jnp.float32
            )
            far[PAD : PAD + width, :] = remote[j, r].astype(jnp.float32)
            pad[(half + rim) * core + r] = far[pl.ds(y_start, rows_y + 2 * PAD), :]
        fill_columns(pad, cols, taps[1], rows_y)
        pad[...] = jnp.zeros(pad.shape, jnp.float32)
        correction = band_dots(cols, 0, rows_y, bwd, j, range(half // 2))
        for r in range(half):
            i, w = r // 2, r % 2
            cells = correction[i * rows_y : (i + 1) * rows_y, w * depth : (w + 1) * depth]
            factor = jnp.where(mask, cells, 1.0)
            at = (r, pl.ds(y_start, rows_y), slice(None))
            product[at] = product[at] * factor
    rows = half // len(pieces)
    for step, piece in enumerate(pieces):
        for r in range(rows):
            piece[r] = product[(chip ^ step) * rows + r]


def combine_kernel(ids, est, *rest):
    *pieces, out = rest
    core, chip = ids[0], ids[1]
    rows = out.shape[0]
    half = est.shape[0] // 2
    for r in range(rows):
        total = est[half * core + chip * rows + r]
        for piece in pieces:
            total = total * piece[r]
        out[r] = total


def gather_kernel(ids, *rest):
    *pieces, out = rest
    core, chip = ids[0], ids[1]
    count = len(pieces) // 2
    rows = pieces[0].shape[0]
    half = out.shape[0] // 2
    for step in range(count):
        for r in range(rows):
            at = (chip ^ step) * rows + r
            out[half * core + at] = pieces[step][r]
            out[half * (1 - core) + at] = pieces[count + step][r]


def call(kernel, name, outs, kinds, scratch=(), flops=0):
    spaces = {"s": pltpu.SMEM, "v": pltpu.VMEM}
    return pl.pallas_call(
        kernel,
        name=name,
        out_shape=outs,
        in_specs=[pl.BlockSpec(memory_space=spaces[kind]) for kind in kinds],
        out_specs=jax.tree.map(lambda _: pl.BlockSpec(memory_space=pltpu.VMEM), outs),
        scratch_shapes=list(scratch),
        compiler_params=pltpu.CompilerParams(vmem_limit_bytes=VMEM_LIMIT),
        cost_estimate=pl.CostEstimate(flops=flops, bytes_accessed=1 << 20, transcendentals=0),
    )


def local(estimate, images, point_spread, covered):
    slab_x, width, depth = estimate.shape
    share_w = images.shape[2]
    _, taps_x, taps_y, taps_z = point_spread.shape
    taps = (taps_x, taps_y, taps_z)
    rim = (taps_x - 1) // 2
    half = slab_x // 2
    blocks = covered.shape[2]
    window = min(CAP, blocks)
    rows_y = window * (width // blocks)
    shares = width // share_w
    views = 2 // shares
    assert shares * views == 2
    group = lax.axis_index("view")
    chips = lax.axis_size("view") // 2
    core, chip = group % 2, group // 2
    ids = jnp.stack([core, chip]).astype(jnp.int32)
    reach = half + 2 * rim
    f32, bf16 = jnp.float32, jnp.bfloat16

    edge = lax.dynamic_slice_in_dim(estimate, (slab_x - rim) * core, rim, 0).astype(bf16)
    halo = swap_layers(edge)
    given = lax.dynamic_slice_in_dim(images[0], half * (1 - core), half, 0)
    img_other = swap_cores(given)

    spread = jnp.pad(point_spread, ((0, 0), (0, 0), (0, 8 - taps_y), (0, depth - taps_z)))
    table = pltpu.VMEM((views, taps_x + 2, taps_y * depth, depth), bf16)
    fwd, bwd = call(
        functools.partial(tables_kernel, taps=taps),
        "tables",
        (table, table),
        "sv",
        [pltpu.VMEM((taps_x * 8, depth), f32)] * 2,
    )(ids, spread)

    work = 2 * half * rows_y * depth * taps_x * taps_y * depth * views
    quot, remote, near = call(
        functools.partial(blur_kernel, taps=taps),
        "blur",
        (
            jax.ShapeDtypeStruct((views, half, rows_y, depth), bf16),
            jax.ShapeDtypeStruct((views, rim, width, depth), bf16),
            jax.ShapeDtypeStruct((views, rim, rows_y, depth), bf16),
        ),
        "ssvvvvv",
        [
            pltpu.VMEM((reach, width + 2 * PAD, depth), f32),
            pltpu.VMEM((reach, width, taps_y * depth), bf16),
            pltpu.VMEM((views, half, width, depth), bf16),
        ],
        work,
    )(ids, covered, estimate, halo, images, img_other, fwd)
    remote = swap_layers(remote)
    near = swap_cores(near)

    rows = half // chips
    pieces = call(
        functools.partial(correct_kernel, taps=taps),
        "correct",
        tuple(jax.ShapeDtypeStruct((rows, width, depth), f32) for _ in range(chips)),
        "ssvvvv",
        [
            pltpu.VMEM((reach, rows_y + 2 * PAD, depth), f32),
            pltpu.VMEM((reach, rows_y, taps_y * depth), bf16),
            pltpu.VMEM((width + 2 * PAD, depth), f32),
            pltpu.VMEM((half, width, depth), f32),
        ],
        work,
    )(ids, covered, quot, near, remote, bwd)
    arrived = [pieces[0]] + [swap_chips(pieces[step], step) for step in range(1, chips)]
    mine = call(
        combine_kernel,
        "combine",
        jax.ShapeDtypeStruct((rows, width, depth), f32),
        "sv" + "v" * chips,
    )(ids, estimate, *arrived)
    column = [mine] + [swap_chips(mine, step) for step in range(1, chips)]
    across = [swap_cores(piece) for piece in column]
    return call(
        gather_kernel,
        "gather",
        jax.ShapeDtypeStruct(estimate.shape, f32),
        "s" + "v" * (2 * chips),
    )(ids, *column, *across)


def solution(mesh):
    in_specs = (P("blk", None, None), P("view", "blk", None, None), P(), P(None, "blk", None))
    out_specs = P("blk", None, None)
    return jax.shard_map(local, mesh=mesh, in_specs=in_specs, out_specs=out_specs, check_vma=False)
```

```python
import functools

import jax
import jax.numpy as jnp
from jax import lax
from jax.experimental import pallas as pl
from jax.experimental.pallas import tpu as pltpu
from jax.sharding import PartitionSpec as P

CAP = 3
LANES = 128
PAD = 8
HEADER = 16
MARK = 256.0
LEVEL = 32767.0
SPAN = 16.6
VMEM_LIMIT = 24 * 1024 * 1024


def swap_cores(cells):
    count = lax.axis_size("view")
    return lax.ppermute(cells, "view", [(i, i ^ 1) for i in range(count)])


def swap_chips(cells, step):
    count = lax.axis_size("view")
    return lax.ppermute(cells, "view", [(i, i ^ (2 * step)) for i in range(count)])


def swap_layers(cells):
    views, layers = lax.axis_size("view"), lax.axis_size("blk")
    route = []
    for chip in range(views // 2):
        for layer in range(layers - 1):
            low = (2 * chip + 1) * layers + layer
            high = 2 * chip * layers + layer + 1
            route += [(low, high), (high, low)]
    return lax.ppermute(cells, ("view", "blk"), route)


def code_header(low, high):
    low_mark = jnp.floor(low * MARK)
    span_mark = jnp.floor(high * MARK) + 1.0 - low_mark
    row = lax.broadcasted_iota(jnp.int32, (HEADER, LANES), 0)
    header = jnp.where(row == 0, low_mark, span_mark).astype(jnp.int32).astype(jnp.int16)
    return header, low_mark / MARK, (2 * LEVEL * MARK) / span_mark


def encode(logs, low, scale):
    steps = (logs - low) * scale - (LEVEL - 0.5)
    steps = jnp.clip(jnp.floor(steps), -LEVEL, LEVEL)
    return steps.astype(jnp.int32).astype(jnp.int16)


def code_marks(piece):
    header = piece[:HEADER, :].astype(jnp.int32).astype(jnp.float32)
    step = header[1:2, :] * (1.0 / (2 * LEVEL * MARK))
    return header[0:1, :] * (1.0 / MARK) + step * LEVEL, step


def decode(piece, marks, at, rows):
    middle, step = marks
    cells = piece[at : at + rows, :].astype(jnp.int32).astype(jnp.float32)
    return cells * step + middle


def window_of(cov, view, blocks, window):
    first = jnp.int32(blocks - window)
    for block in range(blocks - window - 1, -1, -1):
        first = jnp.where(cov[view, 0, block] > 0, jnp.int32(block), first)
    return first


def window_mask(cov, view, first, window, block_width):
    row = lax.broadcasted_iota(jnp.int32, (window * block_width, LANES), 0)
    mask = jnp.zeros(row.shape, jnp.int32)
    for block in range(window):
        inside = (row >= block * block_width) & (row < (block + 1) * block_width)
        mask = jnp.where(inside, cov[view, 0, first + block], mask)
    return mask > 0


def tables_kernel(ids, spread, fwd, bwd, rows_f, rows_b, *, taps):
    taps_x, taps_y, taps_z = taps
    rim_z = (taps_z - 1) // 2
    depth = LANES
    row = lax.broadcasted_iota(jnp.int32, (depth, depth), 0)
    col = lax.broadcasted_iota(jnp.int32, (depth, depth), 1)
    band = jnp.abs(row - col) <= rim_z
    real = row < taps_z
    at_f = rim_z - row
    at_b = row - rim_z
    place_f = ((col == at_f) | (col == at_f + depth)) & real
    place_b = ((col == at_b) | (col == at_b + depth)) & real
    place_f = jnp.where(place_f, 1.0, 0.0).astype(jnp.bfloat16)
    place_b = jnp.where(place_b, 1.0, 0.0).astype(jnp.bfloat16)
    for j in range(fwd.shape[0]):
        taps_all = spread[ids[1] * fwd.shape[0] + j]
        kernel = (taps_all / jnp.sum(taps_all)).astype(jnp.bfloat16)
        kernel = kernel.reshape(-1, LANES)
        rows_f[...] = jnp.dot(kernel, place_f, preferred_element_type=jnp.float32)
        rows_b[...] = jnp.dot(kernel, place_b, preferred_element_type=jnp.float32)
        zero = jnp.zeros((taps_y * depth, depth), jnp.bfloat16)
        for table in (fwd, bwd):
            table[j, 0] = zero
            table[j, taps_x + 1] = zero

        def fill(a, carry):
            for b in range(taps_y):
                for table, source, at in (
                    (fwd, rows_f, a * 8 + b),
                    (bwd, rows_b, (taps_x - 1 - a) * 8 + (taps_y - 1 - b)),
                ):
                    line = jnp.broadcast_to(source[pl.ds(at, 1), :], (depth, depth))
                    line = pltpu.roll(line, 0, 1, stride=1, stride_axis=0)
                    line = jnp.where(band, line, 0.0).astype(jnp.bfloat16)
                    table[j, a + 1, b * depth : (b + 1) * depth, :] = line
            return carry

        lax.fori_loop(0, taps_x, fill, 0)


def fill_columns(pad, cols, taps_y, rows_y):
    rim_y = (taps_y - 1) // 2

    def fill(x, carry):
        for b in range(taps_y):
            low = PAD - rim_y + b
            cols[x, :, b * LANES : (b + 1) * LANES] = pad[x, low : low + rows_y, :].astype(
                jnp.bfloat16
            )
        return carry

    lax.fori_loop(0, pad.shape[0], fill, 0)


def band_dots(cols, y_start, rows_y, table, j, pairs):
    steps = (table.shape[1] - 1) // 2
    total = None
    for s in range(steps):
        left = jnp.concatenate(
            [
                jnp.concatenate(
                    [cols[2 * (i + s) + u, pl.ds(y_start, rows_y), :] for u in range(2)], axis=1
                )
                for i in pairs
            ],
            axis=0,
        )
        right = jnp.concatenate(
            [
                jnp.concatenate([table[j, 2 * s + u + 1], table[j, 2 * s + u]], axis=1)
                for u in range(2)
            ],
            axis=0,
        )
        part = jnp.dot(left, right, preferred_element_type=jnp.float32)
        total = part if total is None else total + part
    return total


def blur_kernel(
    ids, cov, est, halo, img_own, img_other, fwd, quot, remote, near, pad, cols, image, *, taps
):
    core = ids[0]
    views, half, rows_y, depth = quot.shape
    rim = halo.shape[0]
    width = est.shape[1]
    blocks = cov.shape[2]
    block_width = width // blocks
    window = rows_y // block_width
    share_w = img_own.shape[2]
    margin = jnp.zeros((pad.shape[0], PAD, depth), jnp.float32)
    pad[:, :PAD, :] = margin
    pad[:, PAD + width :, :] = margin
    for r in range(half + rim):
        pad[rim * (1 - core) + r, PAD : PAD + width, :] = est[rim * core + r]
    for r in range(rim):
        pad[(half + rim) * core + r, PAD : PAD + width, :] = halo[r].astype(jnp.float32)
    fill_columns(pad, cols, taps[1], width)
    for r in range(half):
        if views == 1:
            own_at = pl.multiple_of(core * share_w, share_w)
            other_at = pl.multiple_of((1 - core) * share_w, share_w)
            image[0, r, pl.ds(own_at, share_w), :] = img_own[0, half * core + r]
            image[0, r, pl.ds(other_at, share_w), :] = img_other[r]
        else:
            image[core, r] = img_own[0, half * core + r]
            image[1 - core, r] = img_other[r]
    for j in range(views):
        view = ids[1] * views + j
        first = window_of(cov, view, blocks, window)
        mask = window_mask(cov, view, first, window, block_width)
        y_start = pl.multiple_of(first * block_width, block_width)
        blurred = band_dots(cols, y_start, rows_y, fwd, j, range(half // 2))
        remote[j] = jnp.zeros(remote.shape[1:], remote.dtype)
        for r in range(half):
            cells = image[j, r, pl.ds(y_start, rows_y), :]
            i, w = r // 2, r % 2
            below = blurred[i * rows_y : (i + 1) * rows_y, w * depth : (w + 1) * depth]
            ratio = jnp.where(mask, cells.astype(jnp.float32) / below, 0.0)
            quot[j, r] = ratio.astype(jnp.bfloat16)
        for r in range(rim):
            remote[j, r, pl.ds(y_start, rows_y), :] = quot[j, rim * core + r]
            near[j, r] = quot[j, rim * (1 - core) + r]


def correct_kernel(ids, cov, quot, near, remote, bwd, *rest, taps):
    *pieces, pad, cols, far, product, logs = rest
    core, chip = ids[0], ids[1]
    views, half, rows_y, depth = quot.shape
    rim = near.shape[1]
    width = remote.shape[2]
    blocks = cov.shape[2]
    block_width = width // blocks
    window = rows_y // block_width
    product[...] = jnp.ones(product.shape, jnp.float32)
    far[...] = jnp.zeros(far.shape, jnp.float32)
    pad[...] = jnp.zeros(pad.shape, jnp.float32)
    for j in range(views):
        view = ids[1] * views + j
        first = window_of(cov, view, blocks, window)
        mask = window_mask(cov, view, first, window, block_width)
        y_start = pl.multiple_of(first * block_width, block_width)
        for r in range(half):
            pad[rim + r, PAD : PAD + rows_y, :] = quot[j, r].astype(jnp.float32)
        for r in range(rim):
            pad[(half + rim) * (1 - core) + r, PAD : PAD + rows_y, :] = near[j, r].astype(
                jnp.float32
            )
            far[PAD : PAD + width, :] = remote[j, r].astype(jnp.float32)
            pad[(half + rim) * core + r] = far[pl.ds(y_start, rows_y + 2 * PAD), :]
        fill_columns(pad, cols, taps[1], rows_y)
        pad[...] = jnp.zeros(pad.shape, jnp.float32)
        correction = band_dots(cols, 0, rows_y, bwd, j, range(half // 2))
        for r in range(half):
            i, w = r // 2, r % 2
            cells = correction[i * rows_y : (i + 1) * rows_y, w * depth : (w + 1) * depth]
            factor = jnp.where(mask, cells, 1.0)
            at = (r, pl.ds(y_start, rows_y), slice(None))
            product[at] = product[at] * factor
    rows = half // len(pieces)
    least = jnp.full((width, depth), jnp.inf, jnp.float32)
    most = -least
    for r in range(half):
        cells = jnp.log(product[r])
        logs[r] = cells
        least = jnp.minimum(least, cells)
        most = jnp.maximum(most, cells)
    header, low, scale = code_header(jnp.min(least), jnp.max(most))
    for r in range(rows):
        pieces[0][r] = product[chip * rows + r]
    for step in range(1, len(pieces)):
        pieces[step][:HEADER, :] = header
        for r in range(rows):
            at = HEADER + r * width
            pieces[step][at : at + width, :] = encode(logs[(chip ^ step) * rows + r], low, scale)


def combine_kernel(ids, est, own, *rest):
    *pieces, out = rest
    core, chip = ids[0], ids[1]
    rows, width, _ = own.shape
    half = est.shape[0] // 2
    marks = [code_marks(piece) for piece in pieces]
    all_logs = []
    for r in range(rows):
        logs = jnp.log(est[half * core + chip * rows + r] * own[r])
        for piece, mark in zip(pieces, marks):
            logs = logs + decode(piece, mark, HEADER + r * width, width)
        all_logs.append(logs)
    low = functools.reduce(jnp.minimum, all_logs)
    high = functools.reduce(jnp.maximum, all_logs)
    high = jnp.max(high)
    header, low, scale = code_header(jnp.maximum(jnp.min(low), high - SPAN), high)
    out[:HEADER, :] = header
    for r, logs in enumerate(all_logs):
        at = HEADER + r * width
        out[at : at + width, :] = encode(logs, low, scale)


def gather_kernel(ids, *rest):
    *pieces, out = rest
    core, chip = ids[0], ids[1]
    count = len(pieces) // 2
    width = out.shape[1]
    half = out.shape[0] // 2
    rows = half // count
    for place, piece in enumerate(pieces):
        side = core if place < count else 1 - core
        marks = code_marks(piece)
        for r in range(rows):
            at = half * side + (chip ^ (place % count)) * rows + r
            out[at] = jnp.exp(decode(piece, marks, HEADER + r * width, width))


def call(kernel, name, outs, kinds, scratch=(), flops=0):
    spaces = {"s": pltpu.SMEM, "v": pltpu.VMEM}
    return pl.pallas_call(
        kernel,
        name=name,
        out_shape=outs,
        in_specs=[pl.BlockSpec(memory_space=spaces[kind]) for kind in kinds],
        out_specs=jax.tree.map(lambda _: pl.BlockSpec(memory_space=pltpu.VMEM), outs),
        scratch_shapes=list(scratch),
        compiler_params=pltpu.CompilerParams(vmem_limit_bytes=VMEM_LIMIT),
        cost_estimate=pl.CostEstimate(flops=flops, bytes_accessed=1 << 20, transcendentals=0),
    )


def local(estimate, images, point_spread, covered):
    slab_x, width, depth = estimate.shape
    share_w = images.shape[2]
    _, taps_x, taps_y, taps_z = point_spread.shape
    taps = (taps_x, taps_y, taps_z)
    rim = (taps_x - 1) // 2
    half = slab_x // 2
    blocks = covered.shape[2]
    window = min(CAP, blocks)
    rows_y = window * (width // blocks)
    shares = width // share_w
    views = 2 // shares
    assert shares * views == 2
    group = lax.axis_index("view")
    chips = lax.axis_size("view") // 2
    core, chip = group % 2, group // 2
    ids = jnp.stack([core, chip]).astype(jnp.int32)
    reach = half + 2 * rim
    f32, bf16 = jnp.float32, jnp.bfloat16

    edge = lax.dynamic_slice_in_dim(estimate, (slab_x - rim) * core, rim, 0).astype(bf16)
    halo = swap_layers(edge)
    given = lax.dynamic_slice_in_dim(images[0], half * (1 - core), half, 0)
    img_other = swap_cores(given)

    spread = jnp.pad(point_spread, ((0, 0), (0, 0), (0, 8 - taps_y), (0, depth - taps_z)))
    table = pltpu.VMEM((views, taps_x + 2, taps_y * depth, depth), bf16)
    fwd, bwd = call(
        functools.partial(tables_kernel, taps=taps),
        "tables",
        (table, table),
        "sv",
        [pltpu.VMEM((taps_x * 8, depth), f32)] * 2,
    )(ids, spread)

    work = 2 * half * rows_y * depth * taps_x * taps_y * depth * views
    quot, remote, near = call(
        functools.partial(blur_kernel, taps=taps),
        "blur",
        (
            jax.ShapeDtypeStruct((views, half, rows_y, depth), bf16),
            jax.ShapeDtypeStruct((views, rim, width, depth), bf16),
            jax.ShapeDtypeStruct((views, rim, rows_y, depth), bf16),
        ),
        "ssvvvvv",
        [
            pltpu.VMEM((reach, width + 2 * PAD, depth), f32),
            pltpu.VMEM((reach, width, taps_y * depth), bf16),
            pltpu.VMEM((views, half, width, depth), bf16),
        ],
        work,
    )(ids, covered, estimate, halo, images, img_other, fwd)
    remote = swap_layers(remote)
    near = swap_cores(near)

    rows = half // chips
    coded = jax.ShapeDtypeStruct((HEADER + rows * width, depth), jnp.int16)
    pieces = call(
        functools.partial(correct_kernel, taps=taps),
        "correct",
        (jax.ShapeDtypeStruct((rows, width, depth), f32),) + (coded,) * (chips - 1),
        "ssvvvv",
        [
            pltpu.VMEM((reach, rows_y + 2 * PAD, depth), f32),
            pltpu.VMEM((reach, rows_y, taps_y * depth), bf16),
            pltpu.VMEM((width + 2 * PAD, depth), f32),
            pltpu.VMEM((half, width, depth), f32),
            pltpu.VMEM((half, width, depth), f32),
        ],
        work,
    )(ids, covered, quot, near, remote, bwd)
    arrived = [pieces[0]] + [swap_chips(pieces[step], step) for step in range(1, chips)]
    mine = call(
        combine_kernel,
        "combine",
        coded,
        "sv" + "v" * chips,
    )(ids, estimate, *arrived)
    column = [mine] + [swap_chips(mine, step) for step in range(1, chips)]
    across = [swap_cores(piece) for piece in column]
    return call(
        gather_kernel,
        "gather",
        jax.ShapeDtypeStruct(estimate.shape, f32),
        "s" + "v" * (2 * chips),
    )(ids, *column, *across)


def solution(mesh):
    in_specs = (P("blk", None, None), P("view", "blk", None, None), P(), P(None, "blk", None))
    out_specs = P("blk", None, None)
    return jax.shard_map(local, mesh=mesh, in_specs=in_specs, out_specs=out_specs, check_vma=False)
```

```python
import functools

import jax
import jax.numpy as jnp
from jax import lax
from jax.experimental import pallas as pl
from jax.experimental.pallas import tpu as pltpu
from jax.sharding import PartitionSpec as P

CAP = 3
LANES = 128
PAD = 8
HEADER = 16
MARK = 256.0
LEVEL = 32767.0
SPAN = 16.6
VMEM_LIMIT = 24 * 1024 * 1024


def swap_cores(cells):
    count = lax.axis_size("view")
    return lax.ppermute(cells, "view", [(i, i ^ 1) for i in range(count)])


def swap_chips(cells, step):
    count = lax.axis_size("view")
    return lax.ppermute(cells, "view", [(i, i ^ (2 * step)) for i in range(count)])


def swap_layers(cells):
    views, layers = lax.axis_size("view"), lax.axis_size("blk")
    route = []
    for chip in range(views // 2):
        for layer in range(layers - 1):
            low = (2 * chip + 1) * layers + layer
            high = 2 * chip * layers + layer + 1
            route += [(low, high), (high, low)]
    return lax.ppermute(cells, ("view", "blk"), route)


def code_header(low, high):
    low_mark = jnp.floor(low * MARK)
    span_mark = jnp.floor(high * MARK) + 1.0 - low_mark
    row = lax.broadcasted_iota(jnp.int32, (HEADER, LANES), 0)
    header = jnp.where(row == 0, low_mark, span_mark).astype(jnp.int32).astype(jnp.int16)
    return header, low_mark / MARK, (2 * LEVEL * MARK) / span_mark


def encode(logs, low, scale):
    steps = (logs - low) * scale - (LEVEL - 0.5)
    steps = jnp.clip(jnp.floor(steps), -LEVEL, LEVEL)
    return steps.astype(jnp.int32).astype(jnp.int16)


def code_marks(piece):
    header = piece[:HEADER, :].astype(jnp.int32).astype(jnp.float32)
    step = header[1:2, :] * (1.0 / (2 * LEVEL * MARK))
    return header[0:1, :] * (1.0 / MARK) + step * LEVEL, step


def decode(piece, marks, at, rows):
    middle, step = marks
    cells = piece[at : at + rows, :].astype(jnp.int32).astype(jnp.float32)
    return cells * step + middle


def window_of(cov, view, blocks, window):
    first = jnp.int32(blocks - window)
    for block in range(blocks - window - 1, -1, -1):
        first = jnp.where(cov[view, 0, block] > 0, jnp.int32(block), first)
    return first


def window_mask(cov, view, first, window, block_width):
    row = lax.broadcasted_iota(jnp.int32, (window * block_width, LANES), 0)
    mask = jnp.zeros(row.shape, jnp.int32)
    for block in range(window):
        inside = (row >= block * block_width) & (row < (block + 1) * block_width)
        mask = jnp.where(inside, cov[view, 0, first + block], mask)
    return mask > 0


def canonical(core, row, last):
    return jnp.where(core == 0, row, last - row)


def payload_kernel(ids, est, images, edge, given, rows, sems):
    core = ids[0]
    rim = edge.shape[0]
    half = given.shape[0]
    copy_rows = pltpu.make_async_copy(
        est.at[pl.ds((est.shape[0] - rim) * core, rim)], rows, sems.at[0]
    )
    copy_given = pltpu.make_async_copy(
        images.at[0, pl.ds(half * (1 - core), half)], given, sems.at[1]
    )
    copy_rows.start()
    copy_given.start()
    copy_rows.wait()
    edge[...] = rows[...].astype(edge.dtype)
    copy_given.wait()


def tables_kernel(ids, spread, est, table, cols, rows, pad, sems, *, taps):
    taps_x, taps_y, taps_z = taps
    core, chip = ids[0], ids[1]
    rim_z = (taps_z - 1) // 2
    depth = LANES
    count, width = cols.shape[0], cols.shape[1]
    margin = jnp.zeros((count, PAD, depth), jnp.float32)
    pad[:, :PAD, :] = margin
    pad[:, PAD + width :, :] = margin
    copies = [
        pltpu.make_async_copy(
            est.at[canonical(core, i, est.shape[0] - 1)], pad.at[i, pl.ds(PAD, width)], sems.at[i]
        )
        for i in range(count)
    ]
    for copy in copies:
        copy.start()
    row = lax.broadcasted_iota(jnp.int32, (depth, depth), 0)
    col = lax.broadcasted_iota(jnp.int32, (depth, depth), 1)
    band = jnp.abs(row - col) <= rim_z
    at = row - rim_z
    place = ((col == at) | (col == at + depth)) & (row < taps_z)
    place = jnp.where(place, 1.0, 0.0).astype(jnp.bfloat16)
    for j in range(table.shape[0]):
        taps_all = spread[chip * table.shape[0] + j]
        kernel = (taps_all / jnp.sum(taps_all)).astype(jnp.bfloat16)
        kernel = kernel.reshape(-1, LANES)
        rows[...] = jnp.dot(kernel, place, preferred_element_type=jnp.float32)
        zero = jnp.zeros((taps_y * depth, depth), jnp.bfloat16)
        table[j, 0] = zero
        table[j, taps_x + 1] = zero

        def fill(a, carry):
            at_x = canonical(1 - core, a, taps_x - 1) * 8
            for b in range(taps_y):
                line = rows[pl.ds(at_x + (taps_y - 1 - b), 1), :]
                line = jnp.broadcast_to(line, (depth, depth))
                line = pltpu.roll(line, 0, 1, stride=1, stride_axis=0)
                line = jnp.where(band, line, 0.0).astype(jnp.bfloat16)
                table[j, a + 1, b * depth : (b + 1) * depth, :] = line
            return carry

        lax.fori_loop(0, taps_x, fill, 0)
    for copy in copies:
        copy.wait()
    fill_columns(pad, cols, taps_y, width)


def fill_columns(pad, cols, taps_y, rows_y):
    rim_y = (taps_y - 1) // 2
    for x in range(cols.shape[0]):
        for b in range(taps_y):
            low = PAD - rim_y + b
            cols[x, :, b * LANES : (b + 1) * LANES] = pad[x, low : low + rows_y, :].astype(
                jnp.bfloat16
            )


def left_side(slab, pairs, s):
    return jnp.concatenate(
        [jnp.concatenate([slab(2 * (i + s) + u) for u in range(2)], axis=1) for i in pairs], axis=0
    )


def right_side(table, j, s):
    return jnp.concatenate(
        [
            jnp.concatenate([table[j, 2 * s + u + 1], table[j, 2 * s + u]], axis=1)
            for u in range(2)
        ],
        axis=0,
    )


def right_side_turned(table, j, s):
    taps_x = table.shape[1] - 2
    taps_y = table.shape[2] // LANES
    lines = []
    for w in range(2):
        line = []
        for u in range(2):
            at = taps_x - 1 - (2 * s + u - w) + 1
            for b in range(taps_y):
                low = (taps_y - 1 - b) * LANES
                line.append(table[j, at, low : low + LANES, :])
        lines.append(jnp.concatenate(line, axis=1))
    return jnp.concatenate(lines, axis=0)


def blur_kernel(
    ids, cov, halo, img_own, img_other, cols, table, quot, remote, near, pad, edge, image, sems, *, taps
):
    core, chip = ids[0], ids[1]
    views, half, rows_y, depth = quot.shape
    rim, width, _ = halo.shape
    blocks = cov.shape[2]
    block_width = width // blocks
    window = rows_y // block_width
    share_w = img_own.shape[2]
    if views == 1:
        own_at = pl.multiple_of(core * share_w, share_w)
        other_at = pl.multiple_of((1 - core) * share_w, share_w)
        own_to = image.at[0, :, pl.ds(own_at, share_w)]
        other_to = image.at[0, :, pl.ds(other_at, share_w)]
    else:
        own_to = image.at[core]
        other_to = image.at[1 - core]
    copies = [
        pltpu.make_async_copy(img_own.at[0, pl.ds(half * core, half)], own_to, sems.at[0]),
        pltpu.make_async_copy(img_other, other_to, sems.at[1]),
    ]
    for copy in copies:
        copy.start()
    margin = jnp.zeros((rim, PAD, depth), jnp.float32)
    pad[:, :PAD, :] = margin
    pad[:, PAD + width :, :] = margin
    for x in range(rim):
        pad[x, PAD : PAD + width, :] = halo[canonical(core, x, rim - 1)].astype(jnp.float32)
    fill_columns(pad, edge, taps[1], width)
    for copy in copies:
        copy.wait()
    for j in range(views):
        view = chip * views + j
        first = window_of(cov, view, blocks, window)
        mask = window_mask(cov, view, first, window, block_width)
        y_start = pl.multiple_of(first * block_width, block_width)

        def slab(x):
            part = edge.at[x] if x < rim else cols.at[x - rim]
            return part[pl.ds(y_start, rows_y), :]

        blurred = None
        for s in range((table.shape[1] - 1) // 2):
            part = lax.dot_general(
                left_side(slab, range(half // 2), s),
                right_side_turned(table, j, s),
                (((1,), (1,)), ((), ())),
                preferred_element_type=jnp.float32,
            )
            blurred = part if blurred is None else blurred + part
        remote[j] = jnp.zeros(remote.shape[1:], remote.dtype)
        for r in range(half):
            cells = image[j, canonical(core, r, half - 1), pl.ds(y_start, rows_y), :]
            i, w = r // 2, r % 2
            below = blurred[i * rows_y : (i + 1) * rows_y, w * depth : (w + 1) * depth]
            ratio = jnp.where(mask, cells.astype(jnp.float32) / below, 0.0).astype(jnp.bfloat16)
            quot[j, r] = ratio
            if r < rim:
                remote[j, r, pl.ds(y_start, rows_y), :] = ratio
            else:
                near[j, r - rim] = ratio


def inner_kernel(quot, near, table, sums, pad, cols, *, taps):
    views, half, rows_y, depth = quot.shape
    rim = near.shape[1]
    pairs = half // 2
    steps = (table.shape[1] - 1) // 2
    margin = jnp.zeros((half + rim, PAD, depth), jnp.float32)
    for j in range(views):
        pad[j, :, :PAD, :] = margin
        pad[j, :, PAD + rows_y :, :] = margin
        for r in range(half):
            pad[j, r, PAD : PAD + rows_y, :] = quot[j, r].astype(jnp.float32)
        for r in range(rim):
            pad[j, half + rim - 1 - r, PAD : PAD + rows_y, :] = near[j, r].astype(jnp.float32)
        fill_columns(pad.at[j], cols.at[j], taps[1], rows_y)
        total = None
        for s in range(steps - 1, -1, -1):
            skip = max(0, rim // 2 - s)
            part = jnp.dot(
                left_side(lambda x: cols[j, x - rim], range(skip, pairs), s),
                right_side(table, j, s),
                preferred_element_type=jnp.float32,
            )
            if total is None:
                total = part
            elif not skip:
                total = total + part
            else:
                cut = skip * rows_y
                total = jnp.concatenate([total[:cut], total[cut:] + part], axis=0)
        sums[j] = total


def correct_kernel(ids, cov, remote, sums, table, *rest, taps):
    *pieces, pad, cols, far, product, logs = rest
    chip = ids[1]
    views, rim, width, depth = remote.shape
    half = product.shape[0]
    rows_y = cols.shape[2]
    blocks = cov.shape[2]
    block_width = width // blocks
    window = rows_y // block_width
    product[...] = jnp.ones(product.shape, jnp.float32)
    margin = jnp.zeros((rim, PAD, depth), jnp.float32)
    for j in range(views):
        view = chip * views + j
        first = window_of(cov, view, blocks, window)
        mask = window_mask(cov, view, first, window, block_width)
        y_start = pl.multiple_of(first * block_width, block_width)
        far[j, :, :PAD, :] = margin
        far[j, :, PAD + width :, :] = margin
        for r in range(rim):
            far[j, rim - 1 - r, PAD : PAD + width, :] = remote[j, r].astype(jnp.float32)
        for r in range(rim):
            pad[j, r] = far[j, r, pl.ds(y_start, rows_y + 2 * PAD), :]
        fill_columns(pad.at[j], cols.at[j], taps[1], rows_y)
        edges = [None] * (half // 2)
        for s in range(rim // 2):
            pairs = range(rim // 2 - s)
            part = jnp.dot(
                left_side(lambda x: cols[j, x], pairs, s),
                right_side(table, j, s),
                preferred_element_type=jnp.float32,
            )
            for i in pairs:
                cells = part[i * rows_y : (i + 1) * rows_y]
                edges[i] = cells if edges[i] is None else edges[i] + cells
        for r in range(half):
            i, w = r // 2, r % 2
            cells = sums[j, i * rows_y : (i + 1) * rows_y, w * depth : (w + 1) * depth]
            if edges[i] is not None:
                cells = cells + edges[i][:, w * depth : (w + 1) * depth]
            factor = jnp.where(mask, cells, 1.0)
            at = (r, pl.ds(y_start, rows_y), slice(None))
            product[at] = product[at] * factor
    rows = half // len(pieces)
    least = jnp.full((width, depth), jnp.inf, jnp.float32)
    most = -least
    for r in range(half):
        cells = jnp.log(product[r])
        logs[r] = cells
        least = jnp.minimum(least, cells)
        most = jnp.maximum(most, cells)
    header, low, scale = code_header(jnp.min(least), jnp.max(most))
    for r in range(rows):
        pieces[0][r] = product[chip * rows + r]
    for step in range(1, len(pieces)):
        pieces[step][:HEADER, :] = header
        for r in range(rows):
            at = HEADER + r * width
            pieces[step][at : at + width, :] = encode(logs[(chip ^ step) * rows + r], low, scale)


def combine_kernel(ids, est, own, *rest):
    *pieces, out, held, sems = rest
    core, chip = ids[0], ids[1]
    rows, width, _ = own.shape
    copies = [
        pltpu.make_async_copy(
            est.at[canonical(core, chip * rows + r, est.shape[0] - 1)], held.at[r], sems.at[r]
        )
        for r in range(rows)
    ]
    for copy in copies:
        copy.start()
    marks = [code_marks(piece) for piece in pieces]
    for copy in copies:
        copy.wait()
    all_logs = []
    for r in range(rows):
        logs = jnp.log(held[r] * own[r])
        for piece, mark in zip(pieces, marks):
            logs = logs + decode(piece, mark, HEADER + r * width, width)
        all_logs.append(logs)
    low = functools.reduce(jnp.minimum, all_logs)
    high = functools.reduce(jnp.maximum, all_logs)
    high = jnp.max(high)
    header, low, scale = code_header(jnp.maximum(jnp.min(low), high - SPAN), high)
    out[:HEADER, :] = header
    for r, logs in enumerate(all_logs):
        at = HEADER + r * width
        out[at : at + width, :] = encode(logs, low, scale)


def gather_kernel(ids, *rest):
    *pieces, out = rest
    core, chip = ids[0], ids[1]
    count = len(pieces) // 2
    slab_x, width, _ = out.shape
    rows = slab_x // 2 // count
    for place, piece in enumerate(pieces):
        side = core if place < count else 1 - core
        marks = code_marks(piece)
        for r in range(rows):
            at = canonical(side, (chip ^ (place % count)) * rows + r, slab_x - 1)
            out[at] = jnp.exp(decode(piece, marks, HEADER + r * width, width))


def call(kernel, name, outs, kinds, scratch=(), flops=0, out_kinds=None):
    spaces = {"s": pltpu.SMEM, "v": pltpu.VMEM, "a": pl.ANY}
    many = isinstance(outs, tuple)
    out_kinds = out_kinds or "v" * (len(outs) if many else 1)
    out_specs = tuple(pl.BlockSpec(memory_space=spaces[kind]) for kind in out_kinds)
    return pl.pallas_call(
        kernel,
        name=name,
        out_shape=outs,
        in_specs=[pl.BlockSpec(memory_space=spaces[kind]) for kind in kinds],
        out_specs=out_specs if many else out_specs[0],
        scratch_shapes=list(scratch),
        compiler_params=pltpu.CompilerParams(vmem_limit_bytes=VMEM_LIMIT),
        cost_estimate=pl.CostEstimate(flops=flops, bytes_accessed=1 << 20, transcendentals=0),
    )


def local(estimate, images, point_spread, covered):
    slab_x, width, depth = estimate.shape
    share_w = images.shape[2]
    _, taps_x, taps_y, taps_z = point_spread.shape
    taps = (taps_x, taps_y, taps_z)
    rim = (taps_x - 1) // 2
    half = slab_x // 2
    blocks = covered.shape[2]
    window = min(CAP, blocks)
    rows_y = window * (width // blocks)
    shares = width // share_w
    views = 2 // shares
    assert shares * views == 2 and half == 2 * rim and depth == LANES
    group = lax.axis_index("view")
    chips = lax.axis_size("view") // 2
    core, chip = group % 2, group // 2
    ids = jnp.stack([core, chip]).astype(jnp.int32)
    inner = half + rim
    f32, bf16 = jnp.float32, jnp.bfloat16
    shape = jax.ShapeDtypeStruct
    deep = taps_y * depth
    wide = width + 2 * PAD
    tall = rows_y + 2 * PAD
    sems = pltpu.SemaphoreType.DMA
    work = 2 * half * rows_y * depth * taps_x * taps_y * depth * views

    edge, given = call(
        payload_kernel,
        "payload",
        (shape((rim, width, depth), bf16), shape((half, share_w, depth), bf16)),
        "saa",
        [pltpu.VMEM((rim, width, depth), f32), sems((2,))],
        out_kinds="va",
    )(ids, estimate, images)
    halo = swap_layers(edge)
    img_other = swap_cores(given)

    spread = jnp.pad(point_spread, ((0, 0), (0, 0), (0, 8 - taps_y), (0, depth - taps_z)))
    table, cols = call(
        functools.partial(tables_kernel, taps=taps),
        "tables",
        (
            pltpu.VMEM((views, taps_x + 2, deep, depth), bf16),
            pltpu.VMEM((inner, width, deep), bf16),
        ),
        "sva",
        [
            pltpu.VMEM((taps_x * 8, depth), f32),
            pltpu.VMEM((inner, wide, depth), f32),
            sems((inner,)),
        ],
        work // 2,
    )(ids, spread, estimate)

    quot, remote, near = call(
        functools.partial(blur_kernel, taps=taps),
        "blur",
        (
            pltpu.VMEM((views, half, rows_y, depth), bf16),
            shape((views, rim, width, depth), bf16),
            shape((views, rim, rows_y, depth), bf16),
        ),
        "ssvaavv",
        [
            pltpu.VMEM((rim, wide, depth), f32),
            pltpu.VMEM((rim, width, deep), bf16),
            pltpu.VMEM((views, half, width, depth), bf16),
            sems((2,)),
        ],
        work,
    )(ids, covered, halo, images, img_other, cols, table)
    near = swap_cores(near)
    remote = swap_layers(remote)

    sums = call(
        functools.partial(inner_kernel, taps=taps),
        "inner",
        pltpu.VMEM((views, half // 2 * rows_y, 2 * depth), f32),
        "vvv",
        [
            pltpu.VMEM((views, inner, tall, depth), f32),
            pltpu.VMEM((views, inner, rows_y, deep), bf16),
        ],
        work,
    )(quot, near, table)

    rows = half // chips
    coded = shape((HEADER + rows * width, depth), jnp.int16)
    pieces = call(
        functools.partial(correct_kernel, taps=taps),
        "correct",
        (shape((rows, width, depth), f32),) + (coded,) * (chips - 1),
        "ssvvv",
        [
            pltpu.VMEM((views, rim, tall, depth), f32),
            pltpu.VMEM((views, rim, rows_y, deep), bf16),
            pltpu.VMEM((views, rim, wide, depth), f32),
            pltpu.VMEM((half, width, depth), f32),
            pltpu.VMEM((half, width, depth), f32),
        ],
        work // 4,
    )(ids, covered, remote, sums, table)
    arrived = [pieces[0]] + [swap_chips(pieces[step], step) for step in range(1, chips)]
    mine = call(
        combine_kernel,
        "combine",
        coded,
        "sa" + "v" * chips,
        [pltpu.VMEM((rows, width, depth), f32), sems((rows,))],
    )(ids, estimate, *arrived)
    column = [mine] + [swap_chips(mine, step) for step in range(1, chips)]
    across = [swap_cores(piece) for piece in column]
    return call(
        gather_kernel,
        "gather",
        shape(estimate.shape, f32),
        "s" + "v" * (2 * chips),
    )(ids, *column, *across)


def solution(mesh):
    in_specs = (P("blk", None, None), P("view", "blk", None, None), P(), P(None, "blk", None))
    out_specs = P("blk", None, None)
    return jax.shard_map(local, mesh=mesh, in_specs=in_specs, out_specs=out_specs, check_vma=False)
```

```python
import functools

import jax
import jax.numpy as jnp
from jax import lax
from jax.experimental import pallas as pl
from jax.experimental.pallas import tpu as pltpu
from jax.sharding import PartitionSpec as P

CAP = 3
LANES = 128
PAD = 8
MARKS = 2
HEADER = 16
MARK = 256.0
LEVEL = 32767.0
SPAN = 16.6
VMEM_LIMIT = 24 * 1024 * 1024


def swap_cores(cells):
    count = lax.axis_size("view")
    return lax.ppermute(cells, "view", [(i, i ^ 1) for i in range(count)])


def swap_chips(cells, step):
    count = lax.axis_size("view")
    return lax.ppermute(cells, "view", [(i, i ^ (2 * step)) for i in range(count)])


def swap_layers(cells):
    views, layers = lax.axis_size("view"), lax.axis_size("blk")
    route = []
    for chip in range(views // 2):
        for layer in range(layers - 1):
            low = (2 * chip + 1) * layers + layer
            high = 2 * chip * layers + layer + 1
            route += [(low, high), (high, low)]
    return lax.ppermute(cells, ("view", "blk"), route)


def code_header(low, high):
    low_mark = jnp.floor(low * MARK)
    span_mark = jnp.floor(high * MARK) + 1.0 - low_mark
    row = lax.broadcasted_iota(jnp.int32, (HEADER, LANES), 0)
    header = jnp.where(row == 0, low_mark, span_mark).astype(jnp.int32).astype(jnp.int16)
    return header, low_mark / MARK, (2 * LEVEL * MARK) / span_mark


def encode(logs, low, scale):
    steps = (logs - low) * scale - (LEVEL - 0.5)
    steps = jnp.clip(jnp.floor(steps), -LEVEL, LEVEL)
    return steps.astype(jnp.int32).astype(jnp.int16)


def code_marks(piece):
    header = piece[:HEADER, :].astype(jnp.int32).astype(jnp.float32)
    step = header[1:2, :] * (1.0 / (2 * LEVEL * MARK))
    return header[0:1, :] * (1.0 / MARK) + step * LEVEL, step


def decode(piece, marks, at, rows):
    middle, step = marks
    cells = piece[at : at + rows, :].astype(jnp.int32).astype(jnp.float32)
    return cells * step + middle


def is_covered(info, j, block):
    return ((info[MARKS + j] >> block) & 1) > 0


def window_of(info, j, blocks, window):
    first = jnp.int32(blocks - window)
    for block in range(blocks - window - 1, -1, -1):
        first = jnp.where(is_covered(info, j, block), jnp.int32(block), first)
    return first


def window_mask(info, j, first, window, block_width):
    row = lax.broadcasted_iota(jnp.int32, (window * block_width, LANES), 0)
    mask = jnp.zeros(row.shape, jnp.int32)
    for block in range(window):
        inside = (row >= block * block_width) & (row < (block + 1) * block_width)
        here = jnp.where(is_covered(info, j, first + block), 1, 0)
        mask = jnp.where(inside, here, mask)
    return mask > 0


def canonical(core, row, last):
    return jnp.where(core == 0, row, last - row)


def payload_kernel(ids, cov, spread, est, edge, cov_here, spread_here, rows, sems):
    core = ids[0]
    rim = edge.shape[0]
    far_rows = est.at[pl.ds((est.shape[0] - rim) * core, rim)]
    copies = [
        pltpu.make_async_copy(far_rows, rows, sems.at[0]),
        pltpu.make_async_copy(spread, spread_here, sems.at[1]),
        pltpu.make_async_copy(cov, cov_here, sems.at[2]),
    ]
    for copy in copies:
        copy.start()
    copies[0].wait()
    edge[...] = rows[...].astype(edge.dtype)
    for copy in copies[1:]:
        copy.wait()


def tables_kernel(
    ids, cov, spread, est, images, table, cols, info, img_own, est_own, rows, pad, sems, *, taps
):
    taps_x, taps_y, taps_z = taps
    core, chip = ids[0], ids[1]
    rim_z = (taps_z - 1) // 2
    depth = LANES
    views = table.shape[0]
    count, width = cols.shape[0], cols.shape[1]
    margin = jnp.zeros((count, PAD, depth), jnp.float32)
    pad[:, :PAD, :] = margin
    pad[:, PAD + width :, :] = margin
    copies = [
        pltpu.make_async_copy(
            est.at[canonical(core, i, est.shape[0] - 1)], pad.at[i, pl.ds(PAD, width)], sems.at[i]
        )
        for i in range(count)
    ]
    half = img_own.shape[0]
    copies.append(
        pltpu.make_async_copy(images.at[0, pl.ds(half * core, half)], img_own, sems.at[count])
    )
    for copy in copies:
        copy.start()
    row = lax.broadcasted_iota(jnp.int32, (depth, depth), 0)
    col = lax.broadcasted_iota(jnp.int32, (depth, depth), 1)
    band = jnp.abs(row - col) <= rim_z
    at = row - rim_z
    place = ((col == at) | (col == at + depth)) & (row < taps_z)
    place = jnp.where(place, 1.0, 0.0).astype(jnp.bfloat16)
    zero = jnp.zeros((taps_y * depth, depth), jnp.bfloat16)
    rows[...] = jnp.zeros(rows.shape, jnp.float32)
    total_views = spread.shape[0] // (taps_x * taps_y)
    info[0] = core
    info[1] = chip
    block = lax.broadcasted_iota(jnp.int32, cov.shape, 0)
    lane = lax.broadcasted_iota(jnp.int32, cov.shape, 1)
    bits = jnp.where(cov[...] != 0, jnp.left_shift(1, block), 0)
    for j in range(views):
        view = chip * views + j
        code = jnp.sum(jnp.where(lane == view, bits, 0).astype(jnp.float32))
        info[MARKS + j] = code.astype(jnp.int32)
        table[j, 0] = zero
        table[j, taps_x + 1] = zero
        taps_all = spread[pl.ds(view, taps_x * taps_y, stride=total_views), :]
        rows[j, : taps_x * taps_y, :taps_z] = taps_all
        weights = rows[j]
        kernel = (weights / jnp.sum(weights)).astype(jnp.bfloat16)
        rows[j] = jnp.dot(kernel, place, preferred_element_type=jnp.float32)

    def fill(a, carry):
        at_x = canonical(1 - core, a, taps_x - 1)
        for j in range(views):
            for b in range(taps_y):
                line = rows[j, pl.ds(at_x * taps_y + taps_y - 1 - b, 1), :]
                line = jnp.broadcast_to(line, (depth, depth))
                line = pltpu.roll(line, 0, 1, stride=1, stride_axis=0)
                line = jnp.where(band, line, 0.0).astype(jnp.bfloat16)
                table[j, a + 1, b * depth : (b + 1) * depth, :] = line
        return carry

    lax.fori_loop(0, taps_x, fill, 0, unroll=3)
    for copy in copies:
        copy.wait()
    fill_columns(pad, cols, taps_y, width)
    for r in range(est_own.shape[0]):
        est_own[r] = pad[chip * est_own.shape[0] + r, PAD : PAD + width, :]


def fill_columns(pad, cols, taps_y, rows_y):
    rim_y = (taps_y - 1) // 2
    for x in range(cols.shape[0]):
        for b in range(taps_y):
            low = PAD - rim_y + b
            cols[x, :, b * LANES : (b + 1) * LANES] = pad[x, low : low + rows_y, :].astype(
                jnp.bfloat16
            )


def left_side(slab, pairs, s):
    return jnp.concatenate(
        [jnp.concatenate([slab(2 * (i + s) + u) for u in range(2)], axis=1) for i in pairs], axis=0
    )


def right_side(table, j, s):
    return jnp.concatenate(
        [
            jnp.concatenate([table[j, 2 * s + u + 1], table[j, 2 * s + u]], axis=1)
            for u in range(2)
        ],
        axis=0,
    )


def right_side_turned(table, j, s):
    taps_x = table.shape[1] - 2
    taps_y = table.shape[2] // LANES
    lines = []
    for w in range(2):
        line = []
        for u in range(2):
            at = taps_x - 1 - (2 * s + u - w) + 1
            for b in range(taps_y):
                low = (taps_y - 1 - b) * LANES
                line.append(table[j, at, low : low + LANES, :])
        lines.append(jnp.concatenate(line, axis=1))
    return jnp.concatenate(lines, axis=0)


def blur_kernel(
    info, halo, img_own, img_other, cols, table, quot, remote, near, pad, edge, image, sems, *, taps, blocks
):
    core, chip = info[0], info[1]
    views, half, rows_y, depth = quot.shape
    rim, width, _ = halo.shape
    block_width = width // blocks
    window = rows_y // block_width
    share_w = img_own.shape[1]
    if views == 1:
        own_at = pl.multiple_of(core * share_w, share_w)
        other_at = pl.multiple_of((1 - core) * share_w, share_w)
        own_to = image.at[0, :, pl.ds(own_at, share_w)]
        other_to = image.at[0, :, pl.ds(other_at, share_w)]
    else:
        own_to = image.at[core]
        other_to = image.at[1 - core]
    copies = [
        pltpu.make_async_copy(img_own, own_to, sems.at[0]),
        pltpu.make_async_copy(img_other.at[pl.ds(half * core, half)], other_to, sems.at[1]),
    ]
    for copy in copies:
        copy.start()
    margin = jnp.zeros((rim, PAD, depth), jnp.float32)
    pad[:, :PAD, :] = margin
    pad[:, PAD + width :, :] = margin
    for x in range(rim):
        pad[x, PAD : PAD + width, :] = halo[canonical(core, x, rim - 1)].astype(jnp.float32)
    fill_columns(pad, edge, taps[1], width)
    for copy in copies:
        copy.wait()
    for j in range(views):
        first = window_of(info, j, blocks, window)
        mask = window_mask(info, j, first, window, block_width)
        y_start = pl.multiple_of(first * block_width, block_width)

        def slab(x):
            part = edge.at[x] if x < rim else cols.at[x - rim]
            return part[pl.ds(y_start, rows_y), :]

        blurred = None
        for s in range((table.shape[1] - 1) // 2):
            part = lax.dot_general(
                left_side(slab, range(half // 2), s),
                right_side_turned(table, j, s),
                (((1,), (1,)), ((), ())),
                preferred_element_type=jnp.float32,
            )
            blurred = part if blurred is None else blurred + part
        remote[j, :HEADER, :] = jnp.full((HEADER, depth), first, jnp.int32).astype(jnp.bfloat16)
        for r in range(half):
            cells = image[j, canonical(core, r, half - 1), pl.ds(y_start, rows_y), :]
            i, w = r // 2, r % 2
            below = blurred[i * rows_y : (i + 1) * rows_y, w * depth : (w + 1) * depth]
            ratio = jnp.where(mask, cells.astype(jnp.float32) / below, 0.0).astype(jnp.bfloat16)
            quot[j, r] = ratio
            if r < rim:
                low = HEADER + r * rows_y
                remote[j, low : low + rows_y, :] = ratio
            else:
                near[j, r - rim] = ratio


def inner_kernel(quot, near, table, sums, pad, cols, *, taps):
    views, half, rows_y, depth = quot.shape
    rim = near.shape[1]
    pairs = half // 2
    steps = (table.shape[1] - 1) // 2
    margin = jnp.zeros((half + rim, PAD, depth), jnp.float32)
    for j in range(views):
        pad[j, :, :PAD, :] = margin
        pad[j, :, PAD + rows_y :, :] = margin
        for r in range(half):
            pad[j, r, PAD : PAD + rows_y, :] = quot[j, r].astype(jnp.float32)
        for r in range(rim):
            pad[j, half + rim - 1 - r, PAD : PAD + rows_y, :] = near[j, r].astype(jnp.float32)
        fill_columns(pad.at[j], cols.at[j], taps[1], rows_y)
        total = None
        for s in range(steps - 1, -1, -1):
            skip = max(0, rim // 2 - s)
            part = jnp.dot(
                left_side(lambda x: cols[j, x - rim], range(skip, pairs), s),
                right_side(table, j, s),
                preferred_element_type=jnp.float32,
            )
            if total is None:
                total = part
            elif not skip:
                total = total + part
            else:
                cut = skip * rows_y
                total = jnp.concatenate([total[:cut], total[cut:] + part], axis=0)
        sums[j] = total


def correct_kernel(info, remote, sums, table, est_own, *rest, taps, blocks):
    *pieces, pad, cols, far, product, logs = rest
    chip = info[1]
    views, rim, rows_y, _ = cols.shape
    half, width, depth = product.shape
    block_width = width // blocks
    window = rows_y // block_width
    rows = half // len(pieces)
    product[...] = jnp.ones(product.shape, jnp.float32)
    far[...] = jnp.zeros(far.shape, jnp.float32)
    for j in range(views):
        first = window_of(info, j, blocks, window)
        mask = window_mask(info, j, first, window, block_width)
        y_start = pl.multiple_of(first * block_width, block_width)
        there = jnp.max(remote[j, :HEADER, :].astype(jnp.float32)).astype(jnp.int32)
        there = jnp.clip(there, 0, blocks - window)
        y_there = pl.multiple_of(there * block_width, block_width)
        for r in range(rim):
            low = HEADER + r * rows_y
            cells = remote[j, low : low + rows_y, :].astype(jnp.float32)
            far[j, rim - 1 - r, pl.ds(PAD + y_there, rows_y), :] = cells
        for r in range(rim):
            pad[j, r] = far[j, r, pl.ds(y_start, rows_y + 2 * PAD), :]
        fill_columns(pad.at[j], cols.at[j], taps[1], rows_y)
        edges = [None] * (half // 2)
        for s in range(rim // 2):
            pairs = range(rim // 2 - s)
            part = jnp.dot(
                left_side(lambda x: cols[j, x], pairs, s),
                right_side(table, j, s),
                preferred_element_type=jnp.float32,
            )
            for i in pairs:
                cells = part[i * rows_y : (i + 1) * rows_y]
                edges[i] = cells if edges[i] is None else edges[i] + cells
        for r in range(half):
            i, w = r // 2, r % 2
            cells = sums[j, i * rows_y : (i + 1) * rows_y, w * depth : (w + 1) * depth]
            if edges[i] is not None:
                cells = cells + edges[i][:, w * depth : (w + 1) * depth]
            factor = jnp.where(mask, cells, 1.0)
            at = (r, pl.ds(y_start, rows_y), slice(None))
            product[at] = product[at] * factor
    least = jnp.full((width, depth), jnp.inf, jnp.float32)
    most = -least
    for r in range(half):
        cells = jnp.log(product[r])
        logs[r] = cells
        least = jnp.minimum(least, cells)
        most = jnp.maximum(most, cells)
    header, low, scale = code_header(jnp.min(least), jnp.max(most))
    for r in range(rows):
        pieces[0][r] = est_own[r] * product[chip * rows + r]
    for step in range(1, len(pieces)):
        pieces[step][:HEADER, :] = header
        for r in range(rows):
            at = HEADER + r * width
            pieces[step][at : at + width, :] = encode(logs[(chip ^ step) * rows + r], low, scale)


def combine_kernel(own, *rest):
    *pieces, out = rest
    rows, width, _ = own.shape
    marks = [code_marks(piece) for piece in pieces]
    all_logs = []
    for r in range(rows):
        logs = jnp.log(own[r])
        for piece, mark in zip(pieces, marks):
            logs = logs + decode(piece, mark, HEADER + r * width, width)
        all_logs.append(logs)
    low = functools.reduce(jnp.minimum, all_logs)
    high = functools.reduce(jnp.maximum, all_logs)
    high = jnp.max(high)
    header, low, scale = code_header(jnp.maximum(jnp.min(low), high - SPAN), high)
    out[:HEADER, :] = header
    for r, logs in enumerate(all_logs):
        at = HEADER + r * width
        out[at : at + width, :] = encode(logs, low, scale)


def gather_kernel(ids, *rest):
    *pieces, out, cells, sems = rest
    core, chip = ids[0], ids[1]
    count = len(pieces) // 2
    slab_x, width, _ = out.shape
    rows = slab_x // 2 // count
    stores = []
    for place, piece in enumerate(pieces):
        side = core if place < count else 1 - core
        marks = code_marks(piece)
        for r in range(rows):
            at = canonical(side, (chip ^ (place % count)) * rows + r, slab_x - 1)
            slot = place * rows + r
            cells[slot] = jnp.exp(decode(piece, marks, HEADER + r * width, width))
            store = pltpu.make_async_copy(cells.at[slot], out.at[at], sems.at[slot])
            store.start()
            stores.append(store)
    for store in stores:
        store.wait()


def call(kernel, name, outs, kinds, scratch=(), flops=0, out_kinds=None):
    spaces = {"s": pltpu.SMEM, "v": pltpu.VMEM, "h": pltpu.HBM}
    many = isinstance(outs, tuple)
    out_kinds = out_kinds or "v" * (len(outs) if many else 1)
    out_specs = tuple(pl.BlockSpec(memory_space=spaces[kind]) for kind in out_kinds)
    return pl.pallas_call(
        kernel,
        name=name,
        out_shape=outs,
        in_specs=[pl.BlockSpec(memory_space=spaces[kind]) for kind in kinds],
        out_specs=out_specs if many else out_specs[0],
        scratch_shapes=list(scratch),
        compiler_params=pltpu.CompilerParams(vmem_limit_bytes=VMEM_LIMIT),
        cost_estimate=pl.CostEstimate(flops=flops, bytes_accessed=1 << 20, transcendentals=0),
    )


def local(estimate, images, point_spread, covered):
    slab_x, width, depth = estimate.shape
    share_w = images.shape[2]
    _, taps_x, taps_y, taps_z = point_spread.shape
    taps = (taps_x, taps_y, taps_z)
    rim = (taps_x - 1) // 2
    half = slab_x // 2
    blocks = covered.shape[2]
    window = min(CAP, blocks)
    rows_y = window * (width // blocks)
    shares = width // share_w
    views = 2 // shares
    assert shares * views == 2 and half == 2 * rim and depth == LANES
    group = lax.axis_index("view")
    chips = lax.axis_size("view") // 2
    core, chip = group % 2, group // 2
    ids = jnp.stack([core, chip]).astype(jnp.int32)
    inner = half + rim
    rows = half // chips
    f32, bf16 = jnp.float32, jnp.bfloat16
    shape = jax.ShapeDtypeStruct
    deep = taps_y * depth
    wide = width + 2 * PAD
    tall = rows_y + 2 * PAD
    sems = pltpu.SemaphoreType.DMA
    work = 2 * half * rows_y * depth * taps_x * taps_y * depth * views

    img_other = swap_cores(images[0])
    estimate = pltpu.with_memory_space_constraint(estimate, pltpu.HBM)
    images = pltpu.with_memory_space_constraint(images, pltpu.HBM)
    spread = jnp.transpose(point_spread, (1, 2, 0, 3)).reshape(-1, taps_z)
    spread = pltpu.with_memory_space_constraint(spread, pltpu.HBM)
    cov = pltpu.with_memory_space_constraint(jnp.transpose(covered[:, 0, :]), pltpu.HBM)

    edge, cov, spread = call(
        payload_kernel,
        "payload",
        (
            shape((rim, width, depth), bf16),
            pltpu.VMEM(cov.shape, jnp.int32),
            pltpu.VMEM(spread.shape, f32),
        ),
        "shhh",
        [pltpu.VMEM((rim, width, depth), f32), sems((3,))],
    )(ids, cov, spread, estimate)
    halo = swap_layers(edge)

    table, cols, info, img_own, est_own = call(
        functools.partial(tables_kernel, taps=taps),
        "tables",
        (
            pltpu.VMEM((views, taps_x + 2, deep, depth), bf16),
            pltpu.VMEM((inner, width, deep), bf16),
            shape((MARKS + views,), jnp.int32),
            pltpu.VMEM((half, share_w, depth), bf16),
            pltpu.VMEM((rows, width, depth), f32),
        ),
        "svvhh",
        [
            pltpu.VMEM((views, -(-taps_x * taps_y // 8) * 8, depth), f32),
            pltpu.VMEM((inner, wide, depth), f32),
            sems((inner + 1,)),
        ],
        work // 2,
        "vvsvv",
    )(ids, cov, spread, estimate, images)

    quot, remote, near = call(
        functools.partial(blur_kernel, taps=taps, blocks=blocks),
        "blur",
        (
            pltpu.VMEM((views, half, rows_y, depth), bf16),
            shape((views, HEADER + rim * rows_y, depth), bf16),
            shape((views, rim, rows_y, depth), bf16),
        ),
        "svvvvv",
        [
            pltpu.VMEM((rim, wide, depth), f32),
            pltpu.VMEM((rim, width, deep), bf16),
            pltpu.VMEM((views, half, width, depth), bf16),
            sems((2,)),
        ],
        work,
    )(info, halo, img_own, img_other, cols, table)
    near = swap_cores(near)
    remote = swap_layers(remote)

    sums = call(
        functools.partial(inner_kernel, taps=taps),
        "inner",
        pltpu.VMEM((views, half // 2 * rows_y, 2 * depth), f32),
        "vvv",
        [
            pltpu.VMEM((views, inner, tall, depth), f32),
            pltpu.VMEM((views, inner, rows_y, deep), bf16),
        ],
        work,
    )(quot, near, table)

    coded = shape((HEADER + rows * width, depth), jnp.int16)
    pieces = call(
        functools.partial(correct_kernel, taps=taps, blocks=blocks),
        "correct",
        (pltpu.VMEM((rows, width, depth), f32),) + (coded,) * (chips - 1),
        "svvvv",
        [
            pltpu.VMEM((views, rim, tall, depth), f32),
            pltpu.VMEM((views, rim, rows_y, deep), bf16),
            pltpu.VMEM((views, rim, wide, depth), f32),
            pltpu.VMEM((half, width, depth), f32),
            pltpu.VMEM((half, width, depth), f32),
        ],
        work // 4,
    )(info, remote, sums, table, est_own)
    arrived = [pieces[0]] + [swap_chips(pieces[step], step) for step in range(1, chips)]
    mine = call(
        combine_kernel,
        "combine",
        coded,
        "v" * chips,
    )(*arrived)
    column = [mine] + [swap_chips(mine, step) for step in range(1, chips)]
    across = [swap_cores(piece) for piece in column]
    return call(
        gather_kernel,
        "gather",
        shape(estimate.shape, f32),
        "s" + "v" * (2 * chips),
        [pltpu.VMEM(estimate.shape, f32), sems((slab_x,))],
        out_kinds="h",
    )(ids, *column, *across)


def solution(mesh):
    in_specs = (P("blk", None, None), P("view", "blk", None, None), P(), P(None, "blk", None))
    out_specs = P("blk", None, None)
    return jax.shard_map(local, mesh=mesh, in_specs=in_specs, out_specs=out_specs, check_vma=False)
```

```python
import functools

import jax
import jax.numpy as jnp
from jax import lax
from jax.experimental import pallas as pl
from jax.experimental.pallas import tpu as pltpu
from jax.sharding import PartitionSpec as P

CAP = 3
LANES = 128
PAD = 8
MARKS = 2
HEADER = 16
MARK = 256.0
LEVEL = 32767.0
SPAN = 16.6
VMEM_LIMIT = 24 * 1024 * 1024


def swap_cores(cells):
    count = lax.axis_size("view")
    return lax.ppermute(cells, "view", [(i, i ^ 1) for i in range(count)])


def swap_chips(cells, step):
    count = lax.axis_size("view")
    return lax.ppermute(cells, "view", [(i, i ^ (2 * step)) for i in range(count)])


def swap_layers(cells):
    views, layers = lax.axis_size("view"), lax.axis_size("blk")
    route = []
    for chip in range(views // 2):
        for layer in range(layers - 1):
            low = (2 * chip + 1) * layers + layer
            high = 2 * chip * layers + layer + 1
            route += [(low, high), (high, low)]
    return lax.ppermute(cells, ("view", "blk"), route)


def code_header(low, high):
    low_mark = jnp.floor(low * MARK)
    span_mark = jnp.floor(high * MARK) + 1.0 - low_mark
    row = lax.broadcasted_iota(jnp.int32, (HEADER, LANES), 0)
    header = jnp.where(row == 0, low_mark, span_mark).astype(jnp.int32).astype(jnp.int16)
    return header, low_mark / MARK, (2 * LEVEL * MARK) / span_mark


def encode(logs, low, scale):
    steps = (logs - low) * scale - (LEVEL - 0.5)
    steps = jnp.clip(jnp.floor(steps), -LEVEL, LEVEL)
    return steps.astype(jnp.int32).astype(jnp.int16)


def code_marks(piece):
    header = piece[:HEADER, :].astype(jnp.int32).astype(jnp.float32)
    step = header[1:2, :] * (1.0 / (2 * LEVEL * MARK))
    return header[0:1, :] * (1.0 / MARK) + step * LEVEL, step


def decode(piece, marks, at, rows):
    middle, step = marks
    cells = piece[at : at + rows, :].astype(jnp.int32).astype(jnp.float32)
    return cells * step + middle


def view_slot(core, j, views):
    return core ^ j if views > 1 else 0


def is_covered(info, j, block):
    return ((info[MARKS + j] >> block) & 1) > 0


def window_of(info, j, blocks, window):
    first = jnp.int32(blocks - window)
    for block in range(blocks - window - 1, -1, -1):
        first = jnp.where(is_covered(info, j, block), jnp.int32(block), first)
    return first


def window_mask(info, j, first, window, block_width):
    row = lax.broadcasted_iota(jnp.int32, (window * block_width, LANES), 0)
    mask = jnp.zeros(row.shape, jnp.int32)
    for block in range(window):
        inside = (row >= block * block_width) & (row < (block + 1) * block_width)
        here = jnp.where(is_covered(info, j, first + block), 1, 0)
        mask = jnp.where(inside, here, mask)
    return mask > 0


def canonical(core, row, last):
    return jnp.where(core == 0, row, last - row)


def payload_kernel(ids, cov, spread, est, edge, cov_here, spread_here, rows, sems):
    core = ids[0]
    rim = edge.shape[0]
    far_rows = est.at[pl.ds((est.shape[0] - rim) * core, rim)]
    copies = [
        pltpu.make_async_copy(far_rows, rows, sems.at[0]),
        pltpu.make_async_copy(spread, spread_here, sems.at[1]),
        pltpu.make_async_copy(cov, cov_here, sems.at[2]),
    ]
    for copy in copies:
        copy.start()
    copies[0].wait()
    edge[...] = rows[...].astype(edge.dtype)
    for copy in copies[1:]:
        copy.wait()


def tables_kernel(
    ids, cov, spread, est, images, table, cols, info, img_own, est_own, rows, pad, sems, *, taps
):
    taps_x, taps_y, taps_z = taps
    core, chip = ids[0], ids[1]
    rim_z = (taps_z - 1) // 2
    depth = LANES
    views = table.shape[0]
    count, width = cols.shape[0], cols.shape[1]
    margin = jnp.zeros((count, PAD, depth), jnp.float32)
    pad[:, :PAD, :] = margin
    pad[:, PAD + width :, :] = margin
    copies = [
        pltpu.make_async_copy(
            est.at[canonical(core, i, est.shape[0] - 1)], pad.at[i, pl.ds(PAD, width)], sems.at[i]
        )
        for i in range(count)
    ]
    copies.append(pltpu.make_async_copy(images.at[0], img_own, sems.at[count]))
    for copy in copies:
        copy.start()
    row = lax.broadcasted_iota(jnp.int32, (depth, depth), 0)
    col = lax.broadcasted_iota(jnp.int32, (depth, depth), 1)
    band = jnp.abs(row - col) <= rim_z
    at = row - rim_z
    place = ((col == at) | (col == at + depth)) & (row < taps_z)
    place = jnp.where(place, 1.0, 0.0).astype(jnp.bfloat16)
    zero = jnp.zeros((taps_y * depth, depth), jnp.bfloat16)
    rows[...] = jnp.zeros(rows.shape, jnp.float32)
    total_views = spread.shape[0] // (taps_x * taps_y)
    info[0] = core
    info[1] = chip
    block = lax.broadcasted_iota(jnp.int32, cov.shape, 0)
    lane = lax.broadcasted_iota(jnp.int32, cov.shape, 1)
    bits = jnp.where(cov[...] != 0, jnp.left_shift(1, block), 0)
    for j in range(views):
        view = chip * views + view_slot(core, j, views)
        code = jnp.sum(jnp.where(lane == view, bits, 0).astype(jnp.float32))
        info[MARKS + j] = code.astype(jnp.int32)
        table[j, 0] = zero
        table[j, taps_x + 1] = zero
        taps_all = spread[pl.ds(view, taps_x * taps_y, stride=total_views), :]
        rows[j, : taps_x * taps_y, :taps_z] = taps_all
        weights = rows[j]
        kernel = (weights / jnp.sum(weights)).astype(jnp.bfloat16)
        rows[j] = jnp.dot(kernel, place, preferred_element_type=jnp.float32)

    def fill(a, carry):
        at_x = canonical(1 - core, a, taps_x - 1)
        for j in range(views):
            for b in range(taps_y):
                line = rows[j, pl.ds(at_x * taps_y + taps_y - 1 - b, 1), :]
                line = jnp.broadcast_to(line, (depth, depth))
                line = pltpu.roll(line, 0, 1, stride=1, stride_axis=0)
                line = jnp.where(band, line, 0.0).astype(jnp.bfloat16)
                table[j, a + 1, b * depth : (b + 1) * depth, :] = line
        return carry

    lax.fori_loop(0, taps_x, fill, 0, unroll=3)
    for copy in copies:
        copy.wait()
    fill_columns(pad, cols, taps_y, width)
    for r in range(est_own.shape[0]):
        est_own[r] = pad[chip * est_own.shape[0] + r, PAD : PAD + width, :]


def fill_columns(pad, cols, taps_y, rows_y):
    rim_y = (taps_y - 1) // 2
    for x in range(cols.shape[0]):
        for b in range(taps_y):
            low = PAD - rim_y + b
            cols[x, :, b * LANES : (b + 1) * LANES] = pad[x, low : low + rows_y, :].astype(
                jnp.bfloat16
            )


def left_side(slab, pairs, s):
    return jnp.concatenate(
        [jnp.concatenate([slab(2 * (i + s) + u) for u in range(2)], axis=1) for i in pairs], axis=0
    )


def right_side(table, j, s):
    return jnp.concatenate(
        [
            jnp.concatenate([table[j, 2 * s + u + 1], table[j, 2 * s + u]], axis=1)
            for u in range(2)
        ],
        axis=0,
    )


def right_side_turned(table, j, s):
    taps_x = table.shape[1] - 2
    taps_y = table.shape[2] // LANES
    lines = []
    for w in range(2):
        line = []
        for u in range(2):
            at = taps_x - 1 - (2 * s + u - w) + 1
            for b in range(taps_y):
                low = (taps_y - 1 - b) * LANES
                line.append(table[j, at, low : low + LANES, :])
        lines.append(jnp.concatenate(line, axis=1))
    return jnp.concatenate(lines, axis=0)


def dot_turned(slab, pairs, table, j, s):
    return lax.dot_general(
        left_side(slab, pairs, s),
        right_side_turned(table, j, s),
        (((1,), (1,)), ((), ())),
        preferred_element_type=jnp.float32,
    )


def add_rows(total, part, cut):
    if total is None:
        return part
    if not cut:
        return total + part
    return jnp.concatenate([total[:cut], total[cut:] + part], axis=0)


def early_steps(j, rim, steps):
    return range(rim // 2 + j, steps)


def early_kernel(info, cols, table, sums, *, blocks):
    views, steps = table.shape[0], (table.shape[1] - 1) // 2
    pairs = cols.shape[0] // 3
    rim = cols.shape[0] // 3
    width = cols.shape[1]
    rows_y = sums.shape[1] // pairs
    block_width = width // blocks
    for j in range(views):
        first = window_of(info, j, blocks, rows_y // block_width)
        y_start = pl.multiple_of(first * block_width, block_width)
        total = None
        for s in early_steps(j, rim, steps):
            part = dot_turned(
                lambda x: cols[x - rim, pl.ds(y_start, rows_y), :], range(pairs), table, j, s
            )
            total = part if total is None else total + part
        sums[j] = total


def blur_kernel(
    info, halo, img_own, img_other, cols, table, early, quot, remote, near, pad, edge, image, *, taps, blocks
):
    core, chip = info[0], info[1]
    views, half, rows_y, depth = quot.shape
    rim, width, _ = halo.shape
    block_width = width // blocks
    window = rows_y // block_width
    share_w = img_own.shape[1]
    if views == 1:
        own_at = pl.multiple_of(core * share_w, share_w)
        other_at = pl.multiple_of((1 - core) * share_w, share_w)
        for r in range(half):
            image[r, pl.ds(own_at, share_w), :] = img_own[half * core + r]
            image[r, pl.ds(other_at, share_w), :] = img_other[half * core + r]
    margin = jnp.zeros((rim, PAD, depth), jnp.float32)
    pad[:, :PAD, :] = margin
    pad[:, PAD + width :, :] = margin
    for x in range(rim):
        pad[x, PAD : PAD + width, :] = halo[canonical(core, x, rim - 1)].astype(jnp.float32)
    fill_columns(pad, edge, taps[1], width)
    for j in range(views):
        first = window_of(info, j, blocks, window)
        mask = window_mask(info, j, first, window, block_width)
        y_start = pl.multiple_of(first * block_width, block_width)

        def slab(x):
            part = edge.at[x] if x < rim else cols.at[x - rim]
            return part[pl.ds(y_start, rows_y), :]

        total = early[j]
        for s in range(early_steps(j, rim, 0).start):
            total = total + dot_turned(slab, range(half // 2), table, j, s)
        blurred = [total[i * rows_y : (i + 1) * rows_y] for i in range(half // 2)]
        slot = view_slot(core, j, views)
        remote[slot, :HEADER, :] = jnp.full((HEADER, depth), first, jnp.int32).astype(jnp.bfloat16)
        for r in range(half):
            row = canonical(core, r, half - 1)
            if views == 1:
                cells = image[row, pl.ds(y_start, rows_y), :]
            else:
                cells = (img_other if j else img_own)[half * core + row, pl.ds(y_start, rows_y), :]
            i, w = r // 2, r % 2
            below = blurred[i][:, w * depth : (w + 1) * depth]
            ratio = jnp.where(mask, cells.astype(jnp.float32) / below, 0.0).astype(jnp.bfloat16)
            quot[j, r] = ratio
            if r < rim:
                low = HEADER + r * rows_y
                remote[slot, low : low + rows_y, :] = ratio
            else:
                near[slot, r - rim] = ratio


def inner_kernel(info, quot, near, table, sums, pad, cols, *, taps):
    views, half, rows_y, depth = quot.shape
    rim = near.shape[1]
    pairs = half // 2
    steps = (table.shape[1] - 1) // 2
    margin = jnp.zeros((half + rim, PAD, depth), jnp.float32)
    for j in range(views):
        pad[j, :, :PAD, :] = margin
        pad[j, :, PAD + rows_y :, :] = margin
        for r in range(half):
            pad[j, r, PAD : PAD + rows_y, :] = quot[j, r].astype(jnp.float32)
        for r in range(rim):
            pad[j, half + rim - 1 - r, PAD : PAD + rows_y, :] = near[view_slot(info[0], j, views), r].astype(
                jnp.float32
            )
        fill_columns(pad.at[j], cols.at[j], taps[1], rows_y)
        total = None
        for s in range(steps - 1, -1, -1):
            skip = max(0, rim // 2 - s)
            part = jnp.dot(
                left_side(lambda x: cols[j, x - rim], range(skip, pairs), s),
                right_side(table, j, s),
                preferred_element_type=jnp.float32,
            )
            total = add_rows(total, part, skip * rows_y)
        sums[j] = total


def correct_kernel(info, remote, sums, table, est_own, *rest, taps, blocks):
    *pieces, pad, cols, far, product, logs = rest
    chip = info[1]
    views, rim, rows_y, _ = cols.shape
    half, width, depth = product.shape
    block_width = width // blocks
    window = rows_y // block_width
    rows = half // len(pieces)
    product[...] = jnp.ones(product.shape, jnp.float32)
    far[...] = jnp.zeros(far.shape, jnp.float32)
    for j in range(views):
        first = window_of(info, j, blocks, window)
        mask = window_mask(info, j, first, window, block_width)
        y_start = pl.multiple_of(first * block_width, block_width)
        slot = view_slot(info[0], j, views)
        there = jnp.max(remote[slot, :HEADER, :].astype(jnp.float32)).astype(jnp.int32)
        there = jnp.clip(there, 0, blocks - window)
        y_there = pl.multiple_of(there * block_width, block_width)
        for r in range(rim):
            low = HEADER + r * rows_y
            cells = remote[slot, low : low + rows_y, :].astype(jnp.float32)
            far[j, rim - 1 - r, pl.ds(PAD + y_there, rows_y), :] = cells
        for r in range(rim):
            pad[j, r] = far[j, r, pl.ds(y_start, rows_y + 2 * PAD), :]
        fill_columns(pad.at[j], cols.at[j], taps[1], rows_y)
        edges = [None] * (half // 2)
        for s in range(rim // 2):
            pairs = range(rim // 2 - s)
            part = jnp.dot(
                left_side(lambda x: cols[j, x], pairs, s),
                right_side(table, j, s),
                preferred_element_type=jnp.float32,
            )
            for i in pairs:
                cells = part[i * rows_y : (i + 1) * rows_y]
                edges[i] = cells if edges[i] is None else edges[i] + cells
        for r in range(half):
            i, w = r // 2, r % 2
            cells = sums[j, i * rows_y : (i + 1) * rows_y, w * depth : (w + 1) * depth]
            if edges[i] is not None:
                cells = cells + edges[i][:, w * depth : (w + 1) * depth]
            factor = jnp.where(mask, cells, 1.0)
            at = (r, pl.ds(y_start, rows_y), slice(None))
            product[at] = product[at] * factor
    least = jnp.full((width, depth), jnp.inf, jnp.float32)
    most = -least
    for r in range(half):
        cells = jnp.log(product[r])
        logs[r] = cells
        least = jnp.minimum(least, cells)
        most = jnp.maximum(most, cells)
    header, low, scale = code_header(jnp.min(least), jnp.max(most))
    for r in range(rows):
        pieces[0][r] = est_own[r] * product[chip * rows + r]
    for step in range(1, len(pieces)):
        pieces[step][:HEADER, :] = header
        for r in range(rows):
            at = HEADER + r * width
            pieces[step][at : at + width, :] = encode(logs[(chip ^ step) * rows + r], low, scale)


def combine_kernel(own, *rest):
    *pieces, out = rest
    rows, width, _ = own.shape
    marks = [code_marks(piece) for piece in pieces]
    all_logs = []
    for r in range(rows):
        logs = jnp.log(own[r])
        for piece, mark in zip(pieces, marks):
            logs = logs + decode(piece, mark, HEADER + r * width, width)
        all_logs.append(logs)
    low = functools.reduce(jnp.minimum, all_logs)
    high = functools.reduce(jnp.maximum, all_logs)
    high = jnp.max(high)
    header, low, scale = code_header(jnp.maximum(jnp.min(low), high - SPAN), high)
    out[:HEADER, :] = header
    for r, logs in enumerate(all_logs):
        at = HEADER + r * width
        out[at : at + width, :] = encode(logs, low, scale)


def gather_kernel(ids, *rest):
    *pieces, out, cells, sems = rest
    core, chip = ids[0], ids[1]
    count = len(pieces) // 2
    slab_x, width, _ = out.shape
    rows = slab_x // 2 // count
    stores = []
    for place, piece in enumerate(pieces):
        side = core if place < count else 1 - core
        marks = code_marks(piece)
        for r in range(rows):
            at = canonical(side, (chip ^ (place % count)) * rows + r, slab_x - 1)
            slot = place * rows + r
            cells[slot] = jnp.exp(decode(piece, marks, HEADER + r * width, width))
            store = pltpu.make_async_copy(cells.at[slot], out.at[at], sems.at[slot])
            store.start()
            stores.append(store)
    for store in stores:
        store.wait()


def call(kernel, name, outs, kinds, scratch=(), flops=0, out_kinds=None):
    spaces = {"s": pltpu.SMEM, "v": pltpu.VMEM, "h": pltpu.HBM}
    many = isinstance(outs, tuple)
    out_kinds = out_kinds or "v" * (len(outs) if many else 1)
    out_specs = tuple(pl.BlockSpec(memory_space=spaces[kind]) for kind in out_kinds)
    return pl.pallas_call(
        kernel,
        name=name,
        out_shape=outs,
        in_specs=[pl.BlockSpec(memory_space=spaces[kind]) for kind in kinds],
        out_specs=out_specs if many else out_specs[0],
        scratch_shapes=list(scratch),
        compiler_params=pltpu.CompilerParams(vmem_limit_bytes=VMEM_LIMIT),
        cost_estimate=pl.CostEstimate(flops=flops, bytes_accessed=1 << 16, transcendentals=0),
    )


def local(estimate, images, point_spread, covered):
    slab_x, width, depth = estimate.shape
    share_w = images.shape[2]
    _, taps_x, taps_y, taps_z = point_spread.shape
    taps = (taps_x, taps_y, taps_z)
    rim = (taps_x - 1) // 2
    half = slab_x // 2
    blocks = covered.shape[2]
    window = min(CAP, blocks)
    rows_y = window * (width // blocks)
    shares = width // share_w
    views = 2 // shares
    assert shares * views == 2 and half == 2 * rim and depth == LANES
    group = lax.axis_index("view")
    chips = lax.axis_size("view") // 2
    core, chip = group % 2, group // 2
    ids = jnp.stack([core, chip]).astype(jnp.int32)
    inner = half + rim
    rows = half // chips
    f32, bf16 = jnp.float32, jnp.bfloat16
    shape = jax.ShapeDtypeStruct
    deep = taps_y * depth
    wide = width + 2 * PAD
    tall = rows_y + 2 * PAD
    sems = pltpu.SemaphoreType.DMA
    work = 2 * half * rows_y * depth * taps_x * taps_y * depth * views

    img_other = swap_cores(images[0])
    estimate = pltpu.with_memory_space_constraint(estimate, pltpu.HBM)
    images = pltpu.with_memory_space_constraint(images, pltpu.HBM)
    spread = jnp.transpose(point_spread, (1, 2, 0, 3)).reshape(-1, taps_z)
    spread = pltpu.with_memory_space_constraint(spread, pltpu.HBM)
    cov = pltpu.with_memory_space_constraint(jnp.transpose(covered[:, 0, :]), pltpu.HBM)

    edge, cov, spread = call(
        payload_kernel,
        "payload",
        (
            shape((rim, width, depth), bf16),
            pltpu.VMEM(cov.shape, jnp.int32),
            pltpu.VMEM(spread.shape, f32),
        ),
        "shhh",
        [pltpu.VMEM((rim, width, depth), f32), sems((3,))],
    )(ids, cov, spread, estimate)
    halo = swap_layers(edge)

    table, cols, info, img_own, est_own = call(
        functools.partial(tables_kernel, taps=taps),
        "tables",
        (
            pltpu.VMEM((views, taps_x + 2, deep, depth), bf16),
            pltpu.VMEM((inner, width, deep), bf16),
            shape((MARKS + views,), jnp.int32),
            pltpu.VMEM((slab_x, share_w, depth), bf16),
            pltpu.VMEM((rows, width, depth), f32),
        ),
        "svvhh",
        [
            pltpu.VMEM((views, -(-taps_x * taps_y // 8) * 8, depth), f32),
            pltpu.VMEM((inner, wide, depth), f32),
            sems((inner + 1,)),
        ],
        work // 2,
        "vvsvv",
    )(ids, cov, spread, estimate, images)

    early = call(
        functools.partial(early_kernel, blocks=blocks),
        "early",
        pltpu.VMEM((views, half // 2 * rows_y, 2 * depth), f32),
        "svv",
        flops=0,
    )(info, cols, table)

    quot, remote, near = call(
        functools.partial(blur_kernel, taps=taps, blocks=blocks),
        "blur",
        (
            pltpu.VMEM((views, half, rows_y, depth), bf16),
            shape((views, HEADER + rim * rows_y, depth), bf16),
            shape((views, rim, rows_y, depth), bf16),
        ),
        "svvvvvv",
        [
            pltpu.VMEM((rim, wide, depth), f32),
            pltpu.VMEM((rim, width, deep), bf16),
            pltpu.VMEM((half, width, depth) if views == 1 else (8, depth), bf16),
        ],
        work,
    )(info, halo, img_own, img_other, cols, table, early)
    near = swap_cores(near)
    remote = swap_layers(remote)

    sums = call(
        functools.partial(inner_kernel, taps=taps),
        "inner",
        pltpu.VMEM((views, half // 2 * rows_y, 2 * depth), f32),
        "svvv",
        [
            pltpu.VMEM((views, inner, tall, depth), f32),
            pltpu.VMEM((views, inner, rows_y, deep), bf16),
        ],
        work,
    )(info, quot, near, table)

    coded = shape((HEADER + rows * width, depth), jnp.int16)
    pieces = call(
        functools.partial(correct_kernel, taps=taps, blocks=blocks),
        "correct",
        (pltpu.VMEM((rows, width, depth), f32),) + (coded,) * (chips - 1),
        "svvvv",
        [
            pltpu.VMEM((views, rim, tall, depth), f32),
            pltpu.VMEM((views, rim, rows_y, deep), bf16),
            pltpu.VMEM((views, rim, wide, depth), f32),
            pltpu.VMEM((half, width, depth), f32),
            pltpu.VMEM((half, width, depth), f32),
        ],
        work // 4,
    )(info, remote, sums, table, est_own)
    arrived = [pieces[0]] + [swap_chips(pieces[step], step) for step in range(1, chips)]
    mine = call(
        combine_kernel,
        "combine",
        coded,
        "v" * chips,
    )(*arrived)
    column = [mine] + [swap_chips(mine, step) for step in range(1, chips)]
    across = [swap_cores(piece) for piece in column]
    return call(
        gather_kernel,
        "gather",
        shape(estimate.shape, f32),
        "s" + "v" * (2 * chips),
        [pltpu.VMEM(estimate.shape, f32), sems((slab_x,))],
        out_kinds="h",
    )(ids, *column, *across)


def solution(mesh):
    in_specs = (P("blk", None, None), P("view", "blk", None, None), P(), P(None, "blk", None))
    out_specs = P("blk", None, None)
    return jax.shard_map(local, mesh=mesh, in_specs=in_specs, out_specs=out_specs, check_vma=False)
```

```python
import functools

import jax
import jax.numpy as jnp
from jax import lax
from jax.experimental import pallas as pl
from jax.experimental.pallas import tpu as pltpu
from jax.sharding import PartitionSpec as P

CAP = 3
LANES = 128
PAD = 8
MARKS = 3
HEADER = 16
MARK = 256.0
LEVEL = 32767.0
SPAN = 16.6
VMEM_LIMIT = 24 * 1024 * 1024


def swap_cores(cells):
    count = lax.axis_size("view")
    return lax.ppermute(cells, "view", [(i, i ^ 1) for i in range(count)])


def swap_chips(cells, step):
    count = lax.axis_size("view")
    return lax.ppermute(cells, "view", [(i, i ^ (2 * step)) for i in range(count)])


def swap_layers(cells):
    views, layers = lax.axis_size("view"), lax.axis_size("blk")
    route = []
    for chip in range(views // 2):
        for layer in range(layers):
            for core in range(2):
                there = layer + (1 if core else -1)
                if 0 <= there < layers:
                    to = (2 * chip + 1 - core) * layers + there
                else:
                    to = (2 * (chip ^ 1) + core) * layers + layer
                route.append(((2 * chip + core) * layers + layer, to))
    return lax.ppermute(cells, ("view", "blk"), route)


def has_far(core):
    layer = lax.axis_index("blk")
    there = layer + 2 * core - 1
    return (there >= 0) & (there < lax.axis_size("blk"))


def code_header(low, high):
    low_mark = jnp.floor(low * MARK)
    span_mark = jnp.floor(high * MARK) + 1.0 - low_mark
    row = lax.broadcasted_iota(jnp.int32, (HEADER, LANES), 0)
    header = jnp.where(row == 0, low_mark, span_mark).astype(jnp.int32).astype(jnp.int16)
    return header, low_mark / MARK, (2 * LEVEL * MARK) / span_mark


def encode(logs, low, scale):
    steps = (logs - low) * scale - (LEVEL - 0.5)
    steps = jnp.clip(jnp.floor(steps), -LEVEL, LEVEL)
    return steps.astype(jnp.int32).astype(jnp.int16)


def code_marks(piece):
    header = piece[:HEADER, :].astype(jnp.int32).astype(jnp.float32)
    step = header[1:2, :] * (1.0 / (2 * LEVEL * MARK))
    return header[0:1, :] * (1.0 / MARK) + step * LEVEL, step


def decode(piece, marks, at, rows):
    middle, step = marks
    cells = piece[at : at + rows, :].astype(jnp.int32).astype(jnp.float32)
    return cells * step + middle


def view_slot(core, j, views):
    return core ^ j if views > 1 else 0


def is_covered(info, j, block):
    return ((info[MARKS + j] >> block) & 1) > 0


def window_of(info, j, blocks, window):
    first = jnp.int32(blocks - window)
    for block in range(blocks - window - 1, -1, -1):
        first = jnp.where(is_covered(info, j, block), jnp.int32(block), first)
    return first


def window_mask(info, j, first, window, block_width):
    row = lax.broadcasted_iota(jnp.int32, (window * block_width, LANES), 0)
    mask = jnp.zeros(row.shape, jnp.int32)
    for block in range(window):
        inside = (row >= block * block_width) & (row < (block + 1) * block_width)
        here = jnp.where(is_covered(info, j, first + block), 1, 0)
        mask = jnp.where(inside, here, mask)
    return mask > 0


def canonical(core, row, last):
    return jnp.where(core == 0, row, last - row)


def payload_kernel(ids, cov, spread, est, edge, cov_here, spread_here, rows, sems):
    core = ids[0]
    rim = edge.shape[0]
    far_rows = est.at[pl.ds((est.shape[0] - rim) * core, rim)]
    copies = [
        pltpu.make_async_copy(far_rows, rows, sems.at[0]),
        pltpu.make_async_copy(spread, spread_here, sems.at[1]),
        pltpu.make_async_copy(cov, cov_here, sems.at[2]),
    ]
    for copy in copies:
        copy.start()
    copies[0].wait()
    edge[...] = rows[...].astype(edge.dtype)
    for copy in copies[1:]:
        copy.wait()


def tables_kernel(
    ids, cov, spread, est, images, table, cols, info, img_own, est_own, rows, pad, sems, *, taps
):
    taps_x, taps_y, taps_z = taps
    core, chip = ids[0], ids[1]
    rim_z = (taps_z - 1) // 2
    depth = LANES
    views = table.shape[0]
    count, width = cols.shape[0], cols.shape[1]
    margin = jnp.zeros((count, PAD, depth), jnp.float32)
    pad[:, :PAD, :] = margin
    pad[:, PAD + width :, :] = margin
    copies = [
        pltpu.make_async_copy(
            est.at[canonical(core, i, est.shape[0] - 1)], pad.at[i, pl.ds(PAD, width)], sems.at[i]
        )
        for i in range(count)
    ]
    copies.append(pltpu.make_async_copy(images.at[0], img_own, sems.at[count]))
    for copy in copies:
        copy.start()
    row = lax.broadcasted_iota(jnp.int32, (depth, depth), 0)
    col = lax.broadcasted_iota(jnp.int32, (depth, depth), 1)
    band = jnp.abs(row - col) <= rim_z
    at = row - rim_z
    place = ((col == at) | (col == at + depth)) & (row < taps_z)
    place = jnp.where(place, 1.0, 0.0).astype(jnp.bfloat16)
    zero = jnp.zeros((taps_y * depth, depth), jnp.bfloat16)
    rows[...] = jnp.zeros(rows.shape, jnp.float32)
    total_views = spread.shape[0] // (taps_x * taps_y)
    info[0] = core
    info[1] = chip
    info[2] = ids[2]
    block = lax.broadcasted_iota(jnp.int32, cov.shape, 0)
    lane = lax.broadcasted_iota(jnp.int32, cov.shape, 1)
    bits = jnp.where(cov[...] != 0, jnp.left_shift(1, block), 0)
    for j in range(views):
        view = chip * views + view_slot(core, j, views)
        code = jnp.sum(jnp.where(lane == view, bits, 0).astype(jnp.float32))
        info[MARKS + j] = code.astype(jnp.int32)
        table[j, 0] = zero
        table[j, taps_x + 1] = zero
        taps_all = spread[pl.ds(view, taps_x * taps_y, stride=total_views), :]
        rows[j, : taps_x * taps_y, :taps_z] = taps_all
        weights = rows[j]
        kernel = (weights / jnp.sum(weights)).astype(jnp.bfloat16)
        rows[j] = jnp.dot(kernel, place, preferred_element_type=jnp.float32)

    def fill(a, carry):
        at_x = canonical(1 - core, a, taps_x - 1)
        for j in range(views):
            for b in range(taps_y):
                line = rows[j, pl.ds(at_x * taps_y + taps_y - 1 - b, 1), :]
                line = jnp.broadcast_to(line, (depth, depth))
                line = pltpu.roll(line, 0, 1, stride=1, stride_axis=0)
                line = jnp.where(band, line, 0.0).astype(jnp.bfloat16)
                table[j, a + 1, b * depth : (b + 1) * depth, :] = line
        return carry

    lax.fori_loop(0, taps_x, fill, 0, unroll=3)
    for copy in copies:
        copy.wait()
    fill_columns(pad, cols, taps_y, width)
    for r in range(est_own.shape[0]):
        est_own[r] = pad[chip * est_own.shape[0] + r, PAD : PAD + width, :]


def fill_columns(pad, cols, taps_y, rows_y):
    rim_y = (taps_y - 1) // 2
    for x in range(cols.shape[0]):
        for b in range(taps_y):
            low = PAD - rim_y + b
            cols[x, :, b * LANES : (b + 1) * LANES] = pad[x, low : low + rows_y, :].astype(
                jnp.bfloat16
            )


def left_side(slab, pairs, s):
    return jnp.concatenate(
        [jnp.concatenate([slab(2 * (i + s) + u) for u in range(2)], axis=1) for i in pairs], axis=0
    )


def right_side(table, j, s):
    return jnp.concatenate(
        [
            jnp.concatenate([table[j, 2 * s + u + 1], table[j, 2 * s + u]], axis=1)
            for u in range(2)
        ],
        axis=0,
    )


def right_side_turned(table, j, s):
    taps_x = table.shape[1] - 2
    taps_y = table.shape[2] // LANES
    lines = []
    for w in range(2):
        line = []
        for u in range(2):
            at = taps_x - 1 - (2 * s + u - w) + 1
            for b in range(taps_y):
                low = (taps_y - 1 - b) * LANES
                line.append(table[j, at, low : low + LANES, :])
        lines.append(jnp.concatenate(line, axis=1))
    return jnp.concatenate(lines, axis=0)


def dot_turned(slab, pairs, table, j, s):
    return lax.dot_general(
        left_side(slab, pairs, s),
        right_side_turned(table, j, s),
        (((1,), (1,)), ((), ())),
        preferred_element_type=jnp.float32,
    )


def add_rows(total, part, cut):
    if total is None:
        return part
    if not cut:
        return total + part
    return jnp.concatenate([total[:cut], total[cut:] + part], axis=0)


def early_steps(j, rim, steps):
    return range(rim // 2 + j, steps)


def early_kernel(info, cols, table, sums, *, blocks):
    views, steps = table.shape[0], (table.shape[1] - 1) // 2
    pairs = cols.shape[0] // 3
    rim = cols.shape[0] // 3
    width = cols.shape[1]
    rows_y = sums.shape[1] // pairs
    block_width = width // blocks
    for j in range(views):
        first = window_of(info, j, blocks, rows_y // block_width)
        y_start = pl.multiple_of(first * block_width, block_width)
        total = None
        for s in early_steps(j, rim, steps):
            part = dot_turned(
                lambda x: cols[x - rim, pl.ds(y_start, rows_y), :], range(pairs), table, j, s
            )
            total = part if total is None else total + part
        sums[j] = total


def blur_kernel(
    info, halo, img_own, img_other, cols, table, early, quot, remote, near, pad, edge, image, *, taps, blocks
):
    core, chip = info[0], info[1]
    views, half, rows_y, depth = quot.shape
    rim, width, _ = halo.shape
    block_width = width // blocks
    window = rows_y // block_width
    share_w = img_own.shape[1]
    if views == 1:
        own_at = pl.multiple_of(core * share_w, share_w)
        other_at = pl.multiple_of((1 - core) * share_w, share_w)
        for r in range(half):
            image[r, pl.ds(own_at, share_w), :] = img_own[half * core + r]
            image[r, pl.ds(other_at, share_w), :] = img_other[half * core + r]
    margin = jnp.zeros((rim, PAD, depth), jnp.float32)
    pad[:, :PAD, :] = margin
    pad[:, PAD + width :, :] = margin
    for x in range(rim):
        cells = halo[canonical(core, x, rim - 1)].astype(jnp.float32)
        pad[x, PAD : PAD + width, :] = jnp.where(info[2] > 0, cells, 0.0)
    fill_columns(pad, edge, taps[1], width)
    for j in range(views):
        first = window_of(info, j, blocks, window)
        mask = window_mask(info, j, first, window, block_width)
        y_start = pl.multiple_of(first * block_width, block_width)

        def slab(x):
            part = edge.at[x] if x < rim else cols.at[x - rim]
            return part[pl.ds(y_start, rows_y), :]

        total = early[j]
        for s in range(early_steps(j, rim, 0).start):
            total = total + dot_turned(slab, range(half // 2), table, j, s)
        blurred = [total[i * rows_y : (i + 1) * rows_y] for i in range(half // 2)]
        slot = view_slot(core, j, views)
        remote[slot, :HEADER, :] = jnp.full((HEADER, depth), first, jnp.int32).astype(jnp.bfloat16)
        for r in range(half):
            row = canonical(core, r, half - 1)
            if views == 1:
                cells = image[row, pl.ds(y_start, rows_y), :]
            else:
                cells = (img_other if j else img_own)[half * core + row, pl.ds(y_start, rows_y), :]
            i, w = r // 2, r % 2
            below = blurred[i][:, w * depth : (w + 1) * depth]
            ratio = jnp.where(mask, cells.astype(jnp.float32) / below, 0.0).astype(jnp.bfloat16)
            quot[j, r] = ratio
            if r < rim:
                low = HEADER + r * rows_y
                remote[slot, low : low + rows_y, :] = ratio
            else:
                near[slot, r - rim] = ratio


def inner_kernel(info, quot, near, table, sums, pad, cols, *, taps):
    views, half, rows_y, depth = quot.shape
    rim = near.shape[1]
    pairs = half // 2
    steps = (table.shape[1] - 1) // 2
    margin = jnp.zeros((half + rim, PAD, depth), jnp.float32)
    for j in range(views):
        pad[j, :, :PAD, :] = margin
        pad[j, :, PAD + rows_y :, :] = margin
        for r in range(half):
            pad[j, r, PAD : PAD + rows_y, :] = quot[j, r].astype(jnp.float32)
        for r in range(rim):
            pad[j, half + rim - 1 - r, PAD : PAD + rows_y, :] = near[view_slot(info[0], j, views), r].astype(
                jnp.float32
            )
        fill_columns(pad.at[j], cols.at[j], taps[1], rows_y)
        total = None
        for s in range(steps - 1, -1, -1):
            skip = max(0, rim // 2 - s)
            part = jnp.dot(
                left_side(lambda x: cols[j, x - rim], range(skip, pairs), s),
                right_side(table, j, s),
                preferred_element_type=jnp.float32,
            )
            total = add_rows(total, part, skip * rows_y)
        sums[j] = total


def correct_kernel(info, remote, sums, table, est_own, *rest, taps, blocks):
    *pieces, pad, cols, far, product, logs = rest
    chip = info[1]
    views, rim, rows_y, _ = cols.shape
    half, width, depth = product.shape
    block_width = width // blocks
    window = rows_y // block_width
    rows = half // len(pieces)
    product[...] = jnp.ones(product.shape, jnp.float32)
    far[...] = jnp.zeros(far.shape, jnp.float32)
    for j in range(views):
        first = window_of(info, j, blocks, window)
        mask = window_mask(info, j, first, window, block_width)
        y_start = pl.multiple_of(first * block_width, block_width)
        slot = view_slot(info[0], j, views)
        there = jnp.max(remote[slot, :HEADER, :].astype(jnp.float32)).astype(jnp.int32)
        there = jnp.clip(there, 0, blocks - window)
        y_there = pl.multiple_of(there * block_width, block_width)
        for r in range(rim):
            low = HEADER + r * rows_y
            cells = remote[slot, low : low + rows_y, :].astype(jnp.float32)
            cells = jnp.where(info[2] > 0, cells, 0.0)
            far[j, rim - 1 - r, pl.ds(PAD + y_there, rows_y), :] = cells
        for r in range(rim):
            pad[j, r] = far[j, r, pl.ds(y_start, rows_y + 2 * PAD), :]
        fill_columns(pad.at[j], cols.at[j], taps[1], rows_y)
        edges = [None] * (half // 2)
        for s in range(rim // 2):
            pairs = range(rim // 2 - s)
            part = jnp.dot(
                left_side(lambda x: cols[j, x], pairs, s),
                right_side(table, j, s),
                preferred_element_type=jnp.float32,
            )
            for i in pairs:
                cells = part[i * rows_y : (i + 1) * rows_y]
                edges[i] = cells if edges[i] is None else edges[i] + cells
        for r in range(half):
            i, w = r // 2, r % 2
            cells = sums[j, i * rows_y : (i + 1) * rows_y, w * depth : (w + 1) * depth]
            if edges[i] is not None:
                cells = cells + edges[i][:, w * depth : (w + 1) * depth]
            factor = jnp.where(mask, cells, 1.0)
            at = (r, pl.ds(y_start, rows_y), slice(None))
            product[at] = product[at] * factor
    least = jnp.full((width, depth), jnp.inf, jnp.float32)
    most = -least
    for r in range(half):
        cells = jnp.log(product[r])
        logs[r] = cells
        least = jnp.minimum(least, cells)
        most = jnp.maximum(most, cells)
    header, low, scale = code_header(jnp.min(least), jnp.max(most))
    for r in range(rows):
        pieces[0][r] = est_own[r] * product[chip * rows + r]
    for step in range(1, len(pieces)):
        pieces[step][:HEADER, :] = header
        for r in range(rows):
            at = HEADER + r * width
            pieces[step][at : at + width, :] = encode(logs[(chip ^ step) * rows + r], low, scale)


def combine_kernel(own, *rest):
    *pieces, out = rest
    rows, width, _ = own.shape
    marks = [code_marks(piece) for piece in pieces]
    all_logs = []
    for r in range(rows):
        logs = jnp.log(own[r])
        for piece, mark in zip(pieces, marks):
            logs = logs + decode(piece, mark, HEADER + r * width, width)
        all_logs.append(logs)
    low = functools.reduce(jnp.minimum, all_logs)
    high = functools.reduce(jnp.maximum, all_logs)
    high = jnp.max(high)
    header, low, scale = code_header(jnp.maximum(jnp.min(low), high - SPAN), high)
    out[:HEADER, :] = header
    for r, logs in enumerate(all_logs):
        at = HEADER + r * width
        out[at : at + width, :] = encode(logs, low, scale)


def gather_kernel(ids, *rest):
    *pieces, out, cells, sems = rest
    core, chip = ids[0], ids[1]
    count = len(pieces) // 2
    slab_x, width, _ = out.shape
    rows = slab_x // 2 // count
    stores = []
    for place, piece in enumerate(pieces):
        side = core if place < count else 1 - core
        marks = code_marks(piece)
        for r in range(rows):
            at = canonical(side, (chip ^ (place % count)) * rows + r, slab_x - 1)
            slot = place * rows + r
            cells[slot] = jnp.exp(decode(piece, marks, HEADER + r * width, width))
            store = pltpu.make_async_copy(cells.at[slot], out.at[at], sems.at[slot])
            store.start()
            stores.append(store)
    for store in stores:
        store.wait()


def call(kernel, name, outs, kinds, scratch=(), flops=0, out_kinds=None):
    spaces = {"s": pltpu.SMEM, "v": pltpu.VMEM, "h": pltpu.HBM}
    many = isinstance(outs, tuple)
    out_kinds = out_kinds or "v" * (len(outs) if many else 1)
    out_specs = tuple(pl.BlockSpec(memory_space=spaces[kind]) for kind in out_kinds)
    return pl.pallas_call(
        kernel,
        name=name,
        out_shape=outs,
        in_specs=[pl.BlockSpec(memory_space=spaces[kind]) for kind in kinds],
        out_specs=out_specs if many else out_specs[0],
        scratch_shapes=list(scratch),
        compiler_params=pltpu.CompilerParams(vmem_limit_bytes=VMEM_LIMIT),
        cost_estimate=pl.CostEstimate(flops=flops, bytes_accessed=1 << 16, transcendentals=0),
    )


def local(estimate, images, point_spread, covered):
    slab_x, width, depth = estimate.shape
    share_w = images.shape[2]
    _, taps_x, taps_y, taps_z = point_spread.shape
    taps = (taps_x, taps_y, taps_z)
    rim = (taps_x - 1) // 2
    half = slab_x // 2
    blocks = covered.shape[2]
    window = min(CAP, blocks)
    rows_y = window * (width // blocks)
    shares = width // share_w
    views = 2 // shares
    assert shares * views == 2 and half == 2 * rim and depth == LANES
    group = lax.axis_index("view")
    chips = lax.axis_size("view") // 2
    core, chip = group % 2, group // 2
    ids = jnp.stack([core, chip, has_far(core)]).astype(jnp.int32)
    inner = half + rim
    rows = half // chips
    f32, bf16 = jnp.float32, jnp.bfloat16
    shape = jax.ShapeDtypeStruct
    deep = taps_y * depth
    wide = width + 2 * PAD
    tall = rows_y + 2 * PAD
    sems = pltpu.SemaphoreType.DMA
    work = 2 * half * rows_y * depth * taps_x * taps_y * depth * views

    img_other = swap_cores(images[0])
    estimate = pltpu.with_memory_space_constraint(estimate, pltpu.HBM)
    images = pltpu.with_memory_space_constraint(images, pltpu.HBM)
    spread = jnp.transpose(point_spread, (1, 2, 0, 3)).reshape(-1, taps_z)
    spread = pltpu.with_memory_space_constraint(spread, pltpu.HBM)
    cov = pltpu.with_memory_space_constraint(jnp.transpose(covered[:, 0, :]), pltpu.HBM)

    edge, cov, spread = call(
        payload_kernel,
        "payload",
        (
            shape((rim, width, depth), bf16),
            pltpu.VMEM(cov.shape, jnp.int32),
            pltpu.VMEM(spread.shape, f32),
        ),
        "shhh",
        [pltpu.VMEM((rim, width, depth), f32), sems((3,))],
    )(ids, cov, spread, estimate)
    halo = swap_layers(edge)

    table, cols, info, img_own, est_own = call(
        functools.partial(tables_kernel, taps=taps),
        "tables",
        (
            pltpu.VMEM((views, taps_x + 2, deep, depth), bf16),
            pltpu.VMEM((inner, width, deep), bf16),
            shape((MARKS + views,), jnp.int32),
            pltpu.VMEM((slab_x, share_w, depth), bf16),
            pltpu.VMEM((rows, width, depth), f32),
        ),
        "svvhh",
        [
            pltpu.VMEM((views, -(-taps_x * taps_y // 8) * 8, depth), f32),
            pltpu.VMEM((inner, wide, depth), f32),
            sems((inner + 1,)),
        ],
        work // 2,
        "vvsvv",
    )(ids, cov, spread, estimate, images)

    early = call(
        functools.partial(early_kernel, blocks=blocks),
        "early",
        pltpu.VMEM((views, half // 2 * rows_y, 2 * depth), f32),
        "svv",
        flops=0,
    )(info, cols, table)

    quot, remote, near = call(
        functools.partial(blur_kernel, taps=taps, blocks=blocks),
        "blur",
        (
            pltpu.VMEM((views, half, rows_y, depth), bf16),
            shape((views, HEADER + rim * rows_y, depth), bf16),
            shape((views, rim, rows_y, depth), bf16),
        ),
        "svvvvvv",
        [
            pltpu.VMEM((rim, wide, depth), f32),
            pltpu.VMEM((rim, width, deep), bf16),
            pltpu.VMEM((half, width, depth) if views == 1 else (8, depth), bf16),
        ],
        work,
    )(info, halo, img_own, img_other, cols, table, early)
    near = swap_cores(near)
    remote = swap_layers(remote)

    sums = call(
        functools.partial(inner_kernel, taps=taps),
        "inner",
        pltpu.VMEM((views, half // 2 * rows_y, 2 * depth), f32),
        "svvv",
        [
            pltpu.VMEM((views, inner, tall, depth), f32),
            pltpu.VMEM((views, inner, rows_y, deep), bf16),
        ],
        work,
    )(info, quot, near, table)

    coded = shape((HEADER + rows * width, depth), jnp.int16)
    pieces = call(
        functools.partial(correct_kernel, taps=taps, blocks=blocks),
        "correct",
        (pltpu.VMEM((rows, width, depth), f32),) + (coded,) * (chips - 1),
        "svvvv",
        [
            pltpu.VMEM((views, rim, tall, depth), f32),
            pltpu.VMEM((views, rim, rows_y, deep), bf16),
            pltpu.VMEM((views, rim, wide, depth), f32),
            pltpu.VMEM((half, width, depth), f32),
            pltpu.VMEM((half, width, depth), f32),
        ],
        work // 4,
    )(info, remote, sums, table, est_own)
    arrived = [pieces[0]] + [swap_chips(pieces[step], step) for step in range(1, chips)]
    mine = call(
        combine_kernel,
        "combine",
        coded,
        "v" * chips,
    )(*arrived)
    column = [mine] + [swap_chips(mine, step) for step in range(1, chips)]
    across = [swap_cores(piece) for piece in column]
    return call(
        gather_kernel,
        "gather",
        shape(estimate.shape, f32),
        "s" + "v" * (2 * chips),
        [pltpu.VMEM(estimate.shape, f32), sems((slab_x,))],
        out_kinds="h",
    )(ids, *column, *across)


def solution(mesh):
    in_specs = (P("blk", None, None), P("view", "blk", None, None), P(), P(None, "blk", None))
    out_specs = P("blk", None, None)
    return jax.shard_map(local, mesh=mesh, in_specs=in_specs, out_specs=out_specs, check_vma=False)
```

```python
import functools

import jax
import jax.numpy as jnp
from jax import lax
from jax.experimental import pallas as pl
from jax.experimental.pallas import tpu as pltpu
from jax.sharding import PartitionSpec as P

CAP = 3
LANES = 128
PAD = 8
MARKS = 3
HEADER = 16
MARK = 256.0
LEVEL = 32767.0
SPAN = 16.6
VMEM_LIMIT = 24 * 1024 * 1024


def swap_cores(cells):
    count = lax.axis_size("view")
    return lax.ppermute(cells, "view", [(i, i ^ 1) for i in range(count)])


def swap_chips(cells, step):
    count = lax.axis_size("view")
    return lax.ppermute(cells, "view", [(i, i ^ (2 * step)) for i in range(count)])


def swap_layers(cells):
    views, layers = lax.axis_size("view"), lax.axis_size("blk")
    route = []
    for chip in range(views // 2):
        for layer in range(layers):
            for core in range(2):
                there = layer + (1 if core else -1)
                if 0 <= there < layers:
                    to = (2 * chip + 1 - core) * layers + there
                else:
                    to = (2 * (chip ^ 1) + core) * layers + layer
                route.append(((2 * chip + core) * layers + layer, to))
    return lax.ppermute(cells, ("view", "blk"), route)


def has_far(core):
    layer = lax.axis_index("blk")
    there = layer + 2 * core - 1
    return (there >= 0) & (there < lax.axis_size("blk"))


def code_header(low, high):
    low_mark = jnp.floor(low * MARK)
    span_mark = jnp.floor(high * MARK) + 1.0 - low_mark
    row = lax.broadcasted_iota(jnp.int32, (HEADER, LANES), 0)
    header = jnp.where(row == 0, low_mark, span_mark).astype(jnp.int32).astype(jnp.int16)
    return header, low_mark / MARK, (2 * LEVEL * MARK) / span_mark


def encode(logs, low, scale):
    steps = (logs - low) * scale - (LEVEL - 0.5)
    steps = jnp.clip(jnp.floor(steps), -LEVEL, LEVEL)
    return steps.astype(jnp.int32).astype(jnp.int16)


def code_marks(piece):
    header = piece[:HEADER, :].astype(jnp.int32).astype(jnp.float32)
    step = header[1:2, :] * (1.0 / (2 * LEVEL * MARK))
    return header[0:1, :] * (1.0 / MARK) + step * LEVEL, step


def decode(piece, marks, at, rows):
    middle, step = marks
    cells = piece[at : at + rows, :].astype(jnp.int32).astype(jnp.float32)
    return cells * step + middle


def view_slot(core, j, views):
    return core ^ j if views > 1 else 0


def is_covered(info, j, block):
    return ((info[MARKS + j] >> block) & 1) > 0


def window_of(info, j, blocks, window):
    first = jnp.int32(blocks - window)
    for block in range(blocks - window - 1, -1, -1):
        first = jnp.where(is_covered(info, j, block), jnp.int32(block), first)
    return first


def window_mask(info, j, first, window, block_width):
    row = lax.broadcasted_iota(jnp.int32, (window * block_width, LANES), 0)
    mask = jnp.zeros(row.shape, jnp.int32)
    for block in range(window):
        inside = (row >= block * block_width) & (row < (block + 1) * block_width)
        here = jnp.where(is_covered(info, j, first + block), 1, 0)
        mask = jnp.where(inside, here, mask)
    return mask > 0


def canonical(core, row, last):
    return jnp.where(core == 0, row, last - row)


def payload_kernel(ids, cov, spread, est, edge, cov_here, spread_here, rows, sems):
    core = ids[0]
    rim = edge.shape[0]
    far_rows = est.at[pl.ds((est.shape[0] - rim) * core, rim)]
    copies = [
        pltpu.make_async_copy(far_rows, rows, sems.at[0]),
        pltpu.make_async_copy(spread, spread_here, sems.at[1]),
        pltpu.make_async_copy(cov, cov_here, sems.at[2]),
    ]
    for copy in copies:
        copy.start()
    copies[0].wait()
    edge[...] = rows[...].astype(edge.dtype)
    for copy in copies[1:]:
        copy.wait()


def tables_kernel(
    ids,
    cov,
    spread,
    est,
    images,
    table,
    cols,
    info,
    img_own,
    est_own,
    sums,
    rows,
    pad,
    sems,
    *,
    taps,
    blocks,
):
    taps_x, taps_y, taps_z = taps
    core, chip = ids[0], ids[1]
    rim_z = (taps_z - 1) // 2
    depth = LANES
    views = table.shape[0]
    count, width = cols.shape[0], cols.shape[1]
    margin = jnp.zeros((count, PAD, depth), jnp.float32)
    pad[:, :PAD, :] = margin
    pad[:, PAD + width :, :] = margin
    copies = [
        pltpu.make_async_copy(
            est.at[canonical(core, i, est.shape[0] - 1)], pad.at[i, pl.ds(PAD, width)], sems.at[i]
        )
        for i in range(count)
    ]
    copies.append(pltpu.make_async_copy(images.at[0], img_own, sems.at[count]))
    for copy in copies:
        copy.start()
    row = lax.broadcasted_iota(jnp.int32, (depth, depth), 0)
    col = lax.broadcasted_iota(jnp.int32, (depth, depth), 1)
    band = jnp.abs(row - col) <= rim_z
    at = row - rim_z
    place = ((col == at) | (col == at + depth)) & (row < taps_z)
    place = jnp.where(place, 1.0, 0.0).astype(jnp.bfloat16)
    rows[...] = jnp.zeros(rows.shape, jnp.float32)
    total_views = spread.shape[0] // (taps_x * taps_y)
    info[0] = core
    info[1] = chip
    info[2] = ids[2]
    block = lax.broadcasted_iota(jnp.int32, cov.shape, 0)
    lane = lax.broadcasted_iota(jnp.int32, cov.shape, 1)
    bits = jnp.where(cov[...] != 0, jnp.left_shift(1, block), 0)
    for j in range(views):
        view = chip * views + view_slot(core, j, views)
        code = jnp.sum(jnp.where(lane == view, bits, 0).astype(jnp.float32))
        info[MARKS + j] = code.astype(jnp.int32)
        taps_all = spread[pl.ds(view, taps_x * taps_y, stride=total_views), :]
        rows[j, : taps_x * taps_y, :taps_z] = taps_all
        weights = rows[j]
        kernel = (weights / jnp.sum(weights)).astype(jnp.bfloat16)
        rows[j] = jnp.dot(kernel, place, preferred_element_type=jnp.float32)

    def fill(a, carry):
        at_x = canonical(1 - core, a, taps_x - 1)
        for j in range(views):
            for b in range(taps_y):
                line = rows[j, pl.ds(at_x * taps_y + taps_y - 1 - b, 1), :]
                line = jnp.broadcast_to(line, (depth, depth))
                line = pltpu.roll(line, 0, 1, stride=1, stride_axis=0)
                line = jnp.where(band, line, 0.0).astype(jnp.bfloat16)
                table[j, a, b * depth : (b + 1) * depth, :] = line
        return carry

    lax.fori_loop(0, taps_x, fill, 0, unroll=3)
    for copy in copies:
        copy.wait()
    fill_columns(pad, cols, taps_y, width)
    for r in range(est_own.shape[0]):
        est_own[r] = pad[chip * est_own.shape[0] + r, PAD : PAD + width, :]
    rim = count // 3
    rows_y = sums.shape[1] // rim
    for j in range(views):
        first = window_of(info, j, blocks, rows_y // (width // blocks))
        y_start = pl.multiple_of(first * (width // blocks), width // blocks)
        total = None
        for s in early_steps(j, rim, (taps_x + 1) // 2):
            part = dot_turned(
                lambda x: cols[x - rim, pl.ds(y_start, rows_y), :], range(rim), table, j, s
            )
            total = part if total is None else total + part
        sums[j] = total


def fill_columns(pad, cols, taps_y, rows_y):
    rim_y = (taps_y - 1) // 2
    for x in range(cols.shape[0]):
        for b in range(taps_y):
            low = PAD - rim_y + b
            cols[x, :, b * LANES : (b + 1) * LANES] = pad[x, low : low + rows_y, :].astype(
                jnp.bfloat16
            )


def left_side(slab, pairs, s):
    return jnp.concatenate(
        [jnp.concatenate([slab(2 * (i + s) + u) for u in range(2)], axis=1) for i in pairs], axis=0
    )


def right_side(table, j, s):
    taps_x = table.shape[1]

    def block(at):
        return table[j, at] if 0 <= at < taps_x else jnp.zeros(table.shape[2:], table.dtype)

    return jnp.concatenate(
        [jnp.concatenate([block(2 * s + u), block(2 * s + u - 1)], axis=1) for u in range(2)],
        axis=0,
    )


def right_side_turned(table, j, s):
    taps_x = table.shape[1]
    taps_y = table.shape[2] // LANES
    lines = []
    for w in range(2):
        line = []
        for u in range(2):
            at = taps_x - 1 - (2 * s + u - w)
            for b in range(taps_y - 1, -1, -1):
                if 0 <= at < taps_x:
                    line.append(table[j, at, b * LANES : (b + 1) * LANES, :])
                else:
                    line.append(jnp.zeros((LANES, LANES), table.dtype))
        lines.append(jnp.concatenate(line, axis=1))
    return jnp.concatenate(lines, axis=0)


def dot_turned(slab, pairs, table, j, s):
    return lax.dot_general(
        left_side(slab, pairs, s),
        right_side_turned(table, j, s),
        (((1,), (1,)), ((), ())),
        preferred_element_type=jnp.float32,
    )


def add_rows(total, part, cut):
    if total is None:
        return part
    if not cut:
        return total + part
    return jnp.concatenate([total[:cut], total[cut:] + part], axis=0)


def early_steps(j, rim, steps):
    return range(rim // 2 + j, steps)


def blur_kernel(
    info, halo, img_own, img_other, cols, table, early, quot, remote, near, pad, edge, image, *, taps, blocks
):
    core, chip = info[0], info[1]
    views, half, rows_y, depth = quot.shape
    rim, width, _ = halo.shape
    block_width = width // blocks
    window = rows_y // block_width
    share_w = img_own.shape[1]
    if views == 1:
        own_at = pl.multiple_of(core * share_w, share_w)
        other_at = pl.multiple_of((1 - core) * share_w, share_w)
        for r in range(half):
            image[r, pl.ds(own_at, share_w), :] = img_own[half * core + r]
            image[r, pl.ds(other_at, share_w), :] = img_other[half * core + r]
    margin = jnp.zeros((rim, PAD, depth), jnp.float32)
    pad[:, :PAD, :] = margin
    pad[:, PAD + width :, :] = margin
    for x in range(rim):
        cells = halo[canonical(core, x, rim - 1)].astype(jnp.float32)
        pad[x, PAD : PAD + width, :] = jnp.where(info[2] > 0, cells, 0.0)
    fill_columns(pad, edge, taps[1], width)
    for j in range(views):
        first = window_of(info, j, blocks, window)
        mask = window_mask(info, j, first, window, block_width)
        y_start = pl.multiple_of(first * block_width, block_width)

        def slab(x):
            part = edge.at[x] if x < rim else cols.at[x - rim]
            return part[pl.ds(y_start, rows_y), :]

        total = early[j]
        for s in range(early_steps(j, rim, 0).start):
            total = total + dot_turned(slab, range(half // 2), table, j, s)
        blurred = [total[i * rows_y : (i + 1) * rows_y] for i in range(half // 2)]
        slot = view_slot(core, j, views)
        remote[slot, :HEADER, :] = jnp.full((HEADER, depth), first, jnp.int32).astype(jnp.bfloat16)
        for r in range(half):
            row = canonical(core, r, half - 1)
            if views == 1:
                cells = image[row, pl.ds(y_start, rows_y), :]
            else:
                cells = (img_other if j else img_own)[half * core + row, pl.ds(y_start, rows_y), :]
            i, w = r // 2, r % 2
            below = blurred[i][:, w * depth : (w + 1) * depth]
            ratio = jnp.where(mask, cells.astype(jnp.float32) / below, 0.0).astype(jnp.bfloat16)
            quot[j, r] = ratio
            if r < rim:
                low = HEADER + r * rows_y
                remote[slot, low : low + rows_y, :] = ratio
            else:
                near[slot, r - rim] = ratio


def inner_kernel(info, quot, near, table, sums, pad, cols, *, taps):
    views, half, rows_y, depth = quot.shape
    rim = near.shape[1]
    pairs = half // 2
    steps = (table.shape[1] + 1) // 2
    margin = jnp.zeros((half + rim, PAD, depth), jnp.float32)
    for j in range(views):
        pad[j, :, :PAD, :] = margin
        pad[j, :, PAD + rows_y :, :] = margin
        for r in range(half):
            pad[j, r, PAD : PAD + rows_y, :] = quot[j, r].astype(jnp.float32)
        for r in range(rim):
            pad[j, half + rim - 1 - r, PAD : PAD + rows_y, :] = near[view_slot(info[0], j, views), r].astype(
                jnp.float32
            )
        fill_columns(pad.at[j], cols.at[j], taps[1], rows_y)
        total = None
        for s in range(steps - 1, -1, -1):
            skip = max(0, rim // 2 - s)
            part = jnp.dot(
                left_side(lambda x: cols[j, x - rim], range(skip, pairs), s),
                right_side(table, j, s),
                preferred_element_type=jnp.float32,
            )
            total = add_rows(total, part, skip * rows_y)
        sums[j] = total


def correct_kernel(info, remote, sums, table, est_own, *rest, taps, blocks):
    *pieces, pad, cols, far, product, logs = rest
    chip = info[1]
    views, rim, rows_y, _ = cols.shape
    half, width, depth = product.shape
    block_width = width // blocks
    window = rows_y // block_width
    rows = half // len(pieces)
    product[...] = jnp.ones(product.shape, jnp.float32)
    far[...] = jnp.zeros(far.shape, jnp.float32)
    for j in range(views):
        first = window_of(info, j, blocks, window)
        mask = window_mask(info, j, first, window, block_width)
        y_start = pl.multiple_of(first * block_width, block_width)
        slot = view_slot(info[0], j, views)
        there = jnp.max(remote[slot, :HEADER, :].astype(jnp.float32)).astype(jnp.int32)
        there = jnp.clip(there, 0, blocks - window)
        y_there = pl.multiple_of(there * block_width, block_width)
        for r in range(rim):
            low = HEADER + r * rows_y
            cells = remote[slot, low : low + rows_y, :].astype(jnp.float32)
            cells = jnp.where(info[2] > 0, cells, 0.0)
            far[j, rim - 1 - r, pl.ds(PAD + y_there, rows_y), :] = cells
        for r in range(rim):
            pad[j, r] = far[j, r, pl.ds(y_start, rows_y + 2 * PAD), :]
        fill_columns(pad.at[j], cols.at[j], taps[1], rows_y)
        edges = [None] * (half // 2)
        for s in range(rim // 2):
            pairs = range(rim // 2 - s)
            part = jnp.dot(
                left_side(lambda x: cols[j, x], pairs, s),
                right_side(table, j, s),
                preferred_element_type=jnp.float32,
            )
            for i in pairs:
                cells = part[i * rows_y : (i + 1) * rows_y]
                edges[i] = cells if edges[i] is None else edges[i] + cells
        for r in range(half):
            i, w = r // 2, r % 2
            cells = sums[j, i * rows_y : (i + 1) * rows_y, w * depth : (w + 1) * depth]
            if edges[i] is not None:
                cells = cells + edges[i][:, w * depth : (w + 1) * depth]
            factor = jnp.where(mask, cells, 1.0)
            at = (r, pl.ds(y_start, rows_y), slice(None))
            product[at] = product[at] * factor
    least = jnp.full((width, depth), jnp.inf, jnp.float32)
    most = -least
    for r in range(half):
        cells = jnp.log(product[r])
        logs[r] = cells
        least = jnp.minimum(least, cells)
        most = jnp.maximum(most, cells)
    header, low, scale = code_header(jnp.min(least), jnp.max(most))
    for r in range(rows):
        pieces[0][r] = est_own[r] * product[chip * rows + r]
    for step in range(1, len(pieces)):
        pieces[step][:HEADER, :] = header
        for r in range(rows):
            at = HEADER + r * width
            pieces[step][at : at + width, :] = encode(logs[(chip ^ step) * rows + r], low, scale)


def combine_kernel(own, *rest):
    *pieces, out = rest
    rows, width, _ = own.shape
    marks = [code_marks(piece) for piece in pieces]
    all_logs = []
    for r in range(rows):
        logs = jnp.log(own[r])
        for piece, mark in zip(pieces, marks):
            logs = logs + decode(piece, mark, HEADER + r * width, width)
        all_logs.append(logs)
    low = functools.reduce(jnp.minimum, all_logs)
    high = functools.reduce(jnp.maximum, all_logs)
    high = jnp.max(high)
    header, low, scale = code_header(jnp.maximum(jnp.min(low), high - SPAN), high)
    out[:HEADER, :] = header
    for r, logs in enumerate(all_logs):
        at = HEADER + r * width
        out[at : at + width, :] = encode(logs, low, scale)


def gather_kernel(ids, *rest):
    *pieces, out, cells, sems = rest
    core, chip = ids[0], ids[1]
    count = len(pieces) // 2
    slab_x, width, _ = out.shape
    rows = slab_x // 2 // count
    stores = []
    for place, piece in enumerate(pieces):
        side = core if place < count else 1 - core
        marks = code_marks(piece)
        for r in range(rows):
            at = canonical(side, (chip ^ (place % count)) * rows + r, slab_x - 1)
            slot = place * rows + r
            cells[slot] = jnp.exp(decode(piece, marks, HEADER + r * width, width))
            store = pltpu.make_async_copy(cells.at[slot], out.at[at], sems.at[slot])
            store.start()
            stores.append(store)
    for store in stores:
        store.wait()


def call(kernel, name, outs, kinds, scratch=(), flops=0, out_kinds=None):
    spaces = {"s": pltpu.SMEM, "v": pltpu.VMEM, "h": pltpu.HBM}
    many = isinstance(outs, tuple)
    out_kinds = out_kinds or "v" * (len(outs) if many else 1)
    out_specs = tuple(pl.BlockSpec(memory_space=spaces[kind]) for kind in out_kinds)
    return pl.pallas_call(
        kernel,
        name=name,
        out_shape=outs,
        in_specs=[pl.BlockSpec(memory_space=spaces[kind]) for kind in kinds],
        out_specs=out_specs if many else out_specs[0],
        scratch_shapes=list(scratch),
        compiler_params=pltpu.CompilerParams(vmem_limit_bytes=VMEM_LIMIT),
        cost_estimate=pl.CostEstimate(flops=flops, bytes_accessed=1 << 16, transcendentals=0),
    )


def local(estimate, images, point_spread, covered):
    slab_x, width, depth = estimate.shape
    share_w = images.shape[2]
    _, taps_x, taps_y, taps_z = point_spread.shape
    taps = (taps_x, taps_y, taps_z)
    rim = (taps_x - 1) // 2
    half = slab_x // 2
    blocks = covered.shape[2]
    window = min(CAP, blocks)
    rows_y = window * (width // blocks)
    shares = width // share_w
    views = 2 // shares
    assert shares * views == 2 and half == 2 * rim and depth == LANES
    group = lax.axis_index("view")
    chips = lax.axis_size("view") // 2
    core, chip = group % 2, group // 2
    ids = jnp.stack([core, chip, has_far(core)]).astype(jnp.int32)
    inner = half + rim
    rows = half // chips
    f32, bf16 = jnp.float32, jnp.bfloat16
    shape = jax.ShapeDtypeStruct
    deep = taps_y * depth
    wide = width + 2 * PAD
    tall = rows_y + 2 * PAD
    sems = pltpu.SemaphoreType.DMA
    work = 2 * half * rows_y * depth * taps_x * taps_y * depth * views

    img_other = swap_cores(images[0])
    estimate = pltpu.with_memory_space_constraint(estimate, pltpu.HBM)
    images = pltpu.with_memory_space_constraint(images, pltpu.HBM)
    spread = jnp.transpose(point_spread, (1, 2, 0, 3)).reshape(-1, taps_z)
    spread = pltpu.with_memory_space_constraint(spread, pltpu.HBM)
    cov = pltpu.with_memory_space_constraint(jnp.transpose(covered[:, 0, :]), pltpu.HBM)

    edge, cov, spread = call(
        payload_kernel,
        "payload",
        (
            shape((rim, width, depth), bf16),
            pltpu.VMEM(cov.shape, jnp.int32),
            pltpu.VMEM(spread.shape, f32),
        ),
        "shhh",
        [pltpu.VMEM((rim, width, depth), f32), sems((3,))],
    )(ids, cov, spread, estimate)
    halo = swap_layers(edge)

    table, cols, info, img_own, est_own, early = call(
        functools.partial(tables_kernel, taps=taps, blocks=blocks),
        "tables",
        (
            pltpu.VMEM((views, taps_x, deep, depth), bf16),
            pltpu.VMEM((inner, width, deep), bf16),
            shape((MARKS + views,), jnp.int32),
            pltpu.VMEM((slab_x, share_w, depth), bf16),
            pltpu.VMEM((rows, width, depth), f32),
            pltpu.VMEM((views, half // 2 * rows_y, 2 * depth), f32),
        ),
        "svvhh",
        [
            pltpu.VMEM((views, -(-taps_x * taps_y // 8) * 8, depth), f32),
            pltpu.VMEM((inner, wide, depth), f32),
            sems((inner + 1,)),
        ],
        work // 2,
        "vvsvvv",
    )(ids, cov, spread, estimate, images)

    quot, remote, near = call(
        functools.partial(blur_kernel, taps=taps, blocks=blocks),
        "blur",
        (
            pltpu.VMEM((views, half, rows_y, depth), bf16),
            shape((views, HEADER + rim * rows_y, depth), bf16),
            shape((views, rim, rows_y, depth), bf16),
        ),
        "svvvvvv",
        [
            pltpu.VMEM((rim, wide, depth), f32),
            pltpu.VMEM((rim, width, deep), bf16),
            pltpu.VMEM((half, width, depth) if views == 1 else (8, depth), bf16),
        ],
        work,
    )(info, halo, img_own, img_other, cols, table, early)
    near = swap_cores(near)
    remote = swap_layers(remote)

    sums = call(
        functools.partial(inner_kernel, taps=taps),
        "inner",
        pltpu.VMEM((views, half // 2 * rows_y, 2 * depth), f32),
        "svvv",
        [
            pltpu.VMEM((views, inner, tall, depth), f32),
            pltpu.VMEM((views, inner, rows_y, deep), bf16),
        ],
        work,
    )(info, quot, near, table)

    coded = shape((HEADER + rows * width, depth), jnp.int16)
    pieces = call(
        functools.partial(correct_kernel, taps=taps, blocks=blocks),
        "correct",
        (pltpu.VMEM((rows, width, depth), f32),) + (coded,) * (chips - 1),
        "svvvv",
        [
            pltpu.VMEM((views, rim, tall, depth), f32),
            pltpu.VMEM((views, rim, rows_y, deep), bf16),
            pltpu.VMEM((views, rim, wide, depth), f32),
            pltpu.VMEM((half, width, depth), f32),
            pltpu.VMEM((half, width, depth), f32),
        ],
        work // 4,
    )(info, remote, sums, table, est_own)
    arrived = [pieces[0]] + [swap_chips(pieces[step], step) for step in range(1, chips)]
    mine = call(
        combine_kernel,
        "combine",
        coded,
        "v" * chips,
    )(*arrived)
    column = [mine] + [swap_chips(mine, step) for step in range(1, chips)]
    across = [swap_cores(piece) for piece in column]
    return call(
        gather_kernel,
        "gather",
        shape(estimate.shape, f32),
        "s" + "v" * (2 * chips),
        [pltpu.VMEM(estimate.shape, f32), sems((slab_x,))],
        out_kinds="h",
    )(ids, *column, *across)


def solution(mesh):
    in_specs = (P("blk", None, None), P("view", "blk", None, None), P(), P(None, "blk", None))
    out_specs = P("blk", None, None)
    return jax.shard_map(local, mesh=mesh, in_specs=in_specs, out_specs=out_specs, check_vma=False)
```

```python
import functools

import jax
import jax.numpy as jnp
from jax import lax
from jax.experimental import pallas as pl
from jax.experimental.pallas import tpu as pltpu
from jax.sharding import PartitionSpec as P

CAP = 3
LANES = 128
PAD = 8
MARKS = 3
HEADER = 16
MARK = 256.0
LEVEL = 32767.0
SPAN = 16.6
VMEM_LIMIT = 24 * 1024 * 1024


def swap_cores(cells):
    count = lax.axis_size("view")
    return lax.ppermute(cells, "view", [(i, i ^ 1) for i in range(count)])


def swap_chips(cells, step):
    count = lax.axis_size("view")
    return lax.ppermute(cells, "view", [(i, i ^ (2 * step)) for i in range(count)])


def swap_layers(cells):
    views, layers = lax.axis_size("view"), lax.axis_size("blk")
    route = []
    for chip in range(views // 2):
        for layer in range(layers):
            for core in range(2):
                there = layer + (1 if core else -1)
                if 0 <= there < layers:
                    to = (2 * chip + 1 - core) * layers + there
                else:
                    to = (2 * (chip ^ 1) + core) * layers + layer
                route.append(((2 * chip + core) * layers + layer, to))
    return lax.ppermute(cells, ("view", "blk"), route)


def has_far(core):
    layer = lax.axis_index("blk")
    there = layer + 2 * core - 1
    return (there >= 0) & (there < lax.axis_size("blk"))


def code_header(low, high):
    low_mark = jnp.floor(low * MARK)
    span_mark = jnp.floor(high * MARK) + 1.0 - low_mark
    row = lax.broadcasted_iota(jnp.int32, (HEADER, LANES), 0)
    header = jnp.where(row == 0, low_mark, span_mark).astype(jnp.int32).astype(jnp.int16)
    return header, low_mark / MARK, (2 * LEVEL * MARK) / span_mark


def encode(logs, low, scale):
    steps = (logs - low) * scale - (LEVEL - 0.5)
    steps = jnp.clip(jnp.floor(steps), -LEVEL, LEVEL)
    return steps.astype(jnp.int32).astype(jnp.int16)


def code_marks(piece):
    header = piece[:HEADER, :].astype(jnp.int32).astype(jnp.float32)
    step = header[1:2, :] * (1.0 / (2 * LEVEL * MARK))
    return header[0:1, :] * (1.0 / MARK) + step * LEVEL, step


def decode(piece, marks, at, rows):
    middle, step = marks
    cells = piece[at : at + rows, :].astype(jnp.int32).astype(jnp.float32)
    return cells * step + middle


def view_slot(core, j, views):
    return core ^ j if views > 1 else 0


def is_covered(info, j, block):
    return ((info[MARKS + j] >> block) & 1) > 0


def window_of(info, j, blocks, window):
    first = jnp.int32(blocks - window)
    for block in range(blocks - window - 1, -1, -1):
        first = jnp.where(is_covered(info, j, block), jnp.int32(block), first)
    return first


def window_mask(info, j, first, window, block_width):
    row = lax.broadcasted_iota(jnp.int32, (window * block_width, LANES), 0)
    mask = jnp.zeros(row.shape, jnp.int32)
    for block in range(window):
        inside = (row >= block * block_width) & (row < (block + 1) * block_width)
        here = jnp.where(is_covered(info, j, first + block), 1, 0)
        mask = jnp.where(inside, here, mask)
    return mask > 0


def canonical(core, row, last):
    return jnp.where(core == 0, row, last - row)


def payload_kernel(ids, cov, spread, est, edge, cov_here, spread_here, rows, sems):
    core = ids[0]
    rim = edge.shape[0]
    far_rows = est.at[pl.ds((est.shape[0] - rim) * core, rim)]
    copies = [
        pltpu.make_async_copy(far_rows, rows, sems.at[0]),
        pltpu.make_async_copy(spread, spread_here, sems.at[1]),
        pltpu.make_async_copy(cov, cov_here, sems.at[2]),
    ]
    for copy in copies:
        copy.start()
    copies[0].wait()
    edge[...] = rows[...].astype(edge.dtype)
    for copy in copies[1:]:
        copy.wait()


def tables_kernel(
    ids,
    cov,
    spread,
    est,
    images,
    table,
    cols,
    info,
    img_own,
    est_own,
    sums,
    rows,
    pad,
    sems,
    *,
    taps,
    blocks,
):
    taps_x, taps_y, taps_z = taps
    core, chip = ids[0], ids[1]
    rim_z = (taps_z - 1) // 2
    depth = LANES
    views = table.shape[0]
    count, width = cols.shape[0], cols.shape[1]
    margin = jnp.zeros((count, PAD, depth), jnp.float32)
    pad[:, :PAD, :] = margin
    pad[:, PAD + width :, :] = margin
    copies = [
        pltpu.make_async_copy(
            est.at[canonical(core, i, est.shape[0] - 1)], pad.at[i, pl.ds(PAD, width)], sems.at[i]
        )
        for i in range(count)
    ]
    copies.append(pltpu.make_async_copy(images.at[0], img_own, sems.at[count]))
    for copy in copies:
        copy.start()
    row = lax.broadcasted_iota(jnp.int32, (depth, depth), 0)
    col = lax.broadcasted_iota(jnp.int32, (depth, depth), 1)
    band = jnp.abs(row - col) <= rim_z
    at = row - rim_z
    place = ((col == at) | (col == at + depth)) & (row < taps_z)
    place = jnp.where(place, 1.0, 0.0).astype(jnp.bfloat16)
    rows[...] = jnp.zeros(rows.shape, jnp.float32)
    total_views = spread.shape[0] // (taps_x * taps_y)
    info[0] = core
    info[1] = chip
    info[2] = ids[2]
    block = lax.broadcasted_iota(jnp.int32, cov.shape, 0)
    lane = lax.broadcasted_iota(jnp.int32, cov.shape, 1)
    bits = jnp.where(cov[...] != 0, jnp.left_shift(1, block), 0)
    for j in range(views):
        view = chip * views + view_slot(core, j, views)
        code = jnp.sum(jnp.where(lane == view, bits, 0).astype(jnp.float32))
        info[MARKS + j] = code.astype(jnp.int32)
        taps_all = spread[pl.ds(view, taps_x * taps_y, stride=total_views), :]
        rows[j, : taps_x * taps_y, :taps_z] = taps_all
        weights = rows[j]
        kernel = (weights / jnp.sum(weights)).astype(jnp.bfloat16)
        rows[j] = jnp.dot(kernel, place, preferred_element_type=jnp.float32)

    def fill(a, carry):
        at_x = canonical(1 - core, a, taps_x - 1)
        for j in range(views):
            for b in range(taps_y):
                line = rows[j, pl.ds(at_x * taps_y + taps_y - 1 - b, 1), :]
                line = jnp.broadcast_to(line, (depth, depth))
                line = pltpu.roll(line, 0, 1, stride=1, stride_axis=0)
                line = jnp.where(band, line, 0.0).astype(jnp.bfloat16)
                table[j, a, b * depth : (b + 1) * depth, :] = line
        return carry

    lax.fori_loop(0, taps_x, fill, 0, unroll=3)
    for copy in copies:
        copy.wait()
    fill_columns(pad, cols, taps_y, width)
    for r in range(est_own.shape[0]):
        est_own[r] = pad[chip * est_own.shape[0] + r, PAD : PAD + width, :]
    rim = count // 3
    rows_y = sums.shape[1] // rim
    for j in range(views):
        first = window_of(info, j, blocks, rows_y // (width // blocks))
        y_start = pl.multiple_of(first * (width // blocks), width // blocks)
        total = None
        for s in early_steps(rim, (taps_x + 1) // 2):
            part = dot_turned(
                lambda x: cols[x - rim, pl.ds(y_start, rows_y), :], range(rim), table, j, s
            )
            total = part if total is None else total + part
        sums[j] = total


def fill_columns(pad, cols, taps_y, rows_y):
    rim_y = (taps_y - 1) // 2
    for x in range(cols.shape[0]):
        for b in range(taps_y):
            low = PAD - rim_y + b
            cols[x, :, b * LANES : (b + 1) * LANES] = pad[x, low : low + rows_y, :].astype(
                jnp.bfloat16
            )


def left_side(slab, pairs, s):
    return jnp.concatenate(
        [jnp.concatenate([slab(2 * (i + s) + u) for u in range(2)], axis=1) for i in pairs], axis=0
    )


def right_side(table, j, s):
    taps_x = table.shape[1]

    def block(at):
        return table[j, at] if 0 <= at < taps_x else jnp.zeros(table.shape[2:], table.dtype)

    return jnp.concatenate(
        [jnp.concatenate([block(2 * s + u), block(2 * s + u - 1)], axis=1) for u in range(2)],
        axis=0,
    )


def right_side_turned(table, j, s):
    taps_x = table.shape[1]
    taps_y = table.shape[2] // LANES
    lines = []
    for w in range(2):
        line = []
        for u in range(2):
            at = taps_x - 1 - (2 * s + u - w)
            for b in range(taps_y - 1, -1, -1):
                if 0 <= at < taps_x:
                    line.append(table[j, at, b * LANES : (b + 1) * LANES, :])
                else:
                    line.append(jnp.zeros((LANES, LANES), table.dtype))
        lines.append(jnp.concatenate(line, axis=1))
    return jnp.concatenate(lines, axis=0)


def dot_turned(slab, pairs, table, j, s):
    return lax.dot_general(
        left_side(slab, pairs, s),
        right_side_turned(table, j, s),
        (((1,), (1,)), ((), ())),
        preferred_element_type=jnp.float32,
    )


def add_rows(total, part, cut):
    if total is None:
        return part
    if not cut:
        return total + part
    return jnp.concatenate([total[:cut], total[cut:] + part], axis=0)


def early_steps(rim, steps):
    return range(rim // 2, steps)


def blur_kernel(
    info, halo, img_own, img_other, cols, table, early, quot, remote, near, pad, edge, image, *, taps, blocks
):
    core, chip = info[0], info[1]
    views, half, rows_y, depth = quot.shape
    rim, width, _ = halo.shape
    block_width = width // blocks
    window = rows_y // block_width
    share_w = img_own.shape[1]
    if views == 1:
        own_at = pl.multiple_of(core * share_w, share_w)
        other_at = pl.multiple_of((1 - core) * share_w, share_w)
        for r in range(half):
            image[r, pl.ds(own_at, share_w), :] = img_own[half * core + r]
            image[r, pl.ds(other_at, share_w), :] = img_other[half * core + r]
    margin = jnp.zeros((rim, PAD, depth), jnp.float32)
    pad[:, :PAD, :] = margin
    pad[:, PAD + width :, :] = margin
    for x in range(rim):
        cells = halo[canonical(core, x, rim - 1)].astype(jnp.float32)
        pad[x, PAD : PAD + width, :] = jnp.where(info[2] > 0, cells, 0.0)
    fill_columns(pad, edge, taps[1], width)
    for j in range(views):
        first = window_of(info, j, blocks, window)
        mask = window_mask(info, j, first, window, block_width)
        y_start = pl.multiple_of(first * block_width, block_width)

        def slab(x):
            part = edge.at[x] if x < rim else cols.at[x - rim]
            return part[pl.ds(y_start, rows_y), :]

        total = early[j]
        for s in range(early_steps(rim, 0).start):
            total = total + dot_turned(slab, range(half // 2), table, j, s)
        blurred = [total[i * rows_y : (i + 1) * rows_y] for i in range(half // 2)]
        slot = view_slot(core, j, views)
        remote[slot, :HEADER, :] = jnp.full((HEADER, depth), first, jnp.int32).astype(jnp.bfloat16)
        for r in range(half):
            row = canonical(core, r, half - 1)
            if views == 1:
                cells = image[row, pl.ds(y_start, rows_y), :]
            else:
                cells = (img_other if j else img_own)[half * core + row, pl.ds(y_start, rows_y), :]
            i, w = r // 2, r % 2
            below = blurred[i][:, w * depth : (w + 1) * depth]
            ratio = jnp.where(mask, cells.astype(jnp.float32) / below, 0.0).astype(jnp.bfloat16)
            quot[j, r] = ratio
            if r < rim:
                low = HEADER + r * rows_y
                remote[slot, low : low + rows_y, :] = ratio
            else:
                near[slot, r - rim] = ratio


def inner_kernel(info, quot, near, table, sums, pad, cols, *, taps):
    views, half, rows_y, depth = quot.shape
    rim = near.shape[1]
    pairs = half // 2
    steps = (table.shape[1] + 1) // 2
    margin = jnp.zeros((half + rim, PAD, depth), jnp.float32)
    for j in range(views):
        pad[j, :, :PAD, :] = margin
        pad[j, :, PAD + rows_y :, :] = margin
        for r in range(half):
            pad[j, r, PAD : PAD + rows_y, :] = quot[j, r].astype(jnp.float32)
        for r in range(rim):
            pad[j, half + rim - 1 - r, PAD : PAD + rows_y, :] = near[view_slot(info[0], j, views), r].astype(
                jnp.float32
            )
        fill_columns(pad.at[j], cols.at[j], taps[1], rows_y)
        total = None
        for s in range(steps - 1, -1, -1):
            skip = max(0, rim // 2 - s)
            part = jnp.dot(
                left_side(lambda x: cols[j, x - rim], range(skip, pairs), s),
                right_side(table, j, s),
                preferred_element_type=jnp.float32,
            )
            total = add_rows(total, part, skip * rows_y)
        sums[j] = total


def correct_kernel(info, remote, sums, table, est_own, *rest, taps, blocks):
    *pieces, pad, cols, far, product, logs = rest
    chip = info[1]
    views, rim, rows_y, _ = cols.shape
    half, width, depth = product.shape
    block_width = width // blocks
    window = rows_y // block_width
    rows = half // len(pieces)
    product[...] = jnp.ones(product.shape, jnp.float32)
    far[...] = jnp.zeros(far.shape, jnp.float32)
    for j in range(views):
        first = window_of(info, j, blocks, window)
        mask = window_mask(info, j, first, window, block_width)
        y_start = pl.multiple_of(first * block_width, block_width)
        slot = view_slot(info[0], j, views)
        there = jnp.max(remote[slot, :HEADER, :].astype(jnp.float32)).astype(jnp.int32)
        there = jnp.clip(there, 0, blocks - window)
        y_there = pl.multiple_of(there * block_width, block_width)
        for r in range(rim):
            low = HEADER + r * rows_y
            cells = remote[slot, low : low + rows_y, :].astype(jnp.float32)
            cells = jnp.where(info[2] > 0, cells, 0.0)
            far[j, rim - 1 - r, pl.ds(PAD + y_there, rows_y), :] = cells
        for r in range(rim):
            pad[j, r] = far[j, r, pl.ds(y_start, rows_y + 2 * PAD), :]
        fill_columns(pad.at[j], cols.at[j], taps[1], rows_y)
        edges = [None] * (half // 2)
        for s in range(rim // 2):
            pairs = range(rim // 2 - s)
            part = jnp.dot(
                left_side(lambda x: cols[j, x], pairs, s),
                right_side(table, j, s),
                preferred_element_type=jnp.float32,
            )
            for i in pairs:
                cells = part[i * rows_y : (i + 1) * rows_y]
                edges[i] = cells if edges[i] is None else edges[i] + cells
        for r in range(half):
            i, w = r // 2, r % 2
            cells = sums[j, i * rows_y : (i + 1) * rows_y, w * depth : (w + 1) * depth]
            if edges[i] is not None:
                cells = cells + edges[i][:, w * depth : (w + 1) * depth]
            factor = jnp.where(mask, cells, 1.0)
            at = (r, pl.ds(y_start, rows_y), slice(None))
            product[at] = product[at] * factor
    least = jnp.full((width, depth), jnp.inf, jnp.float32)
    most = -least
    for r in range(half):
        cells = jnp.log(product[r])
        logs[r] = cells
        least = jnp.minimum(least, cells)
        most = jnp.maximum(most, cells)
    header, low, scale = code_header(jnp.min(least), jnp.max(most))
    for r in range(rows):
        pieces[0][r] = est_own[r] * product[chip * rows + r]
    for step in range(1, len(pieces)):
        pieces[step][:HEADER, :] = header
        for r in range(rows):
            at = HEADER + r * width
            pieces[step][at : at + width, :] = encode(logs[(chip ^ step) * rows + r], low, scale)


def combine_kernel(own, *rest):
    *pieces, out = rest
    rows, width, _ = own.shape
    marks = [code_marks(piece) for piece in pieces]
    all_logs = []
    for r in range(rows):
        logs = jnp.log(own[r])
        for piece, mark in zip(pieces, marks):
            logs = logs + decode(piece, mark, HEADER + r * width, width)
        all_logs.append(logs)
    low = functools.reduce(jnp.minimum, all_logs)
    high = functools.reduce(jnp.maximum, all_logs)
    high = jnp.max(high)
    header, low, scale = code_header(jnp.maximum(jnp.min(low), high - SPAN), high)
    out[:HEADER, :] = header
    for r, logs in enumerate(all_logs):
        at = HEADER + r * width
        out[at : at + width, :] = encode(logs, low, scale)


def gather_kernel(ids, *rest):
    *pieces, out, cells, sems = rest
    core, chip = ids[0], ids[1]
    count = len(pieces) // 2
    slab_x, width, _ = out.shape
    rows = slab_x // 2 // count
    stores = []
    for place, piece in enumerate(pieces):
        side = core if place < count else 1 - core
        marks = code_marks(piece)
        for r in range(rows):
            at = canonical(side, (chip ^ (place % count)) * rows + r, slab_x - 1)
            slot = place * rows + r
            cells[slot] = jnp.exp(decode(piece, marks, HEADER + r * width, width))
            store = pltpu.make_async_copy(cells.at[slot], out.at[at], sems.at[slot])
            store.start()
            stores.append(store)
    for store in stores:
        store.wait()


def call(kernel, name, outs, kinds, scratch=(), flops=0, out_kinds=None):
    spaces = {"s": pltpu.SMEM, "v": pltpu.VMEM, "h": pltpu.HBM}
    many = isinstance(outs, tuple)
    out_kinds = out_kinds or "v" * (len(outs) if many else 1)
    out_specs = tuple(pl.BlockSpec(memory_space=spaces[kind]) for kind in out_kinds)
    return pl.pallas_call(
        kernel,
        name=name,
        out_shape=outs,
        in_specs=[pl.BlockSpec(memory_space=spaces[kind]) for kind in kinds],
        out_specs=out_specs if many else out_specs[0],
        scratch_shapes=list(scratch),
        compiler_params=pltpu.CompilerParams(vmem_limit_bytes=VMEM_LIMIT),
        cost_estimate=pl.CostEstimate(flops=flops, bytes_accessed=1 << 16, transcendentals=0),
    )


def local(estimate, images, point_spread, covered):
    slab_x, width, depth = estimate.shape
    share_w = images.shape[2]
    _, taps_x, taps_y, taps_z = point_spread.shape
    taps = (taps_x, taps_y, taps_z)
    rim = (taps_x - 1) // 2
    half = slab_x // 2
    blocks = covered.shape[2]
    window = min(CAP, blocks)
    rows_y = window * (width // blocks)
    shares = width // share_w
    views = 2 // shares
    assert shares * views == 2 and half == 2 * rim and depth == LANES
    group = lax.axis_index("view")
    chips = lax.axis_size("view") // 2
    core, chip = group % 2, group // 2
    ids = jnp.stack([core, chip, has_far(core)]).astype(jnp.int32)
    inner = half + rim
    rows = half // chips
    f32, bf16 = jnp.float32, jnp.bfloat16
    shape = jax.ShapeDtypeStruct
    deep = taps_y * depth
    wide = width + 2 * PAD
    tall = rows_y + 2 * PAD
    sems = pltpu.SemaphoreType.DMA
    work = 2 * half * rows_y * depth * taps_x * taps_y * depth * views

    img_other = swap_cores(images[0])
    estimate = pltpu.with_memory_space_constraint(estimate, pltpu.HBM)
    images = pltpu.with_memory_space_constraint(images, pltpu.HBM)
    spread = jnp.transpose(point_spread, (1, 2, 0, 3)).reshape(-1, taps_z)
    spread = pltpu.with_memory_space_constraint(spread, pltpu.HBM)
    cov = pltpu.with_memory_space_constraint(jnp.transpose(covered[:, 0, :]), pltpu.HBM)

    edge, cov, spread = call(
        payload_kernel,
        "payload",
        (
            shape((rim, width, depth), bf16),
            pltpu.VMEM(cov.shape, jnp.int32),
            pltpu.VMEM(spread.shape, f32),
        ),
        "shhh",
        [pltpu.VMEM((rim, width, depth), f32), sems((3,))],
    )(ids, cov, spread, estimate)
    halo = swap_layers(edge)

    table, cols, info, img_own, est_own, early = call(
        functools.partial(tables_kernel, taps=taps, blocks=blocks),
        "tables",
        (
            pltpu.VMEM((views, taps_x, deep, depth), bf16),
            pltpu.VMEM((inner, width, deep), bf16),
            shape((MARKS + views,), jnp.int32),
            pltpu.VMEM((slab_x, share_w, depth), bf16),
            pltpu.VMEM((rows, width, depth), f32),
            pltpu.VMEM((views, half // 2 * rows_y, 2 * depth), f32),
        ),
        "svvhh",
        [
            pltpu.VMEM((views, -(-taps_x * taps_y // 8) * 8, depth), f32),
            pltpu.VMEM((inner, wide, depth), f32),
            sems((inner + 1,)),
        ],
        work // 2,
        "vvsvvv",
    )(ids, cov, spread, estimate, images)

    quot, remote, near = call(
        functools.partial(blur_kernel, taps=taps, blocks=blocks),
        "blur",
        (
            pltpu.VMEM((views, half, rows_y, depth), bf16),
            shape((views, HEADER + rim * rows_y, depth), bf16),
            shape((views, rim, rows_y, depth), bf16),
        ),
        "svvvvvv",
        [
            pltpu.VMEM((rim, wide, depth), f32),
            pltpu.VMEM((rim, width, deep), bf16),
            pltpu.VMEM((half, width, depth) if views == 1 else (8, depth), bf16),
        ],
        work,
    )(info, halo, img_own, img_other, cols, table, early)
    near = swap_cores(near)
    remote = swap_layers(remote)

    sums = call(
        functools.partial(inner_kernel, taps=taps),
        "inner",
        pltpu.VMEM((views, half // 2 * rows_y, 2 * depth), f32),
        "svvv",
        [
            pltpu.VMEM((views, inner, tall, depth), f32),
            pltpu.VMEM((views, inner, rows_y, deep), bf16),
        ],
        work,
    )(info, quot, near, table)

    coded = shape((HEADER + rows * width, depth), jnp.int16)
    pieces = call(
        functools.partial(correct_kernel, taps=taps, blocks=blocks),
        "correct",
        (pltpu.VMEM((rows, width, depth), f32),) + (coded,) * (chips - 1),
        "svvvv",
        [
            pltpu.VMEM((views, rim, tall, depth), f32),
            pltpu.VMEM((views, rim, rows_y, deep), bf16),
            pltpu.VMEM((views, rim, wide, depth), f32),
            pltpu.VMEM((half, width, depth), f32),
            pltpu.VMEM((half, width, depth), f32),
        ],
        work // 4,
    )(info, remote, sums, table, est_own)
    steps = range(chips - 1, 0, -1)
    arrived = [pieces[0]] + [swap_chips(pieces[step], step) for step in steps]
    mine = call(
        combine_kernel,
        "combine",
        coded,
        "v" * chips,
    )(*arrived)
    column = [mine] + [swap_chips(mine, step) for step in range(1, chips)]
    across = [swap_cores(piece) for piece in column]
    return call(
        gather_kernel,
        "gather",
        shape(estimate.shape, f32),
        "s" + "v" * (2 * chips),
        [pltpu.VMEM(estimate.shape, f32), sems((slab_x,))],
        out_kinds="h",
    )(ids, *column, *across)


def solution(mesh):
    in_specs = (P("blk", None, None), P("view", "blk", None, None), P(), P(None, "blk", None))
    out_specs = P("blk", None, None)
    return jax.shard_map(local, mesh=mesh, in_specs=in_specs, out_specs=out_specs, check_vma=False)
```

```python
import functools

import jax
import jax.numpy as jnp
from jax import lax
from jax.experimental import pallas as pl
from jax.experimental.pallas import tpu as pltpu
from jax.sharding import PartitionSpec as P

CAP = 3
LANES = 128
PAD = 8
MARKS = 3
HEADER = 16
MARK = 256.0
LEVEL = 32767.0
SPAN = 16.6
VMEM_LIMIT = 24 * 1024 * 1024


def swap_cores(cells):
    count = lax.axis_size("view")
    return lax.ppermute(cells, "view", [(i, i ^ 1) for i in range(count)])


def swap_chips(cells, step):
    count = lax.axis_size("view")
    return lax.ppermute(cells, "view", [(i, i ^ (2 * step)) for i in range(count)])


def swap_layers(cells):
    views, layers = lax.axis_size("view"), lax.axis_size("blk")
    route = []
    for chip in range(views // 2):
        for layer in range(layers):
            for core in range(2):
                there = layer + (1 if core else -1)
                if 0 <= there < layers:
                    to = (2 * chip + 1 - core) * layers + there
                else:
                    to = (2 * (chip ^ 1) + core) * layers + layer
                route.append(((2 * chip + core) * layers + layer, to))
    return lax.ppermute(cells, ("view", "blk"), route)


def has_far(core):
    layer = lax.axis_index("blk")
    there = layer + 2 * core - 1
    return (there >= 0) & (there < lax.axis_size("blk"))


def code_header(low, high):
    low_mark = jnp.floor(low * MARK)
    span_mark = jnp.floor(high * MARK) + 1.0 - low_mark
    row = lax.broadcasted_iota(jnp.int32, (HEADER, LANES), 0)
    header = jnp.where(row == 0, low_mark, span_mark).astype(jnp.int32).astype(jnp.int16)
    return header, low_mark / MARK, (2 * LEVEL * MARK) / span_mark


def encode(logs, low, scale):
    steps = (logs - low) * scale - (LEVEL - 0.5)
    steps = jnp.clip(jnp.floor(steps), -LEVEL, LEVEL)
    return steps.astype(jnp.int32).astype(jnp.int16)


def code_marks(piece):
    header = piece[:HEADER, :].astype(jnp.int32).astype(jnp.float32)
    step = header[1:2, :] * (1.0 / (2 * LEVEL * MARK))
    return header[0:1, :] * (1.0 / MARK) + step * LEVEL, step


def decode(piece, marks, at, rows):
    middle, step = marks
    cells = piece[at : at + rows, :].astype(jnp.int32).astype(jnp.float32)
    return cells * step + middle


def view_slot(core, j, views):
    return core ^ j if views > 1 else 0


def is_covered(info, j, block):
    return ((info[MARKS + j] >> block) & 1) > 0


def window_of(info, j, blocks, window):
    first = jnp.int32(blocks - window)
    for block in range(blocks - window - 1, -1, -1):
        first = jnp.where(is_covered(info, j, block), jnp.int32(block), first)
    return first


def window_mask(info, j, first, window, block_width):
    row = lax.broadcasted_iota(jnp.int32, (window * block_width, LANES), 0)
    mask = jnp.zeros(row.shape, jnp.int32)
    for block in range(window):
        inside = (row >= block * block_width) & (row < (block + 1) * block_width)
        here = jnp.where(is_covered(info, j, first + block), 1, 0)
        mask = jnp.where(inside, here, mask)
    return mask > 0


def canonical(core, row, last):
    return jnp.where(core == 0, row, last - row)


def payload_kernel(ids, cov, spread, est, edge, cov_here, spread_here, rows, sems):
    core = ids[0]
    rim = edge.shape[0]
    far_rows = est.at[pl.ds((est.shape[0] - rim) * core, rim)]
    copies = [
        pltpu.make_async_copy(far_rows, rows, sems.at[0]),
        pltpu.make_async_copy(spread, spread_here, sems.at[1]),
        pltpu.make_async_copy(cov, cov_here, sems.at[2]),
    ]
    for copy in copies:
        copy.start()
    copies[0].wait()
    edge[...] = rows[...].astype(edge.dtype)
    for copy in copies[1:]:
        copy.wait()


def tables_kernel(
    ids,
    cov,
    spread,
    est,
    images,
    table,
    cols,
    info,
    img_own,
    est_own,
    sums,
    rows,
    pad,
    sems,
    *,
    taps,
    blocks,
):
    taps_x, taps_y, taps_z = taps
    core, chip = ids[0], ids[1]
    rim_z = (taps_z - 1) // 2
    depth = LANES
    views = table.shape[0]
    count, width = cols.shape[0], cols.shape[1]
    margin = jnp.zeros((count, PAD, depth), jnp.float32)
    pad[:, :PAD, :] = margin
    pad[:, PAD + width :, :] = margin
    copies = [
        pltpu.make_async_copy(
            est.at[canonical(core, i, est.shape[0] - 1)], pad.at[i, pl.ds(PAD, width)], sems.at[i]
        )
        for i in range(count)
    ]
    copies.append(pltpu.make_async_copy(images.at[0], img_own, sems.at[count]))
    for copy in copies:
        copy.start()
    row = lax.broadcasted_iota(jnp.int32, (depth, depth), 0)
    col = lax.broadcasted_iota(jnp.int32, (depth, depth), 1)
    band = jnp.abs(row - col) <= rim_z
    at = row - rim_z
    place = ((col == at) | (col == at + depth)) & (row < taps_z)
    place = jnp.where(place, 1.0, 0.0).astype(jnp.bfloat16)
    rows[...] = jnp.zeros(rows.shape, jnp.float32)
    total_views = spread.shape[0] // (taps_x * taps_y)
    info[0] = core
    info[1] = chip
    info[2] = ids[2]
    block = lax.broadcasted_iota(jnp.int32, cov.shape, 0)
    lane = lax.broadcasted_iota(jnp.int32, cov.shape, 1)
    bits = jnp.where(cov[...] != 0, jnp.left_shift(1, block), 0)
    for j in range(views):
        view = chip * views + view_slot(core, j, views)
        code = jnp.sum(jnp.where(lane == view, bits, 0).astype(jnp.float32))
        info[MARKS + j] = code.astype(jnp.int32)
        taps_all = spread[pl.ds(view, taps_x * taps_y, stride=total_views), :]
        rows[j, : taps_x * taps_y, :taps_z] = taps_all
        weights = rows[j]
        kernel = (weights / jnp.sum(weights)).astype(jnp.bfloat16)
        rows[j] = jnp.dot(kernel, place, preferred_element_type=jnp.float32)

    def fill(a, carry):
        at_x = canonical(1 - core, a, taps_x - 1)
        for j in range(views):
            for b in range(taps_y):
                line = rows[j, pl.ds(at_x * taps_y + taps_y - 1 - b, 1), :]
                line = jnp.broadcast_to(line, (depth, depth))
                line = pltpu.roll(line, 0, 1, stride=1, stride_axis=0)
                line = jnp.where(band, line, 0.0).astype(jnp.bfloat16)
                table[j, a, b * depth : (b + 1) * depth, :] = line
        return carry

    lax.fori_loop(0, taps_x, fill, 0, unroll=3)
    for copy in copies:
        copy.wait()
    fill_columns(pad, cols, taps_y, width)
    for r in range(est_own.shape[0]):
        est_own[r] = pad[chip * est_own.shape[0] + r, PAD : PAD + width, :]
    rim = count // 3
    rows_y = sums.shape[1] // rim
    for j in range(views):
        first = window_of(info, j, blocks, rows_y // (width // blocks))
        y_start = pl.multiple_of(first * (width // blocks), width // blocks)
        total = None
        for s in early_steps(rim, (taps_x + 1) // 2):
            part = dot_turned(
                lambda x: cols[x - rim, pl.ds(y_start, rows_y), :], range(rim), table, j, s
            )
            total = part if total is None else total + part
        sums[j] = total


def fill_columns(pad, cols, taps_y, rows_y):
    rim_y = (taps_y - 1) // 2
    for x in range(cols.shape[0]):
        for b in range(taps_y):
            low = PAD - rim_y + b
            cols[x, :, b * LANES : (b + 1) * LANES] = pad[x, low : low + rows_y, :].astype(
                jnp.bfloat16
            )


def left_side(slab, pairs, s):
    return jnp.concatenate(
        [jnp.concatenate([slab(2 * (i + s) + u) for u in range(2)], axis=1) for i in pairs], axis=0
    )


def right_side(table, j, s):
    taps_x = table.shape[1]

    def block(at):
        return table[j, at] if 0 <= at < taps_x else jnp.zeros(table.shape[2:], table.dtype)

    return jnp.concatenate(
        [jnp.concatenate([block(2 * s + u), block(2 * s + u - 1)], axis=1) for u in range(2)],
        axis=0,
    )


def right_side_turned(table, j, s):
    taps_x = table.shape[1]
    taps_y = table.shape[2] // LANES
    lines = []
    for w in range(2):
        line = []
        for u in range(2):
            at = taps_x - 1 - (2 * s + u - w)
            for b in range(taps_y - 1, -1, -1):
                if 0 <= at < taps_x:
                    line.append(table[j, at, b * LANES : (b + 1) * LANES, :])
                else:
                    line.append(jnp.zeros((LANES, LANES), table.dtype))
        lines.append(jnp.concatenate(line, axis=1))
    return jnp.concatenate(lines, axis=0)


def dot_turned(slab, pairs, table, j, s):
    return lax.dot_general(
        left_side(slab, pairs, s),
        right_side_turned(table, j, s),
        (((1,), (1,)), ((), ())),
        preferred_element_type=jnp.float32,
    )


def add_rows(total, part, cut):
    if total is None:
        return part
    if not cut:
        return total + part
    return jnp.concatenate([total[:cut], total[cut:] + part], axis=0)


def early_steps(rim, steps):
    return range(rim // 2, steps)


def blur_kernel(
    info, halo, img_own, img_other, cols, table, early, quot, remote, near, pad, edge, image, *, taps, blocks
):
    core, chip = info[0], info[1]
    views, half, rows_y, depth = quot.shape
    rim, width, _ = halo.shape
    block_width = width // blocks
    window = rows_y // block_width
    share_w = img_own.shape[1]
    if views == 1:
        own_at = pl.multiple_of(core * share_w, share_w)
        other_at = pl.multiple_of((1 - core) * share_w, share_w)
        for r in range(half):
            image[r, pl.ds(own_at, share_w), :] = img_own[half * core + r]
            image[r, pl.ds(other_at, share_w), :] = img_other[half * core + r]
    margin = jnp.zeros((rim, PAD, depth), jnp.float32)
    pad[:, :PAD, :] = margin
    pad[:, PAD + width :, :] = margin
    for x in range(rim):
        cells = halo[canonical(core, x, rim - 1)].astype(jnp.float32)
        pad[x, PAD : PAD + width, :] = jnp.where(info[2] > 0, cells, 0.0)
    fill_columns(pad, edge, taps[1], width)
    for j in range(views):
        first = window_of(info, j, blocks, window)
        mask = window_mask(info, j, first, window, block_width)
        y_start = pl.multiple_of(first * block_width, block_width)

        def slab(x):
            part = edge.at[x] if x < rim else cols.at[x - rim]
            return part[pl.ds(y_start, rows_y), :]

        total = early[j]
        for s in range(early_steps(rim, 0).start):
            total = total + dot_turned(slab, range(half // 2), table, j, s)
        blurred = [total[i * rows_y : (i + 1) * rows_y] for i in range(half // 2)]
        slot = view_slot(core, j, views)
        remote[slot, :HEADER, :] = jnp.full((HEADER, depth), first, jnp.int32).astype(jnp.bfloat16)
        for r in range(half):
            row = canonical(core, r, half - 1)
            if views == 1:
                cells = image[row, pl.ds(y_start, rows_y), :]
            else:
                cells = (img_other if j else img_own)[half * core + row, pl.ds(y_start, rows_y), :]
            i, w = r // 2, r % 2
            below = blurred[i][:, w * depth : (w + 1) * depth]
            ratio = jnp.where(mask, cells.astype(jnp.float32) / below, 0.0).astype(jnp.bfloat16)
            quot[j, r] = ratio
            if r < rim:
                low = HEADER + r * rows_y
                remote[slot, low : low + rows_y, :] = ratio
            else:
                near[slot, r - rim] = ratio


def inner_kernel(
    info, quot, near, table, sums, product, logs, ends, pad, cols, *, taps, blocks
):
    views, half, rows_y, depth = quot.shape
    rim = near.shape[1]
    pairs = half // 2
    steps = (table.shape[1] + 1) // 2
    margin = jnp.zeros((half + rim, PAD, depth), jnp.float32)
    product[...] = jnp.ones(product.shape, jnp.float32)
    for j in range(views):
        pad[j, :, :PAD, :] = margin
        pad[j, :, PAD + rows_y :, :] = margin
        for r in range(half):
            pad[j, r, PAD : PAD + rows_y, :] = quot[j, r].astype(jnp.float32)
        for r in range(rim):
            pad[j, half + rim - 1 - r, PAD : PAD + rows_y, :] = near[view_slot(info[0], j, views), r].astype(
                jnp.float32
            )
        fill_columns(pad.at[j], cols.at[j], taps[1], rows_y)
        total = None
        for s in range(steps - 1, -1, -1):
            skip = max(0, rim // 2 - s)
            part = jnp.dot(
                left_side(lambda x: cols[j, x - rim], range(skip, pairs), s),
                right_side(table, j, s),
                preferred_element_type=jnp.float32,
            )
            total = add_rows(total, part, skip * rows_y)
        whole = rim // 2 * rows_y
        sums[j] = total[:whole]
        block_width = product.shape[1] // blocks
        first = window_of(info, j, blocks, rows_y // block_width)
        mask = window_mask(info, j, first, rows_y // block_width, block_width)
        y_start = pl.multiple_of(first * block_width, block_width)
        for r in range(half - rim):
            low, w = whole + r // 2 * rows_y, r % 2
            factor = jnp.where(mask, total[low : low + rows_y, w * depth : (w + 1) * depth], 1.0)
            at = (r, pl.ds(y_start, rows_y), slice(None))
            product[at] = product[at] * factor
    least = jnp.full(ends.shape[1:], jnp.inf, jnp.float32)
    most = -least
    for r in range(half - rim):
        cells = jnp.log(product[r])
        logs[r] = cells
        least = jnp.minimum(least, cells)
        most = jnp.maximum(most, cells)
    ends[0] = least
    ends[1] = most


def correct_kernel(info, remote, sums, table, est_own, near_product, near_logs, ends, *rest, taps, blocks):
    *pieces, pad, cols, far, product, logs = rest
    chip = info[1]
    views, rim, rows_y, _ = cols.shape
    half, width, depth = product.shape
    block_width = width // blocks
    window = rows_y // block_width
    rows = half // len(pieces)
    product[:rim] = jnp.ones((rim, width, depth), jnp.float32)
    product[rim:] = near_product[...]
    logs[rim:] = near_logs[...]
    far[...] = jnp.zeros(far.shape, jnp.float32)
    for j in range(views):
        first = window_of(info, j, blocks, window)
        mask = window_mask(info, j, first, window, block_width)
        y_start = pl.multiple_of(first * block_width, block_width)
        slot = view_slot(info[0], j, views)
        there = jnp.max(remote[slot, :HEADER, :].astype(jnp.float32)).astype(jnp.int32)
        there = jnp.clip(there, 0, blocks - window)
        y_there = pl.multiple_of(there * block_width, block_width)
        for r in range(rim):
            low = HEADER + r * rows_y
            cells = remote[slot, low : low + rows_y, :].astype(jnp.float32)
            cells = jnp.where(info[2] > 0, cells, 0.0)
            far[j, rim - 1 - r, pl.ds(PAD + y_there, rows_y), :] = cells
        for r in range(rim):
            pad[j, r] = far[j, r, pl.ds(y_start, rows_y + 2 * PAD), :]
        fill_columns(pad.at[j], cols.at[j], taps[1], rows_y)
        edges = [None] * (rim // 2)
        for s in range(rim // 2):
            pairs = range(rim // 2 - s)
            part = jnp.dot(
                left_side(lambda x: cols[j, x], pairs, s),
                right_side(table, j, s),
                preferred_element_type=jnp.float32,
            )
            for i in pairs:
                cells = part[i * rows_y : (i + 1) * rows_y]
                edges[i] = cells if edges[i] is None else edges[i] + cells
        for r in range(rim):
            i, w = r // 2, r % 2
            cells = sums[j, i * rows_y : (i + 1) * rows_y, w * depth : (w + 1) * depth]
            cells = cells + edges[i][:, w * depth : (w + 1) * depth]
            factor = jnp.where(mask, cells, 1.0)
            at = (r, pl.ds(y_start, rows_y), slice(None))
            product[at] = product[at] * factor
    least, most = ends[0], ends[1]
    for r in range(rim):
        cells = jnp.log(product[r])
        logs[r] = cells
        least = jnp.minimum(least, cells)
        most = jnp.maximum(most, cells)
    header, low, scale = code_header(jnp.min(least), jnp.max(most))
    for r in range(rows):
        pieces[0][r] = est_own[r] * product[chip * rows + r]
    for step in range(1, len(pieces)):
        pieces[step][:HEADER, :] = header
        for r in range(rows):
            at = HEADER + r * width
            pieces[step][at : at + width, :] = encode(logs[(chip ^ step) * rows + r], low, scale)


def combine_kernel(own, *rest):
    *pieces, out = rest
    rows, width, _ = own.shape
    marks = [code_marks(piece) for piece in pieces]
    all_logs = []
    for r in range(rows):
        logs = jnp.log(own[r])
        for piece, mark in zip(pieces, marks):
            logs = logs + decode(piece, mark, HEADER + r * width, width)
        all_logs.append(logs)
    low = functools.reduce(jnp.minimum, all_logs)
    high = functools.reduce(jnp.maximum, all_logs)
    high = jnp.max(high)
    header, low, scale = code_header(jnp.maximum(jnp.min(low), high - SPAN), high)
    out[:HEADER, :] = header
    for r, logs in enumerate(all_logs):
        at = HEADER + r * width
        out[at : at + width, :] = encode(logs, low, scale)


def gather_kernel(ids, *rest):
    *pieces, out, cells, sems = rest
    core, chip = ids[0], ids[1]
    count = len(pieces) // 2
    slab_x, width, _ = out.shape
    rows = slab_x // 2 // count
    stores = []
    for place, piece in enumerate(pieces):
        side = core if place < count else 1 - core
        marks = code_marks(piece)
        for r in range(rows):
            at = canonical(side, (chip ^ (place % count)) * rows + r, slab_x - 1)
            slot = place * rows + r
            cells[slot] = jnp.exp(decode(piece, marks, HEADER + r * width, width))
            store = pltpu.make_async_copy(cells.at[slot], out.at[at], sems.at[slot])
            store.start()
            stores.append(store)
    for store in stores:
        store.wait()


def call(kernel, name, outs, kinds, scratch=(), flops=0, out_kinds=None):
    spaces = {"s": pltpu.SMEM, "v": pltpu.VMEM, "h": pltpu.HBM}
    many = isinstance(outs, tuple)
    out_kinds = out_kinds or "v" * (len(outs) if many else 1)
    out_specs = tuple(pl.BlockSpec(memory_space=spaces[kind]) for kind in out_kinds)
    return pl.pallas_call(
        kernel,
        name=name,
        out_shape=outs,
        in_specs=[pl.BlockSpec(memory_space=spaces[kind]) for kind in kinds],
        out_specs=out_specs if many else out_specs[0],
        scratch_shapes=list(scratch),
        compiler_params=pltpu.CompilerParams(vmem_limit_bytes=VMEM_LIMIT),
        cost_estimate=pl.CostEstimate(flops=flops, bytes_accessed=1 << 16, transcendentals=0),
    )


def local(estimate, images, point_spread, covered):
    slab_x, width, depth = estimate.shape
    share_w = images.shape[2]
    _, taps_x, taps_y, taps_z = point_spread.shape
    taps = (taps_x, taps_y, taps_z)
    rim = (taps_x - 1) // 2
    half = slab_x // 2
    blocks = covered.shape[2]
    window = min(CAP, blocks)
    rows_y = window * (width // blocks)
    shares = width // share_w
    views = 2 // shares
    assert shares * views == 2 and half == 2 * rim and depth == LANES
    group = lax.axis_index("view")
    chips = lax.axis_size("view") // 2
    core, chip = group % 2, group // 2
    ids = jnp.stack([core, chip, has_far(core)]).astype(jnp.int32)
    inner = half + rim
    rows = half // chips
    f32, bf16 = jnp.float32, jnp.bfloat16
    shape = jax.ShapeDtypeStruct
    deep = taps_y * depth
    wide = width + 2 * PAD
    tall = rows_y + 2 * PAD
    sems = pltpu.SemaphoreType.DMA
    work = 2 * half * rows_y * depth * taps_x * taps_y * depth * views

    img_other = swap_cores(images[0])
    estimate = pltpu.with_memory_space_constraint(estimate, pltpu.HBM)
    images = pltpu.with_memory_space_constraint(images, pltpu.HBM)
    spread = jnp.transpose(point_spread, (1, 2, 0, 3)).reshape(-1, taps_z)
    spread = pltpu.with_memory_space_constraint(spread, pltpu.HBM)
    cov = pltpu.with_memory_space_constraint(jnp.transpose(covered[:, 0, :]), pltpu.HBM)

    edge, cov, spread = call(
        payload_kernel,
        "payload",
        (
            shape((rim, width, depth), bf16),
            pltpu.VMEM(cov.shape, jnp.int32),
            pltpu.VMEM(spread.shape, f32),
        ),
        "shhh",
        [pltpu.VMEM((rim, width, depth), f32), sems((3,))],
    )(ids, cov, spread, estimate)
    halo = swap_layers(edge)

    table, cols, info, img_own, est_own, early = call(
        functools.partial(tables_kernel, taps=taps, blocks=blocks),
        "tables",
        (
            pltpu.VMEM((views, taps_x, deep, depth), bf16),
            pltpu.VMEM((inner, width, deep), bf16),
            shape((MARKS + views,), jnp.int32),
            pltpu.VMEM((slab_x, share_w, depth), bf16),
            pltpu.VMEM((rows, width, depth), f32),
            pltpu.VMEM((views, half // 2 * rows_y, 2 * depth), f32),
        ),
        "svvhh",
        [
            pltpu.VMEM((views, -(-taps_x * taps_y // 8) * 8, depth), f32),
            pltpu.VMEM((inner, wide, depth), f32),
            sems((inner + 1,)),
        ],
        work // 2,
        "vvsvvv",
    )(ids, cov, spread, estimate, images)

    quot, remote, near = call(
        functools.partial(blur_kernel, taps=taps, blocks=blocks),
        "blur",
        (
            pltpu.VMEM((views, half, rows_y, depth), bf16),
            shape((views, HEADER + rim * rows_y, depth), bf16),
            shape((views, rim, rows_y, depth), bf16),
        ),
        "svvvvvv",
        [
            pltpu.VMEM((rim, wide, depth), f32),
            pltpu.VMEM((rim, width, deep), bf16),
            pltpu.VMEM((half, width, depth) if views == 1 else (8, depth), bf16),
        ],
        work,
    )(info, halo, img_own, img_other, cols, table, early)
    near = swap_cores(near)
    remote = swap_layers(remote)

    part = pltpu.VMEM((half - rim, width, depth), f32)
    sums, near_product, near_logs, ends = call(
        functools.partial(inner_kernel, taps=taps, blocks=blocks),
        "inner",
        (
            pltpu.VMEM((views, rim // 2 * rows_y, 2 * depth), f32),
            part,
            part,
            pltpu.VMEM((2, width, depth), f32),
        ),
        "svvv",
        [
            pltpu.VMEM((views, inner, tall, depth), f32),
            pltpu.VMEM((views, inner, rows_y, deep), bf16),
        ],
        work,
    )(info, quot, near, table)

    coded = shape((HEADER + rows * width, depth), jnp.int16)
    pieces = call(
        functools.partial(correct_kernel, taps=taps, blocks=blocks),
        "correct",
        (pltpu.VMEM((rows, width, depth), f32),) + (coded,) * (chips - 1),
        "svvvvvvv",
        [
            pltpu.VMEM((views, rim, tall, depth), f32),
            pltpu.VMEM((views, rim, rows_y, deep), bf16),
            pltpu.VMEM((views, rim, wide, depth), f32),
            pltpu.VMEM((half, width, depth), f32),
            pltpu.VMEM((half, width, depth), f32),
        ],
        work // 4,
    )(info, remote, sums, table, est_own, near_product, near_logs, ends)
    steps = range(chips - 1, 0, -1)
    arrived = [pieces[0]] + [swap_chips(pieces[step], step) for step in steps]
    mine = call(
        combine_kernel,
        "combine",
        coded,
        "v" * chips,
    )(*arrived)
    column = [mine] + [swap_chips(mine, step) for step in range(1, chips)]
    across = [swap_cores(piece) for piece in column]
    return call(
        gather_kernel,
        "gather",
        shape(estimate.shape, f32),
        "s" + "v" * (2 * chips),
        [pltpu.VMEM(estimate.shape, f32), sems((slab_x,))],
        out_kinds="h",
    )(ids, *column, *across)


def solution(mesh):
    in_specs = (P("blk", None, None), P("view", "blk", None, None), P(), P(None, "blk", None))
    out_specs = P("blk", None, None)
    return jax.shard_map(local, mesh=mesh, in_specs=in_specs, out_specs=out_specs, check_vma=False)
```

```python
import functools

import jax
import jax.numpy as jnp
from jax import lax
from jax.experimental import pallas as pl
from jax.experimental.pallas import tpu as pltpu
from jax.sharding import PartitionSpec as P

CAP = 3
LANES = 128
PAD = 8
MARKS = 3
HEADER = 16
MARK = 256.0
LEVEL = 32767.0
SPAN = 16.6
VMEM_LIMIT = 24 * 1024 * 1024


def swap_cores(cells):
    count = lax.axis_size("view")
    return lax.ppermute(cells, "view", [(i, i ^ 1) for i in range(count)])


def swap_chips(cells, step):
    count = lax.axis_size("view")
    return lax.ppermute(cells, "view", [(i, i ^ (2 * step)) for i in range(count)])


def swap_layers(cells):
    views, layers = lax.axis_size("view"), lax.axis_size("blk")
    route = []
    for chip in range(views // 2):
        for layer in range(layers):
            for core in range(2):
                there = layer + (1 if core else -1)
                if 0 <= there < layers:
                    to = (2 * chip + 1 - core) * layers + there
                else:
                    to = (2 * (chip ^ 1) + core) * layers + layer
                route.append(((2 * chip + core) * layers + layer, to))
    return lax.ppermute(cells, ("view", "blk"), route)


def has_far(core):
    layer = lax.axis_index("blk")
    there = layer + 2 * core - 1
    return (there >= 0) & (there < lax.axis_size("blk"))


def code_header(low, high):
    low_mark = jnp.floor(low * MARK)
    span_mark = jnp.floor(high * MARK) + 1.0 - low_mark
    row = lax.broadcasted_iota(jnp.int32, (HEADER, LANES), 0)
    header = jnp.where(row == 0, low_mark, span_mark).astype(jnp.int32).astype(jnp.int16)
    return header, low_mark / MARK, (2 * LEVEL * MARK) / span_mark


def encode(logs, low, scale):
    steps = (logs - low) * scale - (LEVEL - 0.5)
    steps = jnp.clip(jnp.floor(steps), -LEVEL, LEVEL)
    return steps.astype(jnp.int32).astype(jnp.int16)


def code_marks(piece):
    header = piece[:HEADER, :].astype(jnp.int32).astype(jnp.float32)
    step = header[1:2, :] * (1.0 / (2 * LEVEL * MARK))
    return header[0:1, :] * (1.0 / MARK) + step * LEVEL, step


def decode(piece, marks, at, rows):
    middle, step = marks
    cells = piece[at : at + rows, :].astype(jnp.int32).astype(jnp.float32)
    return cells * step + middle


def view_slot(core, j, views):
    return core ^ j if views > 1 else 0


def is_covered(info, j, block):
    return ((info[MARKS + j] >> block) & 1) > 0


def window_of(info, j, blocks, window):
    first = jnp.int32(blocks - window)
    for block in range(blocks - window - 1, -1, -1):
        first = jnp.where(is_covered(info, j, block), jnp.int32(block), first)
    return first


def window_mask(info, j, first, window, block_width):
    row = lax.broadcasted_iota(jnp.int32, (window * block_width, LANES), 0)
    mask = jnp.zeros(row.shape, jnp.int32)
    for block in range(window):
        inside = (row >= block * block_width) & (row < (block + 1) * block_width)
        here = jnp.where(is_covered(info, j, first + block), 1, 0)
        mask = jnp.where(inside, here, mask)
    return mask > 0


def canonical(core, row, last):
    return jnp.where(core == 0, row, last - row)


def payload_kernel(ids, cov, spread, est, edge, cov_here, spread_here, rows, sems):
    core = ids[0]
    rim = edge.shape[0]
    far_rows = est.at[pl.ds((est.shape[0] - rim) * core, rim)]
    copies = [
        pltpu.make_async_copy(far_rows, rows, sems.at[0]),
        pltpu.make_async_copy(spread, spread_here, sems.at[1]),
        pltpu.make_async_copy(cov, cov_here, sems.at[2]),
    ]
    for copy in copies:
        copy.start()
    copies[0].wait()
    edge[...] = rows[...].astype(edge.dtype)
    for copy in copies[1:]:
        copy.wait()


def tables_kernel(
    ids,
    cov,
    spread,
    est,
    images,
    table,
    cols,
    info,
    img_own,
    est_own,
    sums,
    rows,
    pad,
    sems,
    *,
    taps,
    blocks,
):
    taps_x, taps_y, taps_z = taps
    core, chip = ids[0], ids[1]
    rim_z = (taps_z - 1) // 2
    depth = LANES
    views = table.shape[0]
    count, width = cols.shape[0], cols.shape[1]
    margin = jnp.zeros((count, PAD, depth), jnp.float32)
    pad[:, :PAD, :] = margin
    pad[:, PAD + width :, :] = margin
    copies = [
        pltpu.make_async_copy(
            est.at[canonical(core, i, est.shape[0] - 1)], pad.at[i, pl.ds(PAD, width)], sems.at[i]
        )
        for i in range(count)
    ]
    copies.append(pltpu.make_async_copy(images.at[0], img_own, sems.at[count]))
    for copy in copies:
        copy.start()
    row = lax.broadcasted_iota(jnp.int32, (depth, depth), 0)
    col = lax.broadcasted_iota(jnp.int32, (depth, depth), 1)
    band = jnp.abs(row - col) <= rim_z
    at = row - rim_z
    place = ((col == at) | (col == at + depth)) & (row < taps_z)
    place = jnp.where(place, 1.0, 0.0).astype(jnp.bfloat16)
    rows[...] = jnp.zeros(rows.shape, jnp.float32)
    total_views = spread.shape[0] // (taps_x * taps_y)
    info[0] = core
    info[1] = chip
    info[2] = ids[2]
    block = lax.broadcasted_iota(jnp.int32, cov.shape, 0)
    lane = lax.broadcasted_iota(jnp.int32, cov.shape, 1)
    bits = jnp.where(cov[...] != 0, jnp.left_shift(1, block), 0)
    for j in range(views):
        view = chip * views + view_slot(core, j, views)
        code = jnp.sum(jnp.where(lane == view, bits, 0).astype(jnp.float32))
        info[MARKS + j] = code.astype(jnp.int32)
        taps_all = spread[pl.ds(view, taps_x * taps_y, stride=total_views), :]
        rows[j, : taps_x * taps_y, :taps_z] = taps_all
        weights = rows[j]
        kernel = (weights / jnp.sum(weights)).astype(jnp.bfloat16)
        rows[j] = jnp.dot(kernel, place, preferred_element_type=jnp.float32)

    def fill(a, carry):
        at_x = canonical(1 - core, a, taps_x - 1)
        for j in range(views):
            for b in range(taps_y):
                line = rows[j, pl.ds(at_x * taps_y + taps_y - 1 - b, 1), :]
                line = jnp.broadcast_to(line, (depth, depth))
                line = pltpu.roll(line, 0, 1, stride=1, stride_axis=0)
                line = jnp.where(band, line, 0.0).astype(jnp.bfloat16)
                table[j, a, b * depth : (b + 1) * depth, :] = line
        return carry

    lax.fori_loop(0, taps_x, fill, 0, unroll=3)
    for copy in copies:
        copy.wait()
    fill_columns(pad, cols, taps_y, width)
    for r in range(est_own.shape[0]):
        est_own[r] = pad[chip * est_own.shape[0] + r, PAD : PAD + width, :]
    rim = count // 3
    rows_y = sums.shape[1] // rim
    for j in range(views):
        first = window_of(info, j, blocks, rows_y // (width // blocks))
        y_start = pl.multiple_of(first * (width // blocks), width // blocks)
        total = None
        for s in early_steps(rim, (taps_x + 1) // 2):
            part = dot_turned(
                lambda x: cols[x - rim, pl.ds(y_start, rows_y), :], range(rim), table, j, s
            )
            total = part if total is None else total + part
        sums[j] = total


def fill_columns(pad, cols, taps_y, rows_y):
    rim_y = (taps_y - 1) // 2
    for x in range(cols.shape[0]):
        for b in range(taps_y):
            low = PAD - rim_y + b
            cols[x, :, b * LANES : (b + 1) * LANES] = pad[x, low : low + rows_y, :].astype(
                jnp.bfloat16
            )


def left_side(slab, pairs, s):
    return jnp.concatenate(
        [jnp.concatenate([slab(2 * (i + s) + u) for u in range(2)], axis=1) for i in pairs], axis=0
    )


def right_side(table, j, s):
    taps_x = table.shape[1]

    def block(at):
        return table[j, at] if 0 <= at < taps_x else jnp.zeros(table.shape[2:], table.dtype)

    return jnp.concatenate(
        [jnp.concatenate([block(2 * s + u), block(2 * s + u - 1)], axis=1) for u in range(2)],
        axis=0,
    )


def right_side_turned(table, j, s):
    taps_x = table.shape[1]
    taps_y = table.shape[2] // LANES
    lines = []
    for w in range(2):
        line = []
        for u in range(2):
            at = taps_x - 1 - (2 * s + u - w)
            for b in range(taps_y - 1, -1, -1):
                if 0 <= at < taps_x:
                    line.append(table[j, at, b * LANES : (b + 1) * LANES, :])
                else:
                    line.append(jnp.zeros((LANES, LANES), table.dtype))
        lines.append(jnp.concatenate(line, axis=1))
    return jnp.concatenate(lines, axis=0)


def dot_turned(slab, pairs, table, j, s):
    return lax.dot_general(
        left_side(slab, pairs, s),
        right_side_turned(table, j, s),
        (((1,), (1,)), ((), ())),
        preferred_element_type=jnp.float32,
    )


def add_rows(total, part, cut):
    if total is None:
        return part
    if not cut:
        return total + part
    return jnp.concatenate([total[:cut], total[cut:] + part], axis=0)


def early_steps(rim, steps):
    return range(rim // 2, steps)


def blur_kernel(
    info, halo, img_own, img_other, cols, table, early, quot, remote, near, pad, edge, image, *, taps, blocks
):
    core, chip = info[0], info[1]
    views, half, rows_y, depth = quot.shape
    rim, width, _ = halo.shape
    block_width = width // blocks
    window = rows_y // block_width
    share_w = img_own.shape[1]
    if views == 1:
        own_at = pl.multiple_of(core * share_w, share_w)
        other_at = pl.multiple_of((1 - core) * share_w, share_w)
        for r in range(half):
            image[r, pl.ds(own_at, share_w), :] = img_own[half * core + r]
            image[r, pl.ds(other_at, share_w), :] = img_other[half * core + r]
    margin = jnp.zeros((rim, PAD, depth), jnp.float32)
    pad[:, :PAD, :] = margin
    pad[:, PAD + width :, :] = margin
    for x in range(rim):
        cells = halo[canonical(core, x, rim - 1)].astype(jnp.float32)
        pad[x, PAD : PAD + width, :] = jnp.where(info[2] > 0, cells, 0.0)
    fill_columns(pad, edge, taps[1], width)
    for j in range(views):
        first = window_of(info, j, blocks, window)
        mask = window_mask(info, j, first, window, block_width)
        y_start = pl.multiple_of(first * block_width, block_width)

        def slab(x):
            part = edge.at[x] if x < rim else cols.at[x - rim]
            return part[pl.ds(y_start, rows_y), :]

        total = early[j]
        for s in range(early_steps(rim, 0).start):
            total = total + dot_turned(slab, range(half // 2), table, j, s)
        blurred = [total[i * rows_y : (i + 1) * rows_y] for i in range(half // 2)]
        slot = view_slot(core, j, views)
        remote[slot, :HEADER, :] = jnp.full((HEADER, depth), first, jnp.int32).astype(jnp.bfloat16)
        for r in range(half):
            row = canonical(core, r, half - 1)
            if views == 1:
                cells = image[row, pl.ds(y_start, rows_y), :]
            else:
                cells = (img_other if j else img_own)[half * core + row, pl.ds(y_start, rows_y), :]
            i, w = r // 2, r % 2
            below = blurred[i][:, w * depth : (w + 1) * depth]
            ratio = jnp.where(mask, cells.astype(jnp.float32) / below, 0.0).astype(jnp.bfloat16)
            quot[j, r] = ratio
            if r < rim:
                low = HEADER + r * rows_y
                remote[slot, low : low + rows_y, :] = ratio
            else:
                near[slot, r - rim] = ratio


def inner_kernel(
    info, quot, near, table, sums, product, logs, ends, pad, cols, *, taps, blocks
):
    views, half, rows_y, depth = quot.shape
    rim = near.shape[1]
    pairs = half // 2
    steps = (table.shape[1] + 1) // 2
    margin = jnp.zeros((half + rim, PAD, depth), jnp.float32)
    product[...] = jnp.ones(product.shape, jnp.float32)
    for j in range(views):
        pad[j, :, :PAD, :] = margin
        pad[j, :, PAD + rows_y :, :] = margin
        for r in range(half):
            pad[j, r, PAD : PAD + rows_y, :] = quot[j, r].astype(jnp.float32)
        for r in range(rim):
            pad[j, half + rim - 1 - r, PAD : PAD + rows_y, :] = near[view_slot(info[0], j, views), r].astype(
                jnp.float32
            )
        fill_columns(pad.at[j], cols.at[j], taps[1], rows_y)
        total = None
        for s in range(steps - 1, -1, -1):
            skip = max(0, rim // 2 - s)
            part = jnp.dot(
                left_side(lambda x: cols[j, x - rim], range(skip, pairs), s),
                right_side(table, j, s),
                preferred_element_type=jnp.float32,
            )
            total = add_rows(total, part, skip * rows_y)
        whole = rim // 2 * rows_y
        sums[j] = total[:whole]
        block_width = product.shape[1] // blocks
        first = window_of(info, j, blocks, rows_y // block_width)
        mask = window_mask(info, j, first, rows_y // block_width, block_width)
        y_start = pl.multiple_of(first * block_width, block_width)
        for r in range(half - rim):
            low, w = whole + r // 2 * rows_y, r % 2
            factor = jnp.where(mask, total[low : low + rows_y, w * depth : (w + 1) * depth], 1.0)
            at = (r, pl.ds(y_start, rows_y), slice(None))
            product[at] = product[at] * factor
    least = jnp.full(ends.shape[1:], jnp.inf, jnp.float32)
    most = -least
    for r in range(half - rim):
        cells = jnp.log(product[r])
        logs[r] = cells
        least = jnp.minimum(least, cells)
        most = jnp.maximum(most, cells)
    ends[0] = least
    ends[1] = most


def correct_kernel(info, remote, sums, table, est_own, near_product, near_logs, ends, *rest, taps, blocks):
    *pieces, pad, cols, far, product, logs = rest
    chip = info[1]
    views, rim, rows_y, _ = cols.shape
    half, width, depth = product.shape
    block_width = width // blocks
    window = rows_y // block_width
    rows = half // len(pieces)
    product[:rim] = jnp.ones((rim, width, depth), jnp.float32)
    product[rim:] = near_product[...]
    logs[rim:] = near_logs[...]
    far[...] = jnp.zeros(far.shape, jnp.float32)
    for j in range(views):
        first = window_of(info, j, blocks, window)
        mask = window_mask(info, j, first, window, block_width)
        y_start = pl.multiple_of(first * block_width, block_width)
        slot = view_slot(info[0], j, views)
        there = jnp.max(remote[slot, :HEADER, :].astype(jnp.float32)).astype(jnp.int32)
        there = jnp.clip(there, 0, blocks - window)
        y_there = pl.multiple_of(there * block_width, block_width)
        for r in range(rim):
            low = HEADER + r * rows_y
            cells = remote[slot, low : low + rows_y, :].astype(jnp.float32)
            cells = jnp.where(info[2] > 0, cells, 0.0)
            far[j, rim - 1 - r, pl.ds(PAD + y_there, rows_y), :] = cells
        for r in range(rim):
            pad[j, r] = far[j, r, pl.ds(y_start, rows_y + 2 * PAD), :]
        fill_columns(pad.at[j], cols.at[j], taps[1], rows_y)
        edges = [None] * (rim // 2)
        for s in range(rim // 2):
            pairs = range(rim // 2 - s)
            part = jnp.dot(
                left_side(lambda x: cols[j, x], pairs, s),
                right_side(table, j, s),
                preferred_element_type=jnp.float32,
            )
            for i in pairs:
                cells = part[i * rows_y : (i + 1) * rows_y]
                edges[i] = cells if edges[i] is None else edges[i] + cells
        for r in range(rim):
            i, w = r // 2, r % 2
            cells = sums[j, i * rows_y : (i + 1) * rows_y, w * depth : (w + 1) * depth]
            cells = cells + edges[i][:, w * depth : (w + 1) * depth]
            factor = jnp.where(mask, cells, 1.0)
            at = (r, pl.ds(y_start, rows_y), slice(None))
            product[at] = product[at] * factor
    least, most = ends[0], ends[1]
    for r in range(rim):
        cells = jnp.log(product[r])
        logs[r] = cells
        least = jnp.minimum(least, cells)
        most = jnp.maximum(most, cells)
    header, low, scale = code_header(jnp.min(least), jnp.max(most))
    for r in range(rows):
        pieces[0][r] = est_own[r] * product[chip * rows + r]
    for step in range(1, len(pieces)):
        pieces[step][:HEADER, :] = header
        for r in range(rows):
            at = HEADER + r * width
            pieces[step][at : at + width, :] = encode(logs[(chip ^ step) * rows + r], low, scale)


def combine_kernel(own, *rest):
    *pieces, out = rest
    rows, width, _ = own.shape
    marks = [code_marks(piece) for piece in pieces]
    all_logs = []
    for r in range(rows):
        logs = jnp.log(own[r])
        for piece, mark in zip(pieces, marks):
            logs = logs + decode(piece, mark, HEADER + r * width, width)
        all_logs.append(logs)
    low = functools.reduce(jnp.minimum, all_logs)
    high = functools.reduce(jnp.maximum, all_logs)
    high = jnp.max(high)
    header, low, scale = code_header(jnp.maximum(jnp.min(low), high - SPAN), high)
    out[:HEADER, :] = header
    for r, logs in enumerate(all_logs):
        at = HEADER + r * width
        out[at : at + width, :] = encode(logs, low, scale)


def gather_kernel(ids, *rest):
    *pieces, out, cells, sems = rest
    core, chip = ids[0], ids[1]
    count = len(pieces) // 2
    slab_x, width, _ = out.shape
    rows = slab_x // 2 // count
    stores = []
    for place, piece in enumerate(pieces):
        side = core if place < count else 1 - core
        marks = code_marks(piece)
        first = canonical(side, (chip ^ (place % count)) * rows, slab_x - rows)
        for r in range(rows):
            slot = place * rows + canonical(side, r, rows - 1)
            cells[slot] = jnp.exp(decode(piece, marks, HEADER + r * width, width))
        store = pltpu.make_async_copy(
            cells.at[pl.ds(place * rows, rows)], out.at[pl.ds(first, rows)], sems.at[place]
        )
        store.start()
        stores.append(store)
    for store in stores:
        store.wait()


def call(kernel, name, outs, kinds, scratch=(), flops=0, out_kinds=None):
    spaces = {"s": pltpu.SMEM, "v": pltpu.VMEM, "h": pltpu.HBM}
    many = isinstance(outs, tuple)
    out_kinds = out_kinds or "v" * (len(outs) if many else 1)
    out_specs = tuple(pl.BlockSpec(memory_space=spaces[kind]) for kind in out_kinds)
    return pl.pallas_call(
        kernel,
        name=name,
        out_shape=outs,
        in_specs=[pl.BlockSpec(memory_space=spaces[kind]) for kind in kinds],
        out_specs=out_specs if many else out_specs[0],
        scratch_shapes=list(scratch),
        compiler_params=pltpu.CompilerParams(vmem_limit_bytes=VMEM_LIMIT),
        cost_estimate=pl.CostEstimate(flops=flops, bytes_accessed=1 << 16, transcendentals=0),
    )


def local(estimate, images, point_spread, covered):
    slab_x, width, depth = estimate.shape
    share_w = images.shape[2]
    _, taps_x, taps_y, taps_z = point_spread.shape
    taps = (taps_x, taps_y, taps_z)
    rim = (taps_x - 1) // 2
    half = slab_x // 2
    blocks = covered.shape[2]
    window = min(CAP, blocks)
    rows_y = window * (width // blocks)
    shares = width // share_w
    views = 2 // shares
    assert shares * views == 2 and half == 2 * rim and depth == LANES
    group = lax.axis_index("view")
    chips = lax.axis_size("view") // 2
    core, chip = group % 2, group // 2
    ids = jnp.stack([core, chip, has_far(core)]).astype(jnp.int32)
    inner = half + rim
    rows = half // chips
    f32, bf16 = jnp.float32, jnp.bfloat16
    shape = jax.ShapeDtypeStruct
    deep = taps_y * depth
    wide = width + 2 * PAD
    tall = rows_y + 2 * PAD
    sems = pltpu.SemaphoreType.DMA
    work = 2 * half * rows_y * depth * taps_x * taps_y * depth * views

    img_other = swap_cores(images[0])
    estimate = pltpu.with_memory_space_constraint(estimate, pltpu.HBM)
    images = pltpu.with_memory_space_constraint(images, pltpu.HBM)
    spread = jnp.transpose(point_spread, (1, 2, 0, 3)).reshape(-1, taps_z)
    spread = pltpu.with_memory_space_constraint(spread, pltpu.HBM)
    cov = pltpu.with_memory_space_constraint(jnp.transpose(covered[:, 0, :]), pltpu.HBM)

    edge, cov, spread = call(
        payload_kernel,
        "payload",
        (
            shape((rim, width, depth), bf16),
            pltpu.VMEM(cov.shape, jnp.int32),
            pltpu.VMEM(spread.shape, f32),
        ),
        "shhh",
        [pltpu.VMEM((rim, width, depth), f32), sems((3,))],
    )(ids, cov, spread, estimate)
    halo = swap_layers(edge)

    table, cols, info, img_own, est_own, early = call(
        functools.partial(tables_kernel, taps=taps, blocks=blocks),
        "tables",
        (
            pltpu.VMEM((views, taps_x, deep, depth), bf16),
            pltpu.VMEM((inner, width, deep), bf16),
            shape((MARKS + views,), jnp.int32),
            pltpu.VMEM((slab_x, share_w, depth), bf16),
            pltpu.VMEM((rows, width, depth), f32),
            pltpu.VMEM((views, half // 2 * rows_y, 2 * depth), f32),
        ),
        "svvhh",
        [
            pltpu.VMEM((views, -(-taps_x * taps_y // 8) * 8, depth), f32),
            pltpu.VMEM((inner, wide, depth), f32),
            sems((inner + 1,)),
        ],
        work // 2,
        "vvsvvv",
    )(ids, cov, spread, estimate, images)

    quot, remote, near = call(
        functools.partial(blur_kernel, taps=taps, blocks=blocks),
        "blur",
        (
            pltpu.VMEM((views, half, rows_y, depth), bf16),
            shape((views, HEADER + rim * rows_y, depth), bf16),
            shape((views, rim, rows_y, depth), bf16),
        ),
        "svvvvvv",
        [
            pltpu.VMEM((rim, wide, depth), f32),
            pltpu.VMEM((rim, width, deep), bf16),
            pltpu.VMEM((half, width, depth) if views == 1 else (8, depth), bf16),
        ],
        work,
    )(info, halo, img_own, img_other, cols, table, early)
    near = swap_cores(near)
    remote = swap_layers(remote)

    part = pltpu.VMEM((half - rim, width, depth), f32)
    sums, near_product, near_logs, ends = call(
        functools.partial(inner_kernel, taps=taps, blocks=blocks),
        "inner",
        (
            pltpu.VMEM((views, rim // 2 * rows_y, 2 * depth), f32),
            part,
            part,
            pltpu.VMEM((2, width, depth), f32),
        ),
        "svvv",
        [
            pltpu.VMEM((views, inner, tall, depth), f32),
            pltpu.VMEM((views, inner, rows_y, deep), bf16),
        ],
        work,
    )(info, quot, near, table)

    coded = shape((HEADER + rows * width, depth), jnp.int16)
    pieces = call(
        functools.partial(correct_kernel, taps=taps, blocks=blocks),
        "correct",
        (pltpu.VMEM((rows, width, depth), f32),) + (coded,) * (chips - 1),
        "svvvvvvv",
        [
            pltpu.VMEM((views, rim, tall, depth), f32),
            pltpu.VMEM((views, rim, rows_y, deep), bf16),
            pltpu.VMEM((views, rim, wide, depth), f32),
            pltpu.VMEM((half, width, depth), f32),
            pltpu.VMEM((half, width, depth), f32),
        ],
        work // 4,
    )(info, remote, sums, table, est_own, near_product, near_logs, ends)
    steps = range(chips - 1, 0, -1)
    arrived = [pieces[0]] + [swap_chips(pieces[step], step) for step in steps]
    mine = call(
        combine_kernel,
        "combine",
        coded,
        "v" * chips,
    )(*arrived)
    column = [mine] + [swap_chips(mine, step) for step in range(1, chips)]
    across = [swap_cores(piece) for piece in column]
    return call(
        gather_kernel,
        "gather",
        shape(estimate.shape, f32),
        "s" + "v" * (2 * chips),
        [pltpu.VMEM(estimate.shape, f32), sems((slab_x,))],
        out_kinds="h",
    )(ids, *column, *across)


def solution(mesh):
    in_specs = (P("blk", None, None), P("view", "blk", None, None), P(), P(None, "blk", None))
    out_specs = P("blk", None, None)
    return jax.shard_map(local, mesh=mesh, in_specs=in_specs, out_specs=out_specs, check_vma=False)
```
